256 devices in a mesh: region: 8 (over x, core), dom: 32 (over y, z).
Axes of the slice: x: 4, y: 4, z: 8, core: 2. Of those that a mesh axis runs over, the one named last changes fastest.
Arguments:
- params: float32 [59, 262144], P(None, ('region', 'dom')), may hold values from -6.4 to 6.4, as said below
- first_moment: float32 [59, 262144], P(None, ('region', 'dom')), may hold values from -0.3 to 0.3
- second_moment: float32 [59, 262144], P(None, ('region', 'dom')), may hold values from 0.0001 to 0.01
- piece_blocks: int32 [256, 32, 2], P(('region', 'dom')), may hold values from 0 to 9, all different within a row
- piece_live: int32 [256, 32], P(('region', 'dom')), may hold values from 1 to 2
- piece_owner: int32 [256, 32], P(('region', 'dom')), may hold values from 0 to 31, as said below
- piece_cell: int32 [256, 32], P(('region', 'dom')), may hold values from 0 to 63, as said below
- target: float32 [256, 8, 3, 256], P(('region', 'dom')), may hold values from 0 to 1
- background: float32 [3], replicated, may hold values from 0 to 1
Outputs:
- gradient: float32 [59, 262144], P(None, ('region', 'dom'))
- new_params: float32 [59, 262144], P(None, ('region', 'dom'))
- new_first: float32 [59, 262144], P(None, ('region', 'dom'))
- new_second: float32 [59, 262144], P(None, ('region', 'dom'))
The draws below stay inside these ranges and needn't reach their ends.
Inputs may be any that keep to these rules, and one draw needn't show every extreme that they name: `params`: rows 0 to 2: z in [2, 4], x / z and y / z in [-1.6, 1.6]; rows 3 to 5 in [-0.9, 0.2]; row 6 in [0.5, 1.5]; rows 7 to 9 in [-1, 1]; row 10 in [-5.5, -1.8]; rows 11 to 58 in [-2, 2]. `piece_blocks`: the entries of one list are different pool blocks. `piece_owner`: each part sends at most 2 pieces to one owner; in every region some owner receives exactly 2 pieces from every part. `piece_cell`: the pieces that one owner receives have different cells.
All inputs are finite; a program needn't handle non-finite values.
Results may differ from the reference program's by a relative error of at most 0.0003.
Values sent between devices are 32-bit elements; how exact they have to be, the bound alone decides.
A program may use at most 64 MiB of HBM per device.

```python
import math
import jax
import jax.numpy as jnp
from jax import lax

PARAMS = 59
TSIDE = 16
WIN = 8
BLOCK = 128
BLOCKS = 8
KB = 2
MAXD = 8
PIECES = 32
PIX = 256
TILE_DEV = 8
CELLS = 64
POOL = 10
SENDERS = 256
GAUSS = 262144
N_REGION = 8
N_DOM = 32


def draw_params(key, part):
    keys = jax.random.split(jax.random.fold_in(key, 11), 7)
    depth_z = jax.random.uniform(keys[0], (1, GAUSS), minval=2.0, maxval=4.0)
    across = jax.random.uniform(keys[1], (2, GAUSS), minval=-1.6, maxval=1.6) * depth_z
    quat_w = jax.random.uniform(keys[3], (1, GAUSS), minval=0.5, maxval=1.5)
    quat_rest = jax.random.uniform(keys[4], (3, GAUSS), minval=-1.0, maxval=1.0)
    degree_scale = jnp.concatenate([jnp.full((1,), 0.6), jnp.full((15,), 0.25)])[None, :, None]
    log_scales = jax.random.uniform(keys[2], (3, GAUSS), minval=-0.7, maxval=0.0)
    logits = jax.random.uniform(keys[5], (1, GAUSS), minval=-5.0, maxval=-2.0)
    coeffs = jax.random.normal(keys[6], (3, 16, GAUSS)) * degree_scale
    coeffs = jnp.clip(coeffs, -2.0, 2.0).reshape(48, GAUSS)
    return jnp.concatenate([across, depth_z, log_scales, quat_w, quat_rest, logits, coeffs], axis=0).astype(jnp.float32)


def routing_draw(key):
    base = jax.random.fold_in(key, 29)
    regions = SENDERS // N_DOM
    capacity = 2 * PIECES // N_DOM
    slot_total = N_DOM * capacity
    region_keys = jax.random.split(jax.random.fold_in(base, 1), regions)
    full_owner = jax.vmap(lambda one_key: jax.random.randint(one_key, (), 0, N_DOM))(region_keys)
    full_each = jnp.repeat(full_owner, N_DOM)
    sender_keys = jax.random.split(jax.random.fold_in(base, 2), SENDERS)

    def choose(one_key, full_dest):
        scores = jax.random.permutation(one_key, slot_total)
        slot_ids = jnp.arange(slot_total)
        scores = jnp.where(slot_ids // capacity == full_dest, slot_ids - slot_total, scores)
        picked = jnp.argsort(scores, stable=True)[:PIECES]
        mixed = jax.random.permutation(jax.random.fold_in(one_key, 3), picked)
        return mixed // capacity
    owners = jax.vmap(choose)(sender_keys, full_each)
    onehot = (owners[:, :, None] == jnp.arange(N_DOM)[None, None, :]).astype(jnp.int32)
    position = jnp.sum((jnp.cumsum(onehot, axis=1) - onehot) * onehot, axis=2)
    owner_keys = jax.random.split(jax.random.fold_in(base, 4), SENDERS)
    perms = jax.vmap(lambda one_key: jax.random.permutation(one_key, slot_total))(owner_keys).reshape(regions, N_DOM, slot_total)
    region_of = jnp.arange(SENDERS) // N_DOM
    dom_of = jnp.arange(SENDERS) % N_DOM
    cells = perms[region_of[:, None], owners, dom_of[:, None] * capacity + position]
    return (owners.astype(jnp.int32), cells.astype(jnp.int32))


def draw_piece_owner(key, part):
    return routing_draw(key)[0]


def draw_piece_cell(key, part):
    return routing_draw(key)[1]


def place_ends(result, rng, smallest, high):
    longest = result.shape.index(max(result.shape))
    spots = []
    for shift in (0, 1):
        where = [jax.random.randint(jax.random.fold_in(rng, axis), (), 0, length) for axis, length in enumerate(result.shape)]
        where[longest] = (where[longest] + shift) % result.shape[longest]
        spots.append(tuple(where))
    return result.at[spots[0]].set(smallest).at[spots[1]].set(high)


def block_scale(rng, extent, cuts, low, top_value):
    def one(axis_at, shards_of):
        draws = jax.random.uniform(jax.random.fold_in(jax.random.fold_in(rng, 6), axis_at), (shards_of,), jnp.float32, low / len(cuts), top_value / len(cuts))
        return jnp.repeat(jnp.exp(draws), extent[axis_at] // shards_of).reshape((-1,) + (1,) * (len(extent) - axis_at - 1))

    factor_of = one(*cuts[0])
    for cut in cuts[1:]:
        factor_of = factor_of * one(*cut)
    return factor_of


def picks_of(stream_key, rows, count, top, lift):
    sequence = jax.random.permutation(jax.random.fold_in(stream_key, 1), count)
    pull = sequence
    for power in range(3):
        pull = pull * pull // count
    pull = pull * lift // count
    lots = jax.random.randint(jax.random.fold_in(stream_key, 2), (rows, count), 0, 4096) + pull
    holders = jax.random.permutation(jax.random.fold_in(stream_key, 3), rows)[jnp.arange(count) % rows]
    lots = jnp.where(jnp.arange(rows)[:, None] == holders[None, :], 1 << 14, lots)
    priority = lots * count + jnp.arange(count)
    return lax.top_k(priority.astype(jnp.int32), top)[1].astype(jnp.int32)


def gaussian(rng, dims, scale, reach, cuts=(), kind=jnp.bfloat16):
    result = jax.random.normal(rng, dims, jnp.float32) * scale
    if len(cuts) > 0:
        result = block_scale(rng, dims, cuts, -0.22, 0.18) * result
    return jnp.clip(result, min=-reach, max=reach).astype(kind)


def setup_inputs(seed: int = 0) -> dict:
    key_list = jax.random.split(jax.random.key(seed), 10)
    return {
        "params": draw_params(jax.random.fold_in(key_list[9], 71), 0),
        "first_moment": gaussian(key_list[1], (PARAMS, GAUSS), 0.05, 0.3, ((1, 256),), jnp.float32),
        "second_moment": jnp.clip(jnp.exp(math.log(0.01) - 4.6051702 * jax.random.uniform(key_list[2], (PARAMS, GAUSS), jnp.float32) ** block_scale(key_list[2], (PARAMS, GAUSS), ((1, 256),), -0.2, 0.2)), 0.0001, 0.01),
        "piece_blocks": picks_of(key_list[3], SENDERS * PIECES, POOL, KB, 0).reshape((SENDERS, PIECES, KB)),
        "piece_live": place_ends(jax.random.randint(key_list[4], (SENDERS, PIECES), 1, KB + 1), jax.random.fold_in(key_list[4], 1), 1, KB).astype(jnp.int32),
        "piece_owner": draw_piece_owner(jax.random.fold_in(key_list[9], 71), 0),
        "piece_cell": draw_piece_cell(jax.random.fold_in(key_list[9], 71), 0),
        "target": jnp.clip(1.0 * jax.random.uniform(key_list[7], (SENDERS, TILE_DEV, 3, PIX), jnp.float32) ** block_scale(key_list[7], (SENDERS, TILE_DEV, 3, PIX), ((0, 256),), -0.2, 0.2), 0.0, 1.0),
        "background": jnp.clip(jax.random.uniform(key_list[8], (3,), jnp.float32, 0.0, 1.0), 0.0, 1.0),
    }


harmonic_zero = 0.28209479177387814
harmonic_one = 0.4886025119029199
harmonic_two = (1.0925484305920792, -1.0925484305920792, 0.31539156525252005, -1.0925484305920792, 0.5462742152960396)
harmonic_three = (-0.5900435899266435, 2.890611442640554, -0.4570457994644658, 0.3731763325901154, -0.4570457994644658, 1.445305721320277, -0.5900435899266435)
beta_one = 0.9
beta_two = 0.999
rate = 0.001
adam_step = 100
tiny = 1e-08

def splat_table(block, screen_px):
    mean_x, mean_y, mean_z = (block[0], block[1], block[2])
    scales = jnp.exp(block[3:6])
    quat_raw = block[6:10]
    quat_norm = quat_raw / jnp.sqrt(lax.optimization_barrier(jnp.sum(quat_raw * quat_raw, axis=0)))
    quat_w, quat_x, quat_y, quat_z = (quat_norm[0], quat_norm[1], quat_norm[2], quat_norm[3])
    rotation = [[1 - 2 * (quat_y * quat_y + quat_z * quat_z), 2 * (quat_x * quat_y - quat_w * quat_z), 2 * (quat_x * quat_z + quat_w * quat_y)], [2 * (quat_x * quat_y + quat_w * quat_z), 1 - 2 * (quat_x * quat_x + quat_z * quat_z), 2 * (quat_y * quat_z - quat_w * quat_x)], [2 * (quat_x * quat_z - quat_w * quat_y), 2 * (quat_y * quat_z + quat_w * quat_x), 1 - 2 * (quat_x * quat_x + quat_y * quat_y)]]
    focal_px = 0.3125 * screen_px
    inv_z = 1.0 / mean_z
    jac_rows = [[focal_px * inv_z, 0.0 * inv_z, -focal_px * mean_x * inv_z * inv_z], [0.0 * inv_z, focal_px * inv_z, -focal_px * mean_y * inv_z * inv_z]]
    projected = []
    for out_row in range(2):
        entries = []
        for out_col in range(3):
            acc_term = jac_rows[out_row][0] * rotation[0][out_col]
            acc_term = acc_term + jac_rows[out_row][1] * rotation[1][out_col]
            acc_term = acc_term + jac_rows[out_row][2] * rotation[2][out_col]
            entries.append(acc_term * scales[out_col])
        projected.append(entries)
    sigma_xx = projected[0][0] * projected[0][0] + projected[0][1] * projected[0][1] + projected[0][2] * projected[0][2] + 0.3
    sigma_xy = projected[0][0] * projected[1][0] + projected[0][1] * projected[1][1] + projected[0][2] * projected[1][2]
    sigma_yy = projected[1][0] * projected[1][0] + projected[1][1] * projected[1][1] + projected[1][2] * projected[1][2] + 0.3
    determinant = sigma_xx * sigma_yy - sigma_xy * sigma_xy
    conic_xx = sigma_yy / determinant
    conic_xy = -sigma_xy / determinant
    conic_yy = sigma_xx / determinant
    centre_u = 0.5 * screen_px + focal_px * mean_x * inv_z
    centre_v = 0.5 * screen_px + focal_px * mean_y * inv_z
    opacity = jax.nn.sigmoid(block[10])
    length = jnp.sqrt(mean_x * mean_x + mean_y * mean_y + mean_z * mean_z)
    dir_x, dir_y, dir_z = (mean_x / length, mean_y / length, mean_z / length)
    sq_x, sq_y, sq_z = (dir_x * dir_x, dir_y * dir_y, dir_z * dir_z)
    harmonics = [harmonic_zero + 0.0 * dir_x, -harmonic_one * dir_y, harmonic_one * dir_z, -harmonic_one * dir_x, harmonic_two[0] * dir_x * dir_y, harmonic_two[1] * dir_y * dir_z, harmonic_two[2] * (2 * sq_z - sq_x - sq_y), harmonic_two[3] * dir_x * dir_z, harmonic_two[4] * (sq_x - sq_y), harmonic_three[0] * dir_y * (3 * sq_x - sq_y), harmonic_three[1] * dir_x * dir_y * dir_z, harmonic_three[2] * dir_y * (4 * sq_z - sq_x - sq_y), harmonic_three[3] * dir_z * (2 * sq_z - 3 * sq_x - 3 * sq_y), harmonic_three[4] * dir_x * (4 * sq_z - sq_x - sq_y), harmonic_three[5] * dir_z * (sq_x - sq_y), harmonic_three[6] * dir_x * (sq_x - 3 * sq_y)]
    basis = jnp.stack(harmonics, axis=0)
    coeffs = block[11:59].reshape(3, 16, block.shape[1])
    colour = jnp.maximum(lax.optimization_barrier(jnp.sum(coeffs * basis[None], axis=1)) + 0.5, 0.0)
    return jnp.stack([centre_u, centre_v, conic_xx, conic_xy, conic_yy, opacity, colour[0], colour[1], colour[2]], axis=0)

def pool_terms(table, present):
    screen_px = float(WIN * TSIDE)
    flat = table.reshape(table.shape[0], table.shape[1] * table.shape[2])
    terms = splat_table(flat, screen_px).reshape(9, table.shape[1], table.shape[2])
    return jnp.where(present[None, :, None] > 0, terms, jnp.zeros_like(terms))

def render_piece(chosen, slot_flags, tile_index):
    pixels = jnp.arange(TSIDE * TSIDE, dtype=jnp.int32)
    column = tile_index % WIN
    tile_row = tile_index // WIN
    pixel_x = (TSIDE * column + pixels % TSIDE).astype(chosen.dtype) + 0.5
    pixel_y = (TSIDE * tile_row + pixels // TSIDE).astype(chosen.dtype) + 0.5
    carry_log = jnp.zeros((TSIDE * TSIDE,), chosen.dtype)
    colour_sum = jnp.zeros((3, TSIDE * TSIDE), chosen.dtype)
    for slot_no in range(chosen.shape[1]):
        terms = chosen[:, slot_no]
        centre_u, centre_v, conic_xx, conic_xy, conic_yy, opacity = (terms[0], terms[1], terms[2], terms[3], terms[4], terms[5])
        colour = terms[6:9]
        offset_x = pixel_x[None, :] - centre_u[:, None]
        offset_y = pixel_y[None, :] - centre_v[:, None]
        quadratic = conic_xx[:, None] * offset_x * offset_x + 2.0 * conic_xy[:, None] * offset_x * offset_y + conic_yy[:, None] * offset_y * offset_y
        alphas = (opacity * slot_flags[slot_no])[:, None] * jnp.exp(-0.5 * quadratic)
        log_keep = jnp.log1p(-alphas)
        before = carry_log[None, :] + jnp.cumsum(log_keep, axis=0) - log_keep
        weight = alphas * jnp.exp(before)
        colour_sum = colour_sum + jnp.dot(colour, weight, precision=lax.Precision.HIGHEST)
        carry_log = carry_log + lax.optimization_barrier(jnp.sum(log_keep, axis=0))
    return jnp.concatenate([colour_sum, jnp.exp(carry_log)[None, :]], axis=0)

def render_listed(terms, present, blocks_row, live_row, tile_index):
    chosen = terms[:, blocks_row]
    slot_ids = jnp.arange(blocks_row.shape[0], dtype=jnp.int32)
    slot_flags = present[blocks_row] * (slot_ids < live_row).astype(present.dtype)
    return render_piece(chosen, slot_flags, tile_index)

def build_pools(params):
    own_cols = params.reshape(PARAMS, N_REGION, N_DOM, BLOCKS * BLOCK)
    blank = jnp.zeros_like(own_cols[:, :1, :, :BLOCK])
    lower = jnp.concatenate([blank, own_cols[:, :-1, :, -BLOCK:]], axis=1)
    upper = jnp.concatenate([own_cols[:, 1:, :, :BLOCK], blank], axis=1)
    pooled = jnp.concatenate([lower, own_cols, upper], axis=3)
    pooled = pooled.reshape(PARAMS, N_REGION * N_DOM, POOL, BLOCK)
    return jnp.transpose(pooled, (1, 0, 2, 3))

def build_present(dtype_like):
    region_of = jnp.arange(N_REGION * N_DOM, dtype=jnp.int32) // N_DOM
    low_flag = (region_of > 0).astype(dtype_like.dtype)[:, None]
    high_flag = (region_of < N_REGION - 1).astype(dtype_like.dtype)[:, None]
    middle = jnp.ones((N_REGION * N_DOM, BLOCKS), dtype_like.dtype)
    return jnp.concatenate([low_flag, middle, high_flag], axis=1)

def total_loss(params, piece_blocks, piece_live, piece_owner, piece_cell, target, background):
    pools = build_pools(params)
    present = build_present(params)
    tile_ids = jnp.arange(PIECES, dtype=jnp.int32)

    def one_part(items):
        table, flags, blocks_part, live_part = items
        terms = pool_terms(table, flags)
        return jax.vmap(render_listed, in_axes=(None, None, 0, 0, 0))(terms, flags, blocks_part, live_part, tile_ids)
    pieces = lax.map(jax.checkpoint(one_part), (pools, present, piece_blocks, piece_live))
    pieces = pieces.reshape(N_REGION, N_DOM * PIECES, 4, PIX)
    cell_index = (piece_owner * CELLS + piece_cell).reshape(N_REGION, N_DOM * PIECES)
    empty = jnp.concatenate([jnp.zeros((N_DOM * CELLS, 3, PIX), pieces.dtype), jnp.ones((N_DOM * CELLS, 1, PIX), pieces.dtype)], axis=1)
    cell_grid = jax.vmap(lambda where_to, values: empty.at[where_to].set(values))(cell_index, pieces)
    cell_grid = cell_grid.reshape(N_REGION, N_DOM, TILE_DEV, MAXD, 4, PIX)
    in_front = jnp.ones((N_REGION, N_DOM, TILE_DEV, PIX), pieces.dtype)
    composite = jnp.zeros((N_REGION, N_DOM, TILE_DEV, 3, PIX), pieces.dtype)
    for depth_slot in range(MAXD):
        composite = composite + in_front[:, :, :, None, :] * cell_grid[:, :, :, depth_slot, :3]
        in_front = in_front * cell_grid[:, :, :, depth_slot, 3]
    composite = composite + in_front[:, :, :, None, :] * background[:, None]
    residual = composite - target.reshape(N_REGION, N_DOM, TILE_DEV, 3, PIX)
    return 0.5 * jnp.sum(residual * residual)

def reference(params, first_moment, second_moment, piece_blocks, piece_live, piece_owner, piece_cell, target, background):
    gradient = jax.grad(total_loss)(params, piece_blocks, piece_live, piece_owner, piece_cell, target, background)
    new_first = beta_one * first_moment + (1 - beta_one) * gradient
    new_second = beta_two * second_moment + (1 - beta_two) * gradient * gradient
    update = new_first / (1 - beta_one ** adam_step) / (jnp.sqrt(new_second / (1 - beta_two ** adam_step)) + tiny)
    new_params = params - rate * update
    return (gradient, new_params, new_first, new_second)
```

```python
import math

import jax
import jax.numpy as jnp
import ml_dtypes
import numpy as np
from jax import lax
from jax.experimental import pallas as pl
from jax.experimental.pallas import tpu as pltpu
from jax.sharding import PartitionSpec as P

PARAMS = 59
TSIDE = 16
WIN = 8
BLOCK = 128
BLOCKS = 8
MAXD = 8
PIECES = 32
PIX = 256
TILE_DEV = 8
CELLS = 64
POOL = 10
SLOTS = 2
SUB = 8
STEPS = BLOCK // SUB
TAB = POOL + 1
PLANES = 16
ROWS = 64
ORIGIN_X = 64.0
ORIGIN_Y = 32.0

harmonic_zero = 0.28209479177387814
harmonic_one = 0.4886025119029199
harmonic_two = (
    1.0925484305920792,
    -1.0925484305920792,
    0.31539156525252005,
    -1.0925484305920792,
    0.5462742152960396,
)
harmonic_three = (
    -0.5900435899266435,
    2.890611442640554,
    -0.4570457994644658,
    0.3731763325901154,
    -0.4570457994644658,
    1.445305721320277,
    -0.5900435899266435,
)
beta_one = 0.9
beta_two = 0.999
rate = 0.001
adam_step = 100
tiny = 1e-08

f32 = jnp.float32
bf16 = jnp.bfloat16
MESH = pl.DeviceIdType.MESH
VMEM_LIMIT = 48 * 1024 * 1024


def pixel_monomials():
    bf = ml_dtypes.bfloat16
    tile = np.arange(PIECES)[:, None]
    pixel = np.arange(PIX)[None, :]
    x = (TSIDE * (tile % WIN) + pixel % TSIDE + 0.5 - ORIGIN_X).astype(np.float32)
    y = (TSIDE * (tile // WIN) + pixel // TSIDE + 0.5 - ORIGIN_Y).astype(np.float32)

    def two(value):
        head = value.astype(bf).astype(np.float32)
        return [head, value - head]

    return [np.ones_like(x), x, y] + two(x * x) + two(x * y) + two(y * y)


def exponent_features():
    rows = [row for row in pixel_monomials() for _ in range(3)]
    rows += [np.zeros_like(rows[0])] * (32 - len(rows))
    return np.stack(rows, axis=1).astype(ml_dtypes.bfloat16)


def moment_features():
    rows = pixel_monomials()
    rows += [np.zeros_like(rows[0])] * (16 - len(rows))
    return np.stack(rows, axis=1).astype(ml_dtypes.bfloat16)


def split(value, parts):
    out = []
    rest = value
    for part in range(parts):
        head = rest.astype(bf16)
        out.append(head)
        if part < parts - 1:
            rest = rest - head.astype(f32)
    return out


def exact_pick(onehot, value):
    picks = onehot.astype(bf16)
    total = None
    for part in reversed(split(value, 3)):
        term = jnp.dot(picks, part, preferred_element_type=f32)
        total = term if total is None else total + term
    return total


def iota(shape, dim):
    return lax.broadcasted_iota(jnp.int32, shape, dim)


def to_column(row):
    n = row.shape[1]
    spread = jnp.broadcast_to(row, (n, n))
    return jnp.sum(jnp.where(iota((n, n), 0) == iota((n, n), 1), spread, 0.0), axis=1, keepdims=True)


def to_row(column):
    n = column.shape[0]
    spread = jnp.broadcast_to(column, (n, n))
    return jnp.sum(jnp.where(iota((n, n), 0) == iota((n, n), 1), spread, 0.0), axis=0, keepdims=True)


def geometry(mean_x, mean_y, mean_z, log_a, log_b, log_c, quat_w, quat_x, quat_y, quat_z):
    screen_px = float(WIN * TSIDE)
    scales = (jnp.exp(log_a), jnp.exp(log_b), jnp.exp(log_c))
    norm = 1.0 / jnp.sqrt(quat_w * quat_w + quat_x * quat_x + quat_y * quat_y + quat_z * quat_z)
    quat_w, quat_x, quat_y, quat_z = quat_w * norm, quat_x * norm, quat_y * norm, quat_z * norm
    rotation = [
        [
            1 - 2 * (quat_y * quat_y + quat_z * quat_z),
            2 * (quat_x * quat_y - quat_w * quat_z),
            2 * (quat_x * quat_z + quat_w * quat_y),
        ],
        [
            2 * (quat_x * quat_y + quat_w * quat_z),
            1 - 2 * (quat_x * quat_x + quat_z * quat_z),
            2 * (quat_y * quat_z - quat_w * quat_x),
        ],
        [
            2 * (quat_x * quat_z - quat_w * quat_y),
            2 * (quat_y * quat_z + quat_w * quat_x),
            1 - 2 * (quat_x * quat_x + quat_y * quat_y),
        ],
    ]
    focal_px = 0.3125 * screen_px
    inv_z = 1.0 / mean_z
    ratio_x, ratio_y = mean_x * inv_z, mean_y * inv_z
    focal_z = focal_px * inv_z
    rows = []
    for ratio, axis in ((ratio_x, 0), (ratio_y, 1)):
        rows.append(
            [
                focal_z * (rotation[axis][col] - ratio * rotation[2][col]) * scales[col]
                for col in range(3)
            ]
        )
    sigma_xx = rows[0][0] * rows[0][0] + rows[0][1] * rows[0][1] + rows[0][2] * rows[0][2] + 0.3
    sigma_xy = rows[0][0] * rows[1][0] + rows[0][1] * rows[1][1] + rows[0][2] * rows[1][2]
    sigma_yy = rows[1][0] * rows[1][0] + rows[1][1] * rows[1][1] + rows[1][2] * rows[1][2] + 0.3
    inv_det = 1.0 / (sigma_xx * sigma_yy - sigma_xy * sigma_xy)
    return (
        focal_px * ratio_x + (0.5 * screen_px - ORIGIN_X),
        focal_px * ratio_y + (0.5 * screen_px - ORIGIN_Y),
        sigma_yy * inv_det,
        -sigma_xy * inv_det,
        sigma_xx * inv_det,
    )


def harmonics(mean_x, mean_y, mean_z):
    inv_length = 1.0 / jnp.sqrt(mean_x * mean_x + mean_y * mean_y + mean_z * mean_z)
    dir_x, dir_y, dir_z = mean_x * inv_length, mean_y * inv_length, mean_z * inv_length
    sq_x, sq_y, sq_z = dir_x * dir_x, dir_y * dir_y, dir_z * dir_z
    return (
        -harmonic_one * dir_y,
        harmonic_one * dir_z,
        -harmonic_one * dir_x,
        harmonic_two[0] * dir_x * dir_y,
        harmonic_two[1] * dir_y * dir_z,
        harmonic_two[2] * (2 * sq_z - sq_x - sq_y),
        harmonic_two[3] * dir_x * dir_z,
        harmonic_two[4] * (sq_x - sq_y),
        harmonic_three[0] * dir_y * (3 * sq_x - sq_y),
        harmonic_three[1] * dir_x * dir_y * dir_z,
        harmonic_three[2] * dir_y * (4 * sq_z - sq_x - sq_y),
        harmonic_three[3] * dir_z * (2 * sq_z - 3 * sq_x - 3 * sq_y),
        harmonic_three[4] * dir_x * (4 * sq_z - sq_x - sq_y),
        harmonic_three[5] * dir_z * (sq_x - sq_y),
        harmonic_three[6] * dir_x * (sq_x - 3 * sq_y),
    )


def fill_pool(pool, params_ref, low_ref, high_ref):
    for b in range(PLANES):
        if b == 0 or b >= POOL:
            block = low_ref[...]
        elif b == POOL - 1:
            block = high_ref[...]
        else:
            block = params_ref[:, (b - 1) * BLOCK : b * BLOCK]
        pool[b * ROWS : b * ROWS + PARAMS, :] = block


def plane(ref, row):
    return ref[pl.ds(row, PLANES, stride=ROWS), :]


def put_plane(ref, row, value):
    ref[pl.ds(row, PLANES, stride=ROWS), :] = value


def raw_colour(pool, basis, colour):
    total = harmonic_zero * plane(pool, 11 + 16 * colour) + 0.5
    for k in range(1, 16):
        total = total + plane(pool, 11 + 16 * colour + k) * basis[k - 1]
    return total


def scan_forward(table, features, block):
    return jnp.dot(table[block], features, preferred_element_type=f32)


def roll_rows(value, shift):
    return pltpu.roll(value, shift % SUB, axis=0)


def forward_kernel(
    blocks_ref,
    live_ref,
    params_ref,
    low_ref,
    high_ref,
    features_ref,
    pieces_ref,
    table_ref,
    colour_table_ref,
    prefix_ref,
    segment_ref,
    pool,
    stage,
    turned,
    spread,
):
    fill_pool(pool, params_ref, low_ref, high_ref)
    region = lax.axis_index("region")
    regions = lax.axis_size("region")
    block_no = iota((PLANES, BLOCK), 0)
    present = (block_no > 0) & (block_no < POOL - 1)
    present = present | ((block_no == 0) & (region > 0))
    present = present | ((block_no == POOL - 1) & (region < regions - 1))

    means = [plane(pool, r) for r in range(3)]
    centre_u, centre_v, conic_xx, conic_xy, conic_yy = geometry(
        *means, *[plane(pool, r) for r in range(3, 10)]
    )
    opacity = 1.0 / (1.0 + jnp.exp(-plane(pool, 10)))
    log2_e = 1.0 / math.log(2.0)
    slope_x = conic_xx * centre_u + conic_xy * centre_v
    slope_y = conic_xy * centre_u + conic_yy * centre_v
    constant = jnp.log(opacity) - 0.5 * (centre_u * slope_x + centre_v * slope_y)
    constant = jnp.where(present, log2_e * constant, -1e30)
    terms = [
        constant,
        log2_e * slope_x,
        log2_e * slope_y,
        (-0.5 * log2_e) * conic_xx,
        (-log2_e) * conic_xy,
        (-0.5 * log2_e) * conic_yy,
    ]
    row = 0
    for term, copies in zip(terms, (1, 1, 1, 2, 2, 2)):
        parts = [part.astype(f32) for part in split(term, 3)]
        for _ in range(copies):
            for part in parts:
                put_plane(stage, row, part)
                row += 1
    for spare in range(row, ROWS):
        put_plane(stage, spare, jnp.zeros((PLANES, BLOCK), f32))
    basis = harmonics(*means)
    for c in range(3):
        put_plane(stage, 32 + c, jnp.maximum(raw_colour(pool, basis, c), 0.0))

    def turn(b, carry):
        rows = stage[pl.ds(pl.multiple_of(b * ROWS, ROWS), ROWS), :]
        turned[:, :ROWS] = rows.T
        ordered = jnp.concatenate(
            [turned[pl.ds(t, SUB, stride=STEPS), :ROWS] for t in range(STEPS)], axis=0
        )
        table_ref[b] = ordered[:, :32].astype(bf16)
        wide = []
        for c in range(3):
            column = ordered[:, 32 + c : 33 + c]
            spread[b, c] = jnp.broadcast_to(column, (BLOCK, BLOCK))
            wide.append([part for part in split(column, 3)])
        lane = iota((BLOCK, 64), 1)
        order = (0, 0, 0, 1, 1, 2)
        columns = jnp.zeros((BLOCK, 64), f32)
        for group, part in enumerate(order):
            for c in range(3):
                columns = jnp.where(
                    lane == group * 8 + c, jnp.broadcast_to(wide[c][part].astype(f32), (BLOCK, 64)), columns
                )
        colour_table_ref[b] = columns.astype(bf16)
        return carry

    lax.fori_loop(0, POOL, turn, 0)
    lane = iota((BLOCK, 32), 1)
    table_ref[POOL] = jnp.where(lane == 0, -1e30, 0.0).astype(bf16)
    colour_table_ref[POOL] = jnp.zeros((BLOCK, 64), bf16)
    spread[POOL] = jnp.zeros((3, BLOCK, BLOCK), f32)

    sub = iota((SUB, PIX), 0)

    def piece(p, carry):
        first = blocks_ref[p, 0]
        second = jnp.where(live_ref[0, p] > 1, blocks_ref[p, 1], POOL)
        features = features_ref[p]
        before = None
        colours = [None] * 3
        for j, block in enumerate((first, second)):
            exponent = scan_forward(table_ref, features, block)
            transmit = jnp.ones((SUB, PIX), f32)
            sums = [jnp.zeros((SUB, PIX), f32) for _ in range(3)]
            for t in range(STEPS):
                rows = slice(t * SUB, (t + 1) * SUB)
                weight = jnp.exp2(exponent[rows]) * transmit
                transmit = transmit - weight
                for c in range(3):
                    tone = spread[block, c, rows, :]
                    sums[c] = sums[c] + jnp.concatenate([tone, tone], axis=1) * weight
            run = transmit
            for shift in (1, 2, 4):
                run = run * jnp.where(sub >= shift, roll_rows(run, shift), 1.0)
            prefix = jnp.where(sub >= 1, roll_rows(run, 1), 1.0)
            total = run[SUB - 1 :, :]
            if before is not None:
                prefix = prefix * before
                total = total * before
            before = total
            prefix_ref[p, j] = prefix
            for c in range(3):
                piece_sum = prefix * sums[c]
                segment_ref[p, j, c] = piece_sum
                colours[c] = piece_sum if j == 0 else colours[c] + piece_sum
        for c in range(3):
            pieces_ref[pl.ds(p, 1), c * PIX : (c + 1) * PIX] = jnp.sum(
                colours[c], axis=0, keepdims=True
            )
        pieces_ref[pl.ds(p, 1), 3 * PIX :] = 1.0 - before
        return carry

    lax.fori_loop(0, PIECES, piece, 0)


def whole(memory=pltpu.VMEM):
    return pl.BlockSpec(memory_space=memory)


def render(blocks, live, params, low, high, features):
    shape = jax.ShapeDtypeStruct
    return pl.pallas_call(
        forward_kernel,
        out_shape=(
            shape((PIECES, 4 * PIX), f32),
            shape((TAB, BLOCK, 32), bf16),
            shape((TAB, BLOCK, 64), bf16),
            shape((PIECES, 2, SUB, PIX), f32),
            shape((PIECES, 2, 3, SUB, PIX), f32),
        ),
        in_specs=[whole(pltpu.SMEM)] * 2 + [whole()] * 4,
        out_specs=(whole(),) * 5,
        scratch_shapes=[
            pltpu.VMEM((PLANES * ROWS, BLOCK), f32),
            pltpu.VMEM((PLANES * ROWS, BLOCK), f32),
            pltpu.VMEM((BLOCK, BLOCK), f32),
            pltpu.VMEM((TAB, 3, BLOCK, BLOCK), f32),
        ],
        compiler_params=pltpu.CompilerParams(vmem_limit_bytes=VMEM_LIMIT),
        name="render_forward",
    )(blocks, live, params, low, high, features)


def backward_kernel(
    blocks_ref,
    live_ref,
    cotangent_ref,
    params_ref,
    low_ref,
    high_ref,
    features_ref,
    moments_ref,
    table_ref,
    colour_table_ref,
    prefix_ref,
    segment_ref,
    own_ref,
    edge_low_ref,
    edge_high_ref,
    pool,
    stage,
    turned,
    sums,
):
    sums[...] = jnp.zeros_like(sums)
    sub = iota((SUB, PIX), 0)
    nothing = jnp.zeros((16, PIX), bf16)

    def piece(p, carry):
        first = blocks_ref[p, 0]
        second = jnp.where(live_ref[0, p] > 1, blocks_ref[p, 1], POOL)
        features = features_ref[p]
        monomials = moments_ref[p]
        cot = jnp.concatenate(
            [
                cotangent_ref[pl.ds(pl.multiple_of(half * PIECES * SUB + p * SUB, SUB), SUB), :]
                for half in range(2)
            ],
            axis=1,
        )
        heads = [part.astype(f32) for part in split(cot, 3)]
        tones = jnp.concatenate([heads[0], heads[1], heads[2], heads[0], heads[1], heads[0]] + [jnp.zeros((16, PIX), f32)], axis=0)
        tones = tones.astype(bf16)
        colour_rows = jnp.concatenate([heads[0], heads[1]], axis=0).astype(bf16)
        for_gradient = jnp.concatenate([monomials, nothing], axis=0)
        for_weight = jnp.concatenate([nothing, colour_rows], axis=0)
        state = []
        for j, block in enumerate((first, second)):
            exponent = scan_forward(table_ref, features, block)
            tone = scan_forward(colour_table_ref, tones, block)
            transmit = prefix_ref[p, j]
            alphas, weights = [], []
            for t in range(STEPS):
                alpha = jnp.exp2(exponent[t * SUB : (t + 1) * SUB])
                weight = alpha * transmit
                transmit = transmit - weight
                alphas.append(alpha)
                weights.append(weight)
            seen = segment_ref[p, j, 0] * cot[0:1]
            for c in (1, 2):
                seen = seen + segment_ref[p, j, c] * cot[c : c + 1]
            run = seen
            for shift in (1, 2, 4):
                run = run + jnp.where(sub < SUB - shift, roll_rows(run, -shift), 0.0)
            state.append((block, tone, transmit, alphas, weights, run))
        behind = state[1][2][SUB - 1 :, :] * cot[3:4]
        for j in (1, 0):
            block, tone, transmit, alphas, weights, run = state[j]
            after = jnp.where(sub < SUB - 1, roll_rows(run, -1), 0.0) + behind
            behind = behind + run[0:1]
            ahead = after / transmit
            gradients = [None] * STEPS
            for t in reversed(range(STEPS)):
                gap = tone[t * SUB : (t + 1) * SUB] - ahead
                gradients[t] = weights[t] * gap
                ahead = ahead + alphas[t] * gap
            total = None
            for values, rows in ((gradients, for_gradient), (weights, for_weight)):
                for part in split(jnp.concatenate(values, axis=0), 2):
                    term = lax.dot_general(
                        part, rows, (((1,), (1,)), ((), ())), preferred_element_type=f32
                    )
                    total = term if total is None else total + term
            sums[block] = sums[block] + total
        return carry

    lax.fori_loop(0, PIECES, piece, 0)

    def turn(b, carry):
        for t in range(STEPS):
            turned[pl.ds(t, SUB, stride=STEPS), :32] = sums[b, t * SUB : (t + 1) * SUB, :]
        stage[pl.ds(pl.multiple_of(b * ROWS, ROWS), 32), :] = turned[:, :32].T
        return carry

    lax.fori_loop(0, POOL, turn, 0)
    for b in range(POOL, PLANES):
        stage[b * ROWS : b * ROWS + 32, :] = jnp.zeros((32, BLOCK), f32)

    fill_pool(pool, params_ref, low_ref, high_ref)
    means = [plane(pool, r) for r in range(3)]
    (centre_u, centre_v, conic_xx, conic_xy, conic_yy), geometry_pull = jax.vjp(
        geometry, *means, *[plane(pool, r) for r in range(3, 10)]
    )
    basis, harmonics_pull = jax.vjp(harmonics, *means)
    opacity = 1.0 / (1.0 + jnp.exp(-plane(pool, 10)))

    total = plane(stage, 0)
    sum_x, sum_y = plane(stage, 1), plane(stage, 2)
    sum_xx = plane(stage, 3) + plane(stage, 4)
    sum_xy = plane(stage, 5) + plane(stage, 6)
    sum_yy = plane(stage, 7) + plane(stage, 8)
    off_x = sum_x - centre_u * total
    off_y = sum_y - centre_v * total
    grad_xx = -0.5 * (sum_xx - centre_u * (sum_x + off_x))
    grad_xy = -(sum_xy - centre_u * sum_y - centre_v * off_x)
    grad_yy = -0.5 * (sum_yy - centre_v * (sum_y + off_y))
    grad_u = conic_xx * off_x + conic_xy * off_y
    grad_v = conic_xy * off_x + conic_yy * off_y
    grads = geometry_pull((grad_u, grad_v, grad_xx, grad_xy, grad_yy))
    tone_grads = []
    for c in range(3):
        grad = plane(stage, 16 + c) + plane(stage, 24 + c)
        raw = raw_colour(pool, basis, c)
        tone_grads.append(jnp.where(raw > 0, grad, jnp.where(raw == 0, 0.5 * grad, 0.0)))
    basis_grads = []
    for k in range(1, 16):
        basis_grads.append(
            sum(tone_grads[c] * plane(pool, 11 + 16 * c + k) for c in range(3))
        )
    mean_grads = harmonics_pull(tuple(basis_grads))
    for r in range(10):
        put_plane(stage, r, grads[r] + mean_grads[r] if r < 3 else grads[r])
    put_plane(stage, 10, total * (1.0 - opacity))
    for c in range(3):
        put_plane(stage, 11 + 16 * c, tone_grads[c] * harmonic_zero)
        for k in range(1, 16):
            put_plane(stage, 11 + 16 * c + k, tone_grads[c] * basis[k - 1])
    for b in range(POOL):
        block = stage[b * ROWS : b * ROWS + PARAMS, :]
        if b == 0:
            edge_low_ref[...] = block
        elif b == POOL - 1:
            edge_high_ref[...] = block
        else:
            own_ref[:, (b - 1) * BLOCK : b * BLOCK] = block


def pull(blocks, live, cotangent, params, low, high, features, moments, tables):
    shape = jax.ShapeDtypeStruct
    return pl.pallas_call(
        backward_kernel,
        out_shape=(
            shape((PARAMS, BLOCKS * BLOCK), f32),
            shape((PARAMS, BLOCK), f32),
            shape((PARAMS, BLOCK), f32),
        ),
        in_specs=[whole(pltpu.SMEM)] * 2 + [whole()] * 10,
        out_specs=(whole(),) * 3,
        scratch_shapes=[
            pltpu.VMEM((PLANES * ROWS, BLOCK), f32),
            pltpu.VMEM((PLANES * ROWS, BLOCK), f32),
            pltpu.VMEM((BLOCK, BLOCK), f32),
            pltpu.VMEM((TAB, BLOCK, 32), f32),
        ],
        compiler_params=pltpu.CompilerParams(vmem_limit_bytes=VMEM_LIMIT),
        name="render_backward",
    )(blocks, live, cotangent, params, low, high, features, moments, *tables)


def swap_kernel(right_cols, left_cols, right_src, left_src, from_left, from_right, send_sem, recv_sem):
    count = lax.axis_size("region")
    me = lax.axis_index("region")
    right, left = lax.rem(me + 1, count), lax.rem(me + count - 1, count)
    barrier = pltpu.get_barrier_semaphore()
    for other in (left, right):
        pl.semaphore_signal(barrier, inc=1, device_id={"region": other}, device_id_type=MESH)
    pl.semaphore_wait(barrier, 2)
    copies = []
    for k, (src, cols, dst, other) in enumerate(
        ((right_src, right_cols, from_left, right), (left_src, left_cols, from_right, left))
    ):
        copies.append(
            pltpu.make_async_remote_copy(
                src_ref=src.at[:, pl.ds(cols, BLOCK)],
                dst_ref=dst,
                send_sem=send_sem.at[k],
                recv_sem=recv_sem.at[k],
                device_id={"region": other},
                device_id_type=MESH,
            )
        )
    for copy in copies:
        copy.start()
    for copy in copies:
        copy.wait()


def swap(right_src, right_cols, left_src, left_cols, collective_id, name):
    def body(*refs):
        swap_kernel(right_cols, left_cols, *refs)

    return pl.pallas_call(
        body,
        out_shape=(jax.ShapeDtypeStruct((PARAMS, BLOCK), f32),) * 2,
        in_specs=[whole(pl.ANY)] * 2,
        out_specs=(whole(),) * 2,
        scratch_shapes=[pltpu.SemaphoreType.DMA((2,)), pltpu.SemaphoreType.DMA((2,))],
        compiler_params=pltpu.CompilerParams(collective_id=collective_id, has_side_effects=True),
        name=name,
    )(right_src, left_src)


def put_slots(ref, values):
    for k in range(SLOTS):
        for r in range(SUB):
            ref[pl.ds(k * SUB + r, 32, stride=SLOTS * SUB), :] = values[
                k * 32 : (k + 1) * 32, r * BLOCK : (r + 1) * BLOCK
            ]


def get_slots(ref):
    return jnp.concatenate(
        [
            jnp.concatenate(
                [ref[pl.ds(k * SUB + r, 32, stride=SLOTS * SUB), :] for r in range(SUB)], axis=1
            )
            for k in range(SLOTS)
        ],
        axis=0,
    )


def exchange_kernel(
    pieces_ref,
    owner_ref,
    cell_ref,
    target_ref,
    background_ref,
    out_ref,
    sent,
    got,
    labels,
    got_labels,
    replies,
    answers,
    send_sem,
    recv_sem,
    label_send,
    label_recv,
    reply_send,
    reply_recv,
):
    count = lax.axis_size("dom")
    me = lax.axis_index("dom")
    barrier = pltpu.get_barrier_semaphore()

    def greet(d, carry):
        pl.semaphore_signal(
            barrier, inc=1, device_id={"dom": lax.rem(me + d, count)}, device_id_type=MESH
        )
        return carry

    lax.fori_loop(1, count, greet, 0)

    owner_row = owner_ref[...].astype(f32)
    owner_col = to_column(owner_row)
    far_row = owner_row - me.astype(f32)
    far_row = jnp.where(far_row < 0, far_row + float(PIECES), far_row)
    far_col = to_column(far_row)
    same = jnp.broadcast_to(owner_row, (PIECES, PIECES)) == jnp.broadcast_to(owner_col, (PIECES, PIECES))
    first, second = iota((PIECES, PIECES), 0), iota((PIECES, PIECES), 1)
    rank_row = jnp.sum(jnp.where(same & (first < second), 1.0, 0.0), axis=0, keepdims=True)
    rank_col = jnp.sum(jnp.where(same & (second < first), 1.0, 0.0), axis=1, keepdims=True)
    slot_row = rank_row * 32.0 + far_row
    slot_col = rank_col * 32.0 + far_col
    slots = SLOTS * 32
    pack = jnp.broadcast_to(slot_row, (slots, PIECES)) == iota((slots, PIECES), 0).astype(f32)
    pack = jnp.where(pack, 1.0, 0.0)
    unpack = jnp.broadcast_to(slot_col, (PIECES, slots)) == iota((PIECES, slots), 1).astype(f32)
    unpack = jnp.where(unpack, 1.0, 0.0)
    cell_row = cell_ref[...].astype(f32) + 1.0
    label_col = jnp.sum(pack * cell_row, axis=1, keepdims=True) - 1.0

    put_slots(sent, exact_pick(pack, pieces_ref[...]))
    lane = iota((32, BLOCK), 1)
    label_rows = jnp.where(lane == 0, label_col[:32], jnp.where(lane == 1, label_col[32:], -1.0))
    for d in range(32):
        labels[d] = label_rows[d : d + 1]

    pl.semaphore_wait(barrier, count - 1)

    def payload(d):
        rows = pl.ds(pl.multiple_of(d * SLOTS * SUB, SLOTS * SUB), SLOTS * SUB)
        return pltpu.make_async_remote_copy(
            src_ref=sent.at[rows],
            dst_ref=got.at[rows],
            send_sem=send_sem.at[d],
            recv_sem=recv_sem.at[d],
            device_id={"dom": lax.rem(me + d, count)},
            device_id_type=MESH,
        )

    def label(d):
        return pltpu.make_async_remote_copy(
            src_ref=labels.at[d],
            dst_ref=got_labels.at[d],
            send_sem=label_send.at[d],
            recv_sem=label_recv.at[d],
            device_id={"dom": lax.rem(me + d, count)},
            device_id_type=MESH,
        )

    def reply(d):
        rows = pl.ds(pl.multiple_of(d * SLOTS * SUB, SLOTS * SUB), SLOTS * SUB)
        return pltpu.make_async_remote_copy(
            src_ref=replies.at[rows],
            dst_ref=answers.at[rows],
            send_sem=reply_send.at[d],
            recv_sem=reply_recv.at[d],
            device_id={"dom": lax.rem(me + count - d, count)},
            device_id_type=MESH,
        )

    def start_out(d, carry):
        payload(d).start()
        label(d).start()
        return carry

    def wait_out(d, carry):
        payload(d).wait()
        label(d).wait()
        return carry

    lax.fori_loop(1, count, start_out, 0)
    got[: SLOTS * SUB] = sent[: SLOTS * SUB]
    got_labels[0] = labels[0]
    lax.fori_loop(1, count, wait_out, 0)

    arrived = jnp.concatenate([got_labels[d] for d in range(32)], axis=0)
    arrived_col = jnp.concatenate([arrived[:, 0:1], arrived[:, 1:2]], axis=0)
    arrived_row = to_row(arrived_col)

    def cell_of(place):
        return ((place % TILE_DEV) * MAXD + place // TILE_DEV).astype(f32)

    gather = jnp.broadcast_to(arrived_row, (CELLS, slots)) == cell_of(iota((CELLS, slots), 0))
    gather = jnp.where(gather, 1.0, 0.0)
    scatter = jnp.broadcast_to(arrived_col, (slots, CELLS)) == cell_of(iota((slots, CELLS), 1))
    scatter = jnp.where(scatter, 1.0, 0.0)
    grid = exact_pick(gather, get_slots(got))

    def at(depth, channel):
        return grid[depth * SUB : (depth + 1) * SUB, channel * PIX : (channel + 1) * PIX]

    in_front = jnp.ones((TILE_DEV, PIX), f32)
    composite = [jnp.zeros((TILE_DEV, PIX), f32) for _ in range(3)]
    fronts = []
    for depth in range(MAXD):
        fronts.append(in_front)
        composite = [composite[c] + in_front * at(depth, c) for c in range(3)]
        in_front = in_front * (1.0 - at(depth, 3))
    residual = [
        composite[c] + in_front * background_ref[c] - target_ref[0, :, c, :] for c in range(3)
    ]
    behind = [jnp.full((TILE_DEV, PIX), background_ref[c], f32) for c in range(3)]
    rows = [None] * MAXD
    for depth in reversed(range(MAXD)):
        seen = residual[0] * behind[0] + residual[1] * behind[1] + residual[2] * behind[2]
        rows[depth] = jnp.concatenate(
            [fronts[depth] * residual[c] for c in range(3)] + [fronts[depth] * seen], axis=1
        )
        through = 1.0 - at(depth, 3)
        behind = [at(depth, c) + through * behind[c] for c in range(3)]
    put_slots(replies, exact_pick(scatter, jnp.concatenate(rows, axis=0)))

    def start_back(d, carry):
        reply(d).start()
        return carry

    def wait_back(d, carry):
        reply(d).wait()
        return carry

    lax.fori_loop(1, count, start_back, 0)
    answers[: SLOTS * SUB] = replies[: SLOTS * SUB]
    lax.fori_loop(1, count, wait_back, 0)

    cotangent = exact_pick(unpack, get_slots(answers))
    for half in range(2):
        for c in range(SUB):
            lanes = slice(c * PIX + half * BLOCK, c * PIX + (half + 1) * BLOCK)
            rows = cotangent[:, lanes] if c < 4 else jnp.zeros((PIECES, BLOCK), f32)
            out_ref[pl.ds(half * PIECES * SUB + c, PIECES, stride=SUB), :] = rows


def exchange(pieces, owner, cell, target, background):
    slots = pltpu.VMEM((32 * SLOTS * SUB, BLOCK), f32)
    label = pltpu.VMEM((32, 1, BLOCK), f32)
    return pl.pallas_call(
        exchange_kernel,
        out_shape=jax.ShapeDtypeStruct((2 * PIECES * SUB, BLOCK), f32),
        in_specs=[whole()] * 4 + [whole(pltpu.SMEM)],
        out_specs=whole(),
        scratch_shapes=[slots, slots, label, label, slots, slots]
        + [pltpu.SemaphoreType.DMA((32,))] * 6,
        compiler_params=pltpu.CompilerParams(
            collective_id=1, has_side_effects=True, vmem_limit_bytes=VMEM_LIMIT
        ),
        name="tiles_to_owners",
    )(pieces, owner, cell, target, background)


def adam_kernel(
    own_ref, from_left_ref, from_right_ref, params_ref, first_ref, second_ref,
    gradient_ref, new_params_ref, new_first_ref, new_second_ref,
):
    for b in range(BLOCKS):
        cols = slice(b * BLOCK, (b + 1) * BLOCK)
        gradient = own_ref[:, cols]
        if b == 0:
            gradient = gradient + from_left_ref[...]
        if b == BLOCKS - 1:
            gradient = gradient + from_right_ref[...]
        new_first = beta_one * first_ref[:, cols] + (1 - beta_one) * gradient
        new_second = beta_two * second_ref[:, cols] + (1 - beta_two) * gradient * gradient
        update = (
            new_first
            / (1 - beta_one**adam_step)
            / (jnp.sqrt(new_second / (1 - beta_two**adam_step)) + tiny)
        )
        gradient_ref[:, cols] = gradient
        new_params_ref[:, cols] = params_ref[:, cols] - rate * update
        new_first_ref[:, cols] = new_first
        new_second_ref[:, cols] = new_second


def adam(own, from_left, from_right, params, first, second):
    return pl.pallas_call(
        adam_kernel,
        out_shape=(jax.ShapeDtypeStruct((PARAMS, BLOCKS * BLOCK), f32),) * 4,
        in_specs=[whole()] * 6,
        out_specs=(whole(),) * 4,
        name="adam",
    )(own, from_left, from_right, params, first, second)


def on_device(
    params,
    first_moment,
    second_moment,
    piece_blocks,
    piece_live,
    piece_owner,
    piece_cell,
    target,
    background,
):
    features = jnp.asarray(exponent_features())
    moments = jnp.asarray(moment_features())
    blocks = piece_blocks[0]
    low, high = swap(params, (BLOCKS - 1) * BLOCK, params, 0, 0, "cut_blocks")
    pieces, *tables = render(blocks, piece_live, params, low, high, features)
    cotangent = exchange(pieces, piece_owner, piece_cell, target, background)
    own, edge_low, edge_high = pull(
        blocks, piece_live, cotangent, params, low, high, features, moments, tables
    )
    from_left, from_right = swap(edge_high, 0, edge_low, 0, 2, "cut_gradients")
    return adam(own, from_left, from_right, params, first_moment, second_moment)


def solution(mesh):
    in_specs = (
        P(None, ("region", "dom")),
        P(None, ("region", "dom")),
        P(None, ("region", "dom")),
        P(("region", "dom"), None, None),
        P(("region", "dom"), None),
        P(("region", "dom"), None),
        P(("region", "dom"), None),
        P(("region", "dom"), None, None, None),
        P(),
    )
    out_specs = (
        P(None, ("region", "dom")),
        P(None, ("region", "dom")),
        P(None, ("region", "dom")),
        P(None, ("region", "dom")),
    )
    return jax.shard_map(
        on_device, mesh=mesh, in_specs=in_specs, out_specs=out_specs, check_vma=False
    )
```

```python
import math

import jax
import jax.numpy as jnp
import ml_dtypes
import numpy as np
from jax import lax
from jax.experimental import pallas as pl
from jax.experimental.pallas import tpu as pltpu
from jax.sharding import PartitionSpec as P

PARAMS = 59
TSIDE = 16
WIN = 8
BLOCK = 128
BLOCKS = 8
MAXD = 8
PIECES = 32
PIX = 256
TILE_DEV = 8
CELLS = 64
POOL = 10
SLOTS = 2
SUB = 8
STEPS = BLOCK // SUB
TAB = POOL + 1
PLANES = 16
ROWS = 64
COLS = 96
UNROLL = 4
HALVES = 2
WIDE = PIX // HALVES
LOW = BLOCKS
HIGH = BLOCKS + 1
DEAD = POOL
ORIGIN_X = 64.0
ORIGIN_Y = 32.0

harmonic_zero = 0.28209479177387814
harmonic_one = 0.4886025119029199
harmonic_two = (
    1.0925484305920792,
    -1.0925484305920792,
    0.31539156525252005,
    -1.0925484305920792,
    0.5462742152960396,
)
harmonic_three = (
    -0.5900435899266435,
    2.890611442640554,
    -0.4570457994644658,
    0.3731763325901154,
    -0.4570457994644658,
    1.445305721320277,
    -0.5900435899266435,
)
beta_one = 0.9
beta_two = 0.999
rate = 0.001
adam_step = 100
tiny = 1e-08

f32 = jnp.float32
bf16 = jnp.bfloat16
MESH = pl.DeviceIdType.MESH
VMEM_LIMIT = 32 * 1024 * 1024


def pixel_monomials():
    bf = ml_dtypes.bfloat16
    tile = np.arange(PIECES)[:, None]
    pixel = np.arange(PIX)[None, :]
    x = (TSIDE * (tile % WIN) + pixel % TSIDE + 0.5 - ORIGIN_X).astype(np.float32)
    y = (TSIDE * (tile // WIN) + pixel // TSIDE + 0.5 - ORIGIN_Y).astype(np.float32)

    def two(value):
        head = value.astype(bf).astype(np.float32)
        return [head, value - head]

    return [np.ones_like(x), x, y] + two(x * x) + two(x * y) + two(y * y)


def exponent_features():
    rows = [row for row in pixel_monomials() for _ in range(3)]
    rows += [np.zeros_like(rows[0])] * (32 - len(rows))
    return np.stack(rows, axis=1).astype(ml_dtypes.bfloat16)


def moment_features():
    rows = pixel_monomials()
    rows += [np.zeros_like(rows[0])] * (16 - len(rows))
    return np.stack(rows, axis=1).astype(ml_dtypes.bfloat16)


def split(value, parts):
    out = []
    rest = value
    for part in range(parts):
        head = rest.astype(bf16)
        out.append(head)
        if part < parts - 1:
            rest = rest - head.astype(f32)
    return out


def exact_pick(onehot, value):
    picks = onehot.astype(bf16)
    total = None
    for part in reversed(split(value, 3)):
        term = jnp.dot(picks, part, preferred_element_type=f32)
        total = term if total is None else total + term
    return total


def iota(shape, dim):
    return lax.broadcasted_iota(jnp.int32, shape, dim)


def to_column(row):
    n = row.shape[1]
    spread = jnp.broadcast_to(row, (n, n))
    return jnp.sum(jnp.where(iota((n, n), 0) == iota((n, n), 1), spread, 0.0), axis=1, keepdims=True)


def to_row(column):
    n = column.shape[0]
    spread = jnp.broadcast_to(column, (n, n))
    return jnp.sum(jnp.where(iota((n, n), 0) == iota((n, n), 1), spread, 0.0), axis=0, keepdims=True)


def geometry(mean_x, mean_y, mean_z, log_a, log_b, log_c, quat_w, quat_x, quat_y, quat_z):
    screen_px = float(WIN * TSIDE)
    scales = (jnp.exp(log_a), jnp.exp(log_b), jnp.exp(log_c))
    norm = 1.0 / jnp.sqrt(quat_w * quat_w + quat_x * quat_x + quat_y * quat_y + quat_z * quat_z)
    quat_w, quat_x, quat_y, quat_z = quat_w * norm, quat_x * norm, quat_y * norm, quat_z * norm
    rotation = [
        [
            1 - 2 * (quat_y * quat_y + quat_z * quat_z),
            2 * (quat_x * quat_y - quat_w * quat_z),
            2 * (quat_x * quat_z + quat_w * quat_y),
        ],
        [
            2 * (quat_x * quat_y + quat_w * quat_z),
            1 - 2 * (quat_x * quat_x + quat_z * quat_z),
            2 * (quat_y * quat_z - quat_w * quat_x),
        ],
        [
            2 * (quat_x * quat_z - quat_w * quat_y),
            2 * (quat_y * quat_z + quat_w * quat_x),
            1 - 2 * (quat_x * quat_x + quat_y * quat_y),
        ],
    ]
    focal_px = 0.3125 * screen_px
    inv_z = 1.0 / mean_z
    ratio_x, ratio_y = mean_x * inv_z, mean_y * inv_z
    focal_z = focal_px * inv_z
    rows = []
    for ratio, axis in ((ratio_x, 0), (ratio_y, 1)):
        rows.append(
            [
                focal_z * (rotation[axis][col] - ratio * rotation[2][col]) * scales[col]
                for col in range(3)
            ]
        )
    sigma_xx = rows[0][0] * rows[0][0] + rows[0][1] * rows[0][1] + rows[0][2] * rows[0][2] + 0.3
    sigma_xy = rows[0][0] * rows[1][0] + rows[0][1] * rows[1][1] + rows[0][2] * rows[1][2]
    sigma_yy = rows[1][0] * rows[1][0] + rows[1][1] * rows[1][1] + rows[1][2] * rows[1][2] + 0.3
    inv_det = 1.0 / (sigma_xx * sigma_yy - sigma_xy * sigma_xy)
    return (
        focal_px * ratio_x + (0.5 * screen_px - ORIGIN_X),
        focal_px * ratio_y + (0.5 * screen_px - ORIGIN_Y),
        sigma_yy * inv_det,
        -sigma_xy * inv_det,
        sigma_xx * inv_det,
    )


def harmonics(mean_x, mean_y, mean_z):
    inv_length = 1.0 / jnp.sqrt(mean_x * mean_x + mean_y * mean_y + mean_z * mean_z)
    dir_x, dir_y, dir_z = mean_x * inv_length, mean_y * inv_length, mean_z * inv_length
    sq_x, sq_y, sq_z = dir_x * dir_x, dir_y * dir_y, dir_z * dir_z
    return (
        -harmonic_one * dir_y,
        harmonic_one * dir_z,
        -harmonic_one * dir_x,
        harmonic_two[0] * dir_x * dir_y,
        harmonic_two[1] * dir_y * dir_z,
        harmonic_two[2] * (2 * sq_z - sq_x - sq_y),
        harmonic_two[3] * dir_x * dir_z,
        harmonic_two[4] * (sq_x - sq_y),
        harmonic_three[0] * dir_y * (3 * sq_x - sq_y),
        harmonic_three[1] * dir_x * dir_y * dir_z,
        harmonic_three[2] * dir_y * (4 * sq_z - sq_x - sq_y),
        harmonic_three[3] * dir_z * (2 * sq_z - 3 * sq_x - 3 * sq_y),
        harmonic_three[4] * dir_x * (4 * sq_z - sq_x - sq_y),
        harmonic_three[5] * dir_z * (sq_x - sq_y),
        harmonic_three[6] * dir_x * (sq_x - 3 * sq_y),
    )


def plane(ref, half, row):
    return ref[pl.ds(half * SUB * ROWS + row, SUB, stride=ROWS), :]


def put_plane(ref, half, row, value):
    ref[pl.ds(half * SUB * ROWS + row, SUB, stride=ROWS), :] = value


def raw_colour(pool, half, basis, colour):
    total = harmonic_zero * plane(pool, half, 11 + 16 * colour) + 0.5
    for k in range(1, 16):
        total = total + plane(pool, half, 11 + 16 * colour + k) * basis[k - 1]
    return total


def own_block(number):
    return jnp.where(number == 0, LOW, jnp.where(number == POOL - 1, HIGH, number - 1))


def roll_rows(value, shift):
    return pltpu.roll(value, shift % SUB, axis=0)


def tabulate(half, count, pool, stage, turned, table, spread):
    region = lax.axis_index("region")
    regions = lax.axis_size("region")
    means = [plane(pool, half, r) for r in range(3)]
    centre_u, centre_v, conic_xx, conic_xy, conic_yy = geometry(
        *means, *[plane(pool, half, r) for r in range(3, 10)]
    )
    opacity = 1.0 / (1.0 + jnp.exp(-plane(pool, half, 10)))
    log2_e = 1.0 / math.log(2.0)
    slope_x = conic_xx * centre_u + conic_xy * centre_v
    slope_y = conic_xy * centre_u + conic_yy * centre_v
    constant = jnp.log(opacity) - 0.5 * (centre_u * slope_x + centre_v * slope_y)
    constant = log2_e * constant
    if half:
        row = iota((SUB, BLOCK), 0)
        absent = ((row == LOW - SUB) & (region == 0)) | ((row == HIGH - SUB) & (region == regions - 1))
        constant = jnp.where(absent, -1e30, constant)
    terms = [
        constant,
        log2_e * slope_x,
        log2_e * slope_y,
        (-0.5 * log2_e) * conic_xx,
        (-log2_e) * conic_xy,
        (-0.5 * log2_e) * conic_yy,
    ]
    stage[...] = jnp.zeros_like(stage)

    def put(row, value):
        stage[pl.ds(row, SUB, stride=COLS), :] = value

    row = 0
    for term, copies in zip(terms, (1, 1, 1, 2, 2, 2)):
        parts = [part.astype(f32) for part in split(term, 3)]
        for _ in range(copies):
            for part in parts:
                put(row, part)
                row += 1
    basis = harmonics(*means)
    for c in range(3):
        tone = jnp.maximum(raw_colour(pool, half, basis, c), 0.0)
        parts = [part.astype(f32) for part in split(tone, 3)]
        for group, part in enumerate((0, 0, 0, 1, 1, 2)):
            put(32 + group * SUB + c, parts[part])
        put(80 + c, tone)

    def turn(b, carry):
        turned[:, :COLS] = stage[pl.ds(pl.multiple_of(b * COLS, COLS), COLS), :].T
        ordered = jnp.concatenate(
            [turned[pl.ds(t, SUB, stride=STEPS), :] for t in range(STEPS)], axis=0
        )
        table[half * SUB + b] = ordered[:, :COLS].astype(bf16)
        for c in range(3):
            spread[half * SUB + b, c] = jnp.broadcast_to(ordered[:, 80 + c : 81 + c], (BLOCK, BLOCK))
        return carry

    lax.fori_loop(0, count, turn, 0, unroll=2)


def exponents(table, features, block):
    return jnp.dot(table[block, :, :32], features, preferred_element_type=f32)


def two_blocks(p, blocks, live):
    first = own_block(blocks[0, p])
    second = jnp.where(live[0, p] > 1, own_block(blocks[1, p]), DEAD)
    return first, second


def forward_half(h, blocks, live, features_ref, table, spread, prefix_ref, segment_ref, pieces):
    sub = iota((SUB, WIDE), 0)

    def piece(p, carry):
        features = features_ref[p, :, h * WIDE : (h + 1) * WIDE]
        before = None
        colours = [None] * 3
        for j, block in enumerate(two_blocks(p, blocks, live)):
            exponent = exponents(table, features, block)
            transmit = jnp.ones((SUB, WIDE), f32)
            sums = [jnp.zeros((SUB, WIDE), f32) for _ in range(3)]
            for t in range(STEPS):
                rows = slice(t * SUB, (t + 1) * SUB)
                weight = jnp.exp2(exponent[rows]) * transmit
                transmit = transmit - weight
                for c in range(3):
                    tone = spread[block, c, rows, :]
                    tone = tone if WIDE == BLOCK else jnp.concatenate([tone, tone], axis=1)
                    sums[c] = sums[c] + tone * weight
            run = transmit
            for shift in (1, 2, 4):
                run = run * jnp.where(sub >= shift, roll_rows(run, shift), 1.0)
            prefix = jnp.where(sub >= 1, roll_rows(run, 1), 1.0)
            total = run[SUB - 1 :, :]
            if before is not None:
                prefix = prefix * before
                total = total * before
            before = total
            prefix_ref[h, p, j] = prefix
            for c in range(3):
                piece_sum = prefix * sums[c]
                segment_ref[h, p, j, c] = piece_sum
                colours[c] = piece_sum if j == 0 else colours[c] + piece_sum
        rows = [jnp.sum(colours[c], axis=0, keepdims=True) for c in range(3)] + [1.0 - before]
        for c in range(4):
            for k in range(WIDE // BLOCK):
                place = (c * (WIDE // BLOCK) + k) * PIECES + p
                pieces[pl.ds(place, 1), :] = rows[c][:, k * BLOCK : (k + 1) * BLOCK]
        return carry

    lax.fori_loop(0, PIECES, piece, 0, unroll=UNROLL)


def backward_half(
    h, blocks, live, features_ref, moments_ref, table, prefix_ref, segment_ref, cotangent, moved
):
    sub = iota((SUB, WIDE), 0)
    nothing = jnp.zeros((16, WIDE), bf16)
    none = jnp.zeros((16, WIDE), f32)
    lanes = slice(h * WIDE, (h + 1) * WIDE)

    def piece(p, carry):
        features = features_ref[p, :, lanes]
        monomials = moments_ref[p, :, lanes]
        cot = jnp.concatenate(
            [
                cotangent[pl.ds(pl.multiple_of((k * PIECES + p) * SUB, SUB), SUB), :]
                for k in range(WIDE // BLOCK)
            ],
            axis=1,
        )
        heads = [part.astype(f32) for part in split(cot, 3)]
        tones = [none, none] + [heads[part] for part in (0, 1, 2, 0, 1, 0)] + [none]
        tones = jnp.concatenate(tones, axis=0).astype(bf16)
        colour_rows = jnp.concatenate([heads[0], heads[1]], axis=0).astype(bf16)
        for_gradient = jnp.concatenate([monomials, nothing], axis=0)
        for_weight = jnp.concatenate([nothing, colour_rows], axis=0)
        state = []
        for j, block in enumerate(two_blocks(p, blocks, live)):
            exponent = exponents(table, features, block)
            tone = jnp.dot(table[block], tones, preferred_element_type=f32)
            transmit = prefix_ref[h, p, j]
            alphas, weights = [], []
            for t in range(STEPS):
                alpha = jnp.exp2(exponent[t * SUB : (t + 1) * SUB])
                weight = alpha * transmit
                transmit = transmit - weight
                alphas.append(alpha)
                weights.append(weight)
            seen = segment_ref[h, p, j, 0] * cot[0:1]
            for c in (1, 2):
                seen = seen + segment_ref[h, p, j, c] * cot[c : c + 1]
            run = seen
            for shift in (1, 2, 4):
                run = run + jnp.where(sub < SUB - shift, roll_rows(run, -shift), 0.0)
            state.append((tone, transmit, alphas, weights, run))
        behind = state[1][1][SUB - 1 :, :] * cot[3:4]
        parts = [None, None]
        for j in (1, 0):
            tone, transmit, alphas, weights, run = state[j]
            after = jnp.where(sub < SUB - 1, roll_rows(run, -1), 0.0) + behind
            behind = behind + run[0:1]
            ahead = after / transmit
            gradients = [None] * STEPS
            for t in reversed(range(STEPS)):
                gap = tone[t * SUB : (t + 1) * SUB] - ahead
                gradients[t] = weights[t] * gap
                ahead = ahead + alphas[t] * gap
            parts[j] = split(jnp.concatenate(gradients, axis=0), 2)
            parts[j] += split(jnp.concatenate(weights, axis=0), 2)
        total = None
        for k in range(4):
            term = lax.dot_general(
                (for_gradient, for_weight)[k // 2],
                jnp.concatenate([parts[0][k], parts[1][k]], axis=0),
                (((1,), (1,)), ((), ())),
                preferred_element_type=f32,
            )
            total = term if total is None else total + term
        for j in range(2):
            rows = pl.ds(pl.multiple_of((j * PIECES + p) * 32, 32), 32)
            part = total[:, j * BLOCK : (j + 1) * BLOCK]
            moved[rows, :] = part if h == 0 else moved[rows, :] + part
        return carry

    lax.fori_loop(0, PIECES, piece, 0, unroll=UNROLL)


def gather_moments(first_row, second_row, moved, summed):
    numbers = iota((2 * SUB, PIECES), 0).astype(f32)
    lane = iota((BLOCK, BLOCK), 0)
    unshuffle = (lane % SUB) * STEPS + lane // SUB == iota((BLOCK, BLOCK), 1)
    unshuffle = jnp.where(unshuffle, 1.0, 0.0).astype(bf16)
    for group in range(3):
        features = range(group * SUB, group * SUB + SUB)
        features = [f for f in features if f < 9] + [16 + f - 9 for f in features if 9 <= f < 12]
        features += [24 + f - 12 for f in range(group * SUB, group * SUB + SUB) if 12 <= f < 15]
        if not features:
            continue
        total = None
        for j, row in enumerate((first_row, second_row)):
            pick = jnp.where(jnp.broadcast_to(row, (2 * SUB, PIECES)) == numbers, 1.0, 0.0)
            values = [
                moved[pl.ds(j * PIECES * 32 + f, PIECES, stride=32), :] for f in features
            ]
            term = exact_pick(pick, jnp.concatenate(values, axis=1))
            total = term if total is None else total + term
        stacked = jnp.concatenate(
            [total[:, k * BLOCK : (k + 1) * BLOCK] for k in range(len(features))], axis=0
        )
        ordered = None
        for part in reversed(split(stacked, 3)):
            term = jnp.dot(part, unshuffle, preferred_element_type=f32)
            ordered = term if ordered is None else ordered + term
        for k, f in enumerate(features):
            summed[f] = ordered[k * 2 * SUB : (k + 1) * 2 * SUB]


def pull_splat(half, pool, summed, grads_ref):
    means = [plane(pool, half, r) for r in range(3)]
    (centre_u, centre_v, conic_xx, conic_xy, conic_yy), geometry_pull = jax.vjp(
        geometry, *means, *[plane(pool, half, r) for r in range(3, 10)]
    )
    basis, harmonics_pull = jax.vjp(harmonics, *means)
    opacity = 1.0 / (1.0 + jnp.exp(-plane(pool, half, 10)))
    sums = [summed[f, half * SUB : (half + 1) * SUB] for f in range(9)]
    total, sum_x, sum_y = sums[:3]
    sum_xx, sum_xy, sum_yy = sums[3] + sums[4], sums[5] + sums[6], sums[7] + sums[8]
    off_x = sum_x - centre_u * total
    off_y = sum_y - centre_v * total
    grad_xx = -0.5 * (sum_xx - centre_u * (sum_x + off_x))
    grad_xy = -(sum_xy - centre_u * sum_y - centre_v * off_x)
    grad_yy = -0.5 * (sum_yy - centre_v * (sum_y + off_y))
    grad_u = conic_xx * off_x + conic_xy * off_y
    grad_v = conic_xy * off_x + conic_yy * off_y
    grads = geometry_pull((grad_u, grad_v, grad_xx, grad_xy, grad_yy))
    tone_grads = []
    for c in range(3):
        grad = summed[16 + c, half * SUB : (half + 1) * SUB] + summed[24 + c, half * SUB : (half + 1) * SUB]
        raw = raw_colour(pool, half, basis, c)
        tone_grads.append(jnp.where(raw > 0, grad, jnp.where(raw == 0, 0.5 * grad, 0.0)))
    basis_grads = []
    for k in range(1, 16):
        basis_grads.append(
            sum(tone_grads[c] * plane(pool, half, 11 + 16 * c + k) for c in range(3))
        )
    mean_grads = harmonics_pull(tuple(basis_grads))
    for r in range(10):
        put_plane(grads_ref, half, r, grads[r] + mean_grads[r] if r < 3 else grads[r])
    put_plane(grads_ref, half, 10, total * (1.0 - opacity))
    for c in range(3):
        put_plane(grads_ref, half, 11 + 16 * c, tone_grads[c] * harmonic_zero)
        for k in range(1, 16):
            put_plane(grads_ref, half, 11 + 16 * c + k, tone_grads[c] * basis[k - 1])


PARTS = 4 * WIDE // BLOCK
MESSAGE = SLOTS * PARTS


def put_slots(ref, values):
    for k in range(SLOTS):
        for r in range(PARTS):
            ref[pl.ds(k * PARTS + r, 32, stride=MESSAGE), :] = values[
                k * 32 : (k + 1) * 32, r * BLOCK : (r + 1) * BLOCK
            ]


def get_slots(ref):
    return jnp.concatenate(
        [
            jnp.concatenate(
                [ref[pl.ds(k * PARTS + r, 32, stride=MESSAGE), :] for r in range(PARTS)], axis=1
            )
            for k in range(SLOTS)
        ],
        axis=0,
    )


def route(owner_row, cell_row, me):
    owner_col = to_column(owner_row)
    far_row = owner_row - me.astype(f32)
    far_row = jnp.where(far_row < 0, far_row + float(PIECES), far_row)
    far_col = to_column(far_row)
    square = (PIECES, PIECES)
    same = jnp.broadcast_to(owner_row, square) == jnp.broadcast_to(owner_col, square)
    first, second = iota(square, 0), iota(square, 1)
    rank_row = jnp.sum(jnp.where(same & (first < second), 1.0, 0.0), axis=0, keepdims=True)
    rank_col = jnp.sum(jnp.where(same & (second < first), 1.0, 0.0), axis=1, keepdims=True)
    slots = SLOTS * 32
    pack = jnp.broadcast_to(rank_row * 32.0 + far_row, (slots, PIECES)) == iota((slots, PIECES), 0).astype(f32)
    pack = jnp.where(pack, 1.0, 0.0)
    unpack = jnp.broadcast_to(rank_col * 32.0 + far_col, (PIECES, slots)) == iota((PIECES, slots), 1).astype(f32)
    unpack = jnp.where(unpack, 1.0, 0.0)
    label_col = jnp.sum(pack * (cell_row + 1.0), axis=1, keepdims=True) - 1.0
    lane = iota((32, BLOCK), 1)
    label_rows = jnp.where(lane == 0, label_col[:32], jnp.where(lane == 1, label_col[32:], -1.0))
    return pack, unpack, label_rows


def composite(h, grid, target, background):
    def at(depth, channel):
        return grid[depth * SUB : (depth + 1) * SUB, channel * WIDE : (channel + 1) * WIDE]

    in_front = jnp.ones((TILE_DEV, WIDE), f32)
    seen = [jnp.zeros((TILE_DEV, WIDE), f32) for _ in range(3)]
    fronts = []
    for depth in range(MAXD):
        fronts.append(in_front)
        seen = [seen[c] + in_front * at(depth, c) for c in range(3)]
        in_front = in_front * (1.0 - at(depth, 3))
    residual = [
        seen[c] + in_front * background[c] - target[c, :, h * WIDE : (h + 1) * WIDE] for c in range(3)
    ]
    behind = [jnp.full((TILE_DEV, WIDE), background[c], f32) for c in range(3)]
    rows = [None] * MAXD
    for depth in reversed(range(MAXD)):
        through = 1.0 - at(depth, 3)
        by_trans = residual[0] * behind[0] + residual[1] * behind[1] + residual[2] * behind[2]
        rows[depth] = jnp.concatenate(
            [fronts[depth] * residual[c] for c in range(3)] + [fronts[depth] * by_trans], axis=1
        )
        behind = [at(depth, c) + through * behind[c] for c in range(3)]
    return jnp.concatenate(rows, axis=0)


def step_kernel(
    params_hbm,
    blocks_hbm,
    live_hbm,
    owner_hbm,
    cell_hbm,
    target_hbm,
    background_hbm,
    features_hbm,
    moments_hbm,
    grads_ref,
    from_left,
    from_right,
    blocks,
    live,
    background,
    block_rows,
    owner,
    cell,
    target,
    features,
    moments,
    pool,
    stage,
    turned,
    table,
    spread,
    prefix,
    segment,
    pieces,
    sent,
    got,
    replies,
    answers,
    labels,
    got_labels,
    cotangent,
    moved,
    summed,
    local_sem,
    halo_send,
    halo_recv,
    edge_send,
    edge_recv,
    label_send,
    label_recv,
    send_sem,
    recv_sem,
    reply_send,
    reply_recv,
):
    regions, region = lax.axis_size("region"), lax.axis_index("region")
    count, me = lax.axis_size("dom"), lax.axis_index("dom")
    upper, lower = lax.rem(region + 1, regions), lax.rem(region + regions - 1, regions)

    def block_rows_of(ref, b):
        return ref.at[pl.ds(b * ROWS, PARAMS)]

    fetches = []

    def fetch(src, dst):
        copy = pltpu.make_async_copy(src, dst, local_sem.at[len(fetches)])
        copy.start()
        fetches.append(copy)
        return copy

    routing = [fetch(owner_hbm, owner), fetch(cell_hbm, cell)]
    own = [
        fetch(params_hbm.at[:, pl.ds(b * BLOCK, BLOCK)], block_rows_of(pool, b)) for b in range(BLOCKS)
    ]
    scalars = [fetch(blocks_hbm, blocks), fetch(live_hbm, live), fetch(features_hbm, features)]
    later = [
        fetch(blocks_hbm, block_rows),
        fetch(target_hbm, target),
        fetch(background_hbm, background),
        fetch(moments_hbm, moments),
    ]

    barrier = pltpu.get_barrier_semaphore()

    def signal(**where):
        pl.semaphore_signal(barrier, inc=1, device_id=where, device_id_type=MESH)

    def greet(d, carry):
        signal(dom=lax.rem(me + d, count))
        return carry

    signal(region=upper)
    signal(region=lower)
    lax.fori_loop(1, count, greet, 0)

    for copy in routing:
        copy.wait()
    pack, unpack, label_rows = route(owner[...].astype(f32), cell[...].astype(f32), me)
    for d in range(32):
        labels[d] = label_rows[d : d + 1]
    pl.semaphore_wait(barrier, count + 1)

    def remote(src, dst, send, recv, **where):
        return pltpu.make_async_remote_copy(
            src_ref=src, dst_ref=dst, send_sem=send, recv_sem=recv, device_id=where, device_id_type=MESH
        )

    def label(d):
        where = lax.rem(me + d, count)
        return remote(labels.at[d], got_labels.at[d], label_send.at[d], label_recv.at[d], dom=where)

    def message(d):
        return pl.ds(pl.multiple_of(d * MESSAGE, MESSAGE), MESSAGE)

    def payload(h, d):
        where = lax.rem(me + d, count)
        rows = message(d)
        return remote(sent.at[h, rows], got.at[h, rows], send_sem.at[h, d], recv_sem.at[h, d], dom=where)

    def reply(h, d):
        where = lax.rem(me + count - d, count)
        rows = message(d)
        return remote(
            replies.at[h, rows], answers.at[h, rows], reply_send.at[h, d], reply_recv.at[h, d], dom=where
        )

    def for_all(act):
        def one(d, carry):
            act(d)
            return carry

        lax.fori_loop(1, count, one, 0)

    halo = [
        remote(
            params_hbm.at[:, pl.ds((BLOCKS - 1) * BLOCK, BLOCK)],
            block_rows_of(pool, LOW),
            halo_send.at[0],
            halo_recv.at[0],
            region=upper,
        ),
        remote(
            params_hbm.at[:, pl.ds(0, BLOCK)],
            block_rows_of(pool, HIGH),
            halo_send.at[1],
            halo_recv.at[1],
            region=lower,
        ),
    ]
    for copy in halo:
        copy.start()
    for_all(lambda d: label(d).start())
    got_labels[0] = labels[0]

    for copy in own:
        copy.wait()
    for b in range(POOL, 2 * SUB):
        pool[b * ROWS : b * ROWS + PARAMS, :] = pool[0:PARAMS, :]
    tabulate(0, SUB, pool, stage, turned, table, spread)
    for copy in halo:
        copy.wait_recv()
    tabulate(1, POOL - SUB, pool, stage, turned, table, spread)
    lane = iota((BLOCK, COLS), 1)
    table[DEAD] = jnp.where(lane == 0, -1e30, 0.0).astype(bf16)
    spread[DEAD] = jnp.zeros((3, BLOCK, BLOCK), f32)

    for copy in scalars:
        copy.wait()
    for h in range(HALVES):
        forward_half(h, blocks, live, features, table, spread, prefix, segment, pieces)
        rendered = [pieces[r * PIECES : (r + 1) * PIECES, :] for r in range(PARTS)]
        rendered = jnp.concatenate(rendered, axis=1)
        put_slots(sent.at[h], exact_pick(pack, rendered))
        for_all(lambda d: payload(h, d).start())
        got[h, :MESSAGE] = sent[h, :MESSAGE]

    for copy in later:
        copy.wait()
    for_all(lambda d: label(d).wait())
    arrived = jnp.concatenate([got_labels[d] for d in range(32)], axis=0)
    arrived_col = jnp.concatenate([arrived[:, 0:1], arrived[:, 1:2]], axis=0)
    arrived_row = to_row(arrived_col)
    slots = SLOTS * 32

    def cell_of(place):
        return ((place % TILE_DEV) * MAXD + place // TILE_DEV).astype(f32)

    gather = jnp.broadcast_to(arrived_row, (CELLS, slots)) == cell_of(iota((CELLS, slots), 0))
    gather = jnp.where(gather, 1.0, 0.0)
    scatter = jnp.broadcast_to(arrived_col, (slots, CELLS)) == cell_of(iota((slots, CELLS), 1))
    scatter = jnp.where(scatter, 1.0, 0.0)
    colours = [background[c] for c in range(3)]
    for h in range(HALVES):
        for_all(lambda d: payload(h, d).wait())
        grid = exact_pick(gather, get_slots(got.at[h]))
        put_slots(replies.at[h], exact_pick(scatter, composite(h, grid, target, colours)))
        for_all(lambda d: reply(h, d).start())
        answers[h, :MESSAGE] = replies[h, :MESSAGE]

    for h in range(HALVES):
        for_all(lambda d: reply(h, d).wait())
        back = exact_pick(unpack, get_slots(answers.at[h]))
        for k in range(WIDE // BLOCK):
            for c in range(SUB):
                lanes = slice(c * WIDE + k * BLOCK, c * WIDE + (k + 1) * BLOCK)
                rows = back[:, lanes] if c < 4 else jnp.zeros((PIECES, BLOCK), f32)
                cotangent[pl.ds(k * PIECES * SUB + c, PIECES, stride=SUB), :] = rows
        backward_half(
            h, blocks, live, features, moments, table, prefix, segment, cotangent, moved
        )

    rows = own_block(block_rows[...]).astype(f32)
    gather_moments(rows[0:1], rows[1:2], moved, summed)
    pull_splat(1, pool, summed, grads_ref)
    edges = [
        remote(block_rows_of(grads_ref, HIGH), from_left, edge_send.at[0], edge_recv.at[0], region=upper),
        remote(block_rows_of(grads_ref, LOW), from_right, edge_send.at[1], edge_recv.at[1], region=lower),
    ]
    for copy in edges:
        copy.start()
    pull_splat(0, pool, summed, grads_ref)
    for copy in halo:
        copy.wait_send()
    for copy in edges:
        copy.wait()


def whole(memory=pltpu.VMEM):
    return pl.BlockSpec(memory_space=memory)


def step(*operands):
    shape = jax.ShapeDtypeStruct
    vmem, smem, dma = pltpu.VMEM, pltpu.SMEM, pltpu.SemaphoreType.DMA
    slots = vmem((HALVES, 32 * MESSAGE, BLOCK), f32)
    label = vmem((32, 1, BLOCK), f32)
    return pl.pallas_call(
        step_kernel,
        out_shape=(
            shape((2 * SUB * ROWS, BLOCK), f32),
            shape((PARAMS, BLOCK), f32),
            shape((PARAMS, BLOCK), f32),
        ),
        in_specs=[whole(pl.ANY)] * 9,
        out_specs=(whole(),) * 3,
        scratch_shapes=[
            smem((2, PIECES), jnp.int32),
            smem((1, PIECES), jnp.int32),
            smem((3,), f32),
            vmem((2, PIECES), jnp.int32),
            vmem((1, PIECES), jnp.int32),
            vmem((1, PIECES), jnp.int32),
            vmem((3, TILE_DEV, PIX), f32),
            vmem((PIECES, 32, PIX), bf16),
            vmem((PIECES, 16, PIX), bf16),
            vmem((2 * SUB * ROWS, BLOCK), f32),
            vmem((SUB * COLS, BLOCK), f32),
            vmem((BLOCK, BLOCK), f32),
            vmem((TAB, BLOCK, COLS), bf16),
            vmem((TAB, 3, BLOCK, BLOCK), f32),
            vmem((HALVES, PIECES, 2, SUB, WIDE), f32),
            vmem((HALVES, PIECES, 2, 3, SUB, WIDE), f32),
            vmem((4 * WIDE // BLOCK * PIECES, BLOCK), f32),
            slots,
            slots,
            slots,
            slots,
            label,
            label,
            vmem((WIDE // BLOCK * PIECES * SUB, BLOCK), f32),
            vmem((2 * PIECES * 32, BLOCK), f32),
            vmem((32, 2 * SUB, BLOCK), f32),
            dma((17,)),
            dma((2,)),
            dma((2,)),
            dma((2,)),
            dma((2,)),
            dma((32,)),
            dma((32,)),
            dma((HALVES, 32)),
            dma((HALVES, 32)),
            dma((HALVES, 32)),
            dma((HALVES, 32)),
        ],
        compiler_params=pltpu.CompilerParams(
            collective_id=0, has_side_effects=True, vmem_limit_bytes=VMEM_LIMIT
        ),
        name="render_step",
    )(*operands)


def adam_kernel(
    grads_ref, from_left_ref, from_right_ref, params_ref, first_ref, second_ref,
    gradient_ref, new_params_ref, new_first_ref, new_second_ref,
):
    for b in range(BLOCKS):
        cols = slice(b * BLOCK, (b + 1) * BLOCK)
        gradient = grads_ref[b * ROWS : b * ROWS + PARAMS, :]
        if b == 0:
            gradient = gradient + from_left_ref[...]
        if b == BLOCKS - 1:
            gradient = gradient + from_right_ref[...]
        new_first = beta_one * first_ref[:, cols] + (1 - beta_one) * gradient
        new_second = beta_two * second_ref[:, cols] + (1 - beta_two) * gradient * gradient
        update = (
            new_first
            / (1 - beta_one**adam_step)
            / (jnp.sqrt(new_second / (1 - beta_two**adam_step)) + tiny)
        )
        gradient_ref[:, cols] = gradient
        new_params_ref[:, cols] = params_ref[:, cols] - rate * update
        new_first_ref[:, cols] = new_first
        new_second_ref[:, cols] = new_second


def adam(*operands):
    return pl.pallas_call(
        adam_kernel,
        out_shape=(jax.ShapeDtypeStruct((PARAMS, BLOCKS * BLOCK), f32),) * 4,
        in_specs=[whole()] * 6,
        out_specs=(whole(),) * 4,
        compiler_params=pltpu.CompilerParams(vmem_limit_bytes=8 * 1024 * 1024),
        name="adam",
    )(*operands)


def on_device(
    params,
    first_moment,
    second_moment,
    piece_blocks,
    piece_live,
    piece_owner,
    piece_cell,
    target,
    background,
):
    grads, from_left, from_right = step(
        params,
        piece_blocks[0].T,
        piece_live,
        piece_owner,
        piece_cell,
        jnp.transpose(target[0], (1, 0, 2)),
        background,
        jnp.asarray(exponent_features()),
        jnp.asarray(moment_features()),
    )
    return adam(grads, from_left, from_right, params, first_moment, second_moment)


def solution(mesh):
    in_specs = (
        P(None, ("region", "dom")),
        P(None, ("region", "dom")),
        P(None, ("region", "dom")),
        P(("region", "dom"), None, None),
        P(("region", "dom"), None),
        P(("region", "dom"), None),
        P(("region", "dom"), None),
        P(("region", "dom"), None, None, None),
        P(),
    )
    out_specs = (
        P(None, ("region", "dom")),
        P(None, ("region", "dom")),
        P(None, ("region", "dom")),
        P(None, ("region", "dom")),
    )
    return jax.shard_map(
        on_device, mesh=mesh, in_specs=in_specs, out_specs=out_specs, check_vma=False
    )
```

```python
import functools
import math

import jax
import jax.numpy as jnp
import ml_dtypes
import numpy as np
from jax import lax
from jax.experimental import pallas as pl
from jax.experimental.pallas import tpu as pltpu
from jax.sharding import PartitionSpec as P

PARAMS = 59
TSIDE = 16
WIN = 8
BLOCK = 128
BLOCKS = 8
MAXD = 8
PIECES = 32
PIX = 256
TILE_DEV = 8
CELLS = 64
POOL = 10
SLOTS = 2
SUB = 8
STEPS = BLOCK // SUB
TAB = POOL + 1
PLANES = 16
ROWS = 64
COLS = 96
UNROLL = 8
START_UNROLL = 1
HALVES = 2
WIDE = PIX // HALVES
LOW = BLOCKS
HIGH = BLOCKS + 1
DEAD = POOL
FROM_LEFT = 2 * SUB
FROM_RIGHT = FROM_LEFT + 1
ORIGIN_X = 64.0
ORIGIN_Y = 32.0

harmonic_zero = 0.28209479177387814
harmonic_one = 0.4886025119029199
harmonic_two = (
    1.0925484305920792,
    -1.0925484305920792,
    0.31539156525252005,
    -1.0925484305920792,
    0.5462742152960396,
)
harmonic_three = (
    -0.5900435899266435,
    2.890611442640554,
    -0.4570457994644658,
    0.3731763325901154,
    -0.4570457994644658,
    1.445305721320277,
    -0.5900435899266435,
)
beta_one = 0.9
beta_two = 0.999
rate = 0.001
adam_step = 100
tiny = 1e-08

f32 = jnp.float32
bf16 = jnp.bfloat16
MESH = pl.DeviceIdType.MESH
VMEM_LIMIT = 60 * 1024 * 1024


def pixel_monomials():
    bf = ml_dtypes.bfloat16
    tile = np.arange(PIECES)[:, None]
    pixel = np.arange(PIX)[None, :]
    x = (TSIDE * (tile % WIN) + pixel % TSIDE + 0.5 - ORIGIN_X).astype(np.float32)
    y = (TSIDE * (tile // WIN) + pixel // TSIDE + 0.5 - ORIGIN_Y).astype(np.float32)

    def two(value):
        head = value.astype(bf).astype(np.float32)
        return [head, value - head]

    return [np.ones_like(x), x, y] + two(x * x) + two(x * y) + two(y * y)


def exponent_features():
    rows = [row for row in pixel_monomials() for _ in range(3)]
    rows += [np.zeros_like(rows[0])] * (32 - len(rows))
    return np.stack(rows, axis=1).astype(ml_dtypes.bfloat16)


def moment_features():
    rows = pixel_monomials()
    rows += [np.zeros_like(rows[0])] * (16 - len(rows))
    return np.stack(rows, axis=1).astype(ml_dtypes.bfloat16)


def split(value, parts):
    out = []
    rest = value
    for part in range(parts):
        head = rest.astype(bf16)
        out.append(head)
        if part < parts - 1:
            rest = rest - head.astype(f32)
    return out


def exact_pick(onehot, value):
    picks = onehot.astype(bf16)
    total = None
    for part in reversed(split(value, 3)):
        term = jnp.dot(picks, part, preferred_element_type=f32)
        total = term if total is None else total + term
    return total


def iota(shape, dim):
    return lax.broadcasted_iota(jnp.int32, shape, dim)


def to_column(row):
    n = row.shape[1]
    spread = jnp.broadcast_to(row, (n, n))
    return jnp.sum(jnp.where(iota((n, n), 0) == iota((n, n), 1), spread, 0.0), axis=1, keepdims=True)


def to_row(column):
    n = column.shape[0]
    spread = jnp.broadcast_to(column, (n, n))
    return jnp.sum(jnp.where(iota((n, n), 0) == iota((n, n), 1), spread, 0.0), axis=0, keepdims=True)


def geometry(mean_x, mean_y, mean_z, log_a, log_b, log_c, quat_w, quat_x, quat_y, quat_z):
    screen_px = float(WIN * TSIDE)
    scales = (jnp.exp(log_a), jnp.exp(log_b), jnp.exp(log_c))
    norm = 1.0 / jnp.sqrt(quat_w * quat_w + quat_x * quat_x + quat_y * quat_y + quat_z * quat_z)
    quat_w, quat_x, quat_y, quat_z = quat_w * norm, quat_x * norm, quat_y * norm, quat_z * norm
    rotation = [
        [
            1 - 2 * (quat_y * quat_y + quat_z * quat_z),
            2 * (quat_x * quat_y - quat_w * quat_z),
            2 * (quat_x * quat_z + quat_w * quat_y),
        ],
        [
            2 * (quat_x * quat_y + quat_w * quat_z),
            1 - 2 * (quat_x * quat_x + quat_z * quat_z),
            2 * (quat_y * quat_z - quat_w * quat_x),
        ],
        [
            2 * (quat_x * quat_z - quat_w * quat_y),
            2 * (quat_y * quat_z + quat_w * quat_x),
            1 - 2 * (quat_x * quat_x + quat_y * quat_y),
        ],
    ]
    focal_px = 0.3125 * screen_px
    inv_z = 1.0 / mean_z
    ratio_x, ratio_y = mean_x * inv_z, mean_y * inv_z
    focal_z = focal_px * inv_z
    rows = []
    for ratio, axis in ((ratio_x, 0), (ratio_y, 1)):
        rows.append(
            [
                focal_z * (rotation[axis][col] - ratio * rotation[2][col]) * scales[col]
                for col in range(3)
            ]
        )
    sigma_xx = rows[0][0] * rows[0][0] + rows[0][1] * rows[0][1] + rows[0][2] * rows[0][2] + 0.3
    sigma_xy = rows[0][0] * rows[1][0] + rows[0][1] * rows[1][1] + rows[0][2] * rows[1][2]
    sigma_yy = rows[1][0] * rows[1][0] + rows[1][1] * rows[1][1] + rows[1][2] * rows[1][2] + 0.3
    inv_det = 1.0 / (sigma_xx * sigma_yy - sigma_xy * sigma_xy)
    return (
        focal_px * ratio_x + (0.5 * screen_px - ORIGIN_X),
        focal_px * ratio_y + (0.5 * screen_px - ORIGIN_Y),
        sigma_yy * inv_det,
        -sigma_xy * inv_det,
        sigma_xx * inv_det,
    )


def harmonics(mean_x, mean_y, mean_z):
    inv_length = 1.0 / jnp.sqrt(mean_x * mean_x + mean_y * mean_y + mean_z * mean_z)
    dir_x, dir_y, dir_z = mean_x * inv_length, mean_y * inv_length, mean_z * inv_length
    sq_x, sq_y, sq_z = dir_x * dir_x, dir_y * dir_y, dir_z * dir_z
    return (
        -harmonic_one * dir_y,
        harmonic_one * dir_z,
        -harmonic_one * dir_x,
        harmonic_two[0] * dir_x * dir_y,
        harmonic_two[1] * dir_y * dir_z,
        harmonic_two[2] * (2 * sq_z - sq_x - sq_y),
        harmonic_two[3] * dir_x * dir_z,
        harmonic_two[4] * (sq_x - sq_y),
        harmonic_three[0] * dir_y * (3 * sq_x - sq_y),
        harmonic_three[1] * dir_x * dir_y * dir_z,
        harmonic_three[2] * dir_y * (4 * sq_z - sq_x - sq_y),
        harmonic_three[3] * dir_z * (2 * sq_z - 3 * sq_x - 3 * sq_y),
        harmonic_three[4] * dir_x * (4 * sq_z - sq_x - sq_y),
        harmonic_three[5] * dir_z * (sq_x - sq_y),
        harmonic_three[6] * dir_x * (sq_x - 3 * sq_y),
    )


def plane(ref, half, row):
    return ref[pl.ds(half * SUB * ROWS + row, SUB, stride=ROWS), :]


def put_plane(ref, half, row, value):
    ref[pl.ds(half * SUB * ROWS + row, SUB, stride=ROWS), :] = value


def raw_colour(pool, half, basis, colour):
    total = harmonic_zero * plane(pool, half, 11 + 16 * colour) + 0.5
    for k in range(1, 16):
        total = total + plane(pool, half, 11 + 16 * colour + k) * basis[k - 1]
    return total


def own_block(number):
    return jnp.where(number == 0, LOW, jnp.where(number == POOL - 1, HIGH, number - 1))


def roll_rows(value, shift):
    return pltpu.roll(value, shift % SUB, axis=0)


def tabulate(half, count, pool, stage, turned, table, spread):
    region = lax.axis_index("region")
    regions = lax.axis_size("region")
    means = [plane(pool, half, r) for r in range(3)]
    centre_u, centre_v, conic_xx, conic_xy, conic_yy = geometry(
        *means, *[plane(pool, half, r) for r in range(3, 10)]
    )
    opacity = 1.0 / (1.0 + jnp.exp(-plane(pool, half, 10)))
    log2_e = 1.0 / math.log(2.0)
    slope_x = conic_xx * centre_u + conic_xy * centre_v
    slope_y = conic_xy * centre_u + conic_yy * centre_v
    constant = jnp.log(opacity) - 0.5 * (centre_u * slope_x + centre_v * slope_y)
    constant = log2_e * constant
    if half:
        row = iota((SUB, BLOCK), 0)
        absent = ((row == LOW - SUB) & (region == 0)) | ((row == HIGH - SUB) & (region == regions - 1))
        constant = jnp.where(absent, -1e30, constant)
    terms = [
        constant,
        log2_e * slope_x,
        log2_e * slope_y,
        (-0.5 * log2_e) * conic_xx,
        (-log2_e) * conic_xy,
        (-0.5 * log2_e) * conic_yy,
    ]
    stage[...] = jnp.zeros_like(stage)

    def put(row, value):
        stage[pl.ds(row, SUB, stride=COLS), :] = value

    row = 0
    for term, copies in zip(terms, (1, 1, 1, 2, 2, 2)):
        parts = [part.astype(f32) for part in split(term, 3)]
        for _ in range(copies):
            for part in parts:
                put(row, part)
                row += 1
    basis = harmonics(*means)
    for c in range(3):
        tone = jnp.maximum(raw_colour(pool, half, basis, c), 0.0)
        parts = [part.astype(f32) for part in split(tone, 3)]
        for group, part in enumerate((0, 0, 0, 1, 1, 2)):
            put(32 + group * SUB + c, parts[part])
        put(80 + c, tone)

    def turn(b, carry):
        turned[:, :COLS] = stage[pl.ds(pl.multiple_of(b * COLS, COLS), COLS), :].T
        ordered = jnp.concatenate(
            [turned[pl.ds(t, SUB, stride=STEPS), :] for t in range(STEPS)], axis=0
        )
        table[half * SUB + b] = ordered[:, :COLS].astype(bf16)
        for c in range(3):
            spread[half * SUB + b, c] = jnp.broadcast_to(ordered[:, 80 + c : 81 + c], (BLOCK, BLOCK))
        return carry

    lax.fori_loop(0, count, turn, 0, unroll=2)


def exponents(table, features, block):
    return jnp.dot(table[block, :, :32], features, preferred_element_type=f32)


def two_blocks(p, blocks, live):
    first = own_block(blocks[0, p])
    second = jnp.where(live[0, p] > 1, own_block(blocks[1, p]), DEAD)
    return first, second


def forward_half(h, blocks, live, features_ref, table, spread, prefix_ref, segment_ref, pieces):
    sub = iota((SUB, WIDE), 0)

    def piece(p, carry):
        features = features_ref[p, :, h * WIDE : (h + 1) * WIDE]
        before = None
        colours = [None] * 3
        for j, block in enumerate(two_blocks(p, blocks, live)):
            exponent = exponents(table, features, block)
            transmit = jnp.ones((SUB, WIDE), f32)
            sums = [jnp.zeros((SUB, WIDE), f32) for _ in range(3)]
            for t in range(STEPS):
                rows = slice(t * SUB, (t + 1) * SUB)
                weight = jnp.exp2(exponent[rows]) * transmit
                transmit = transmit - weight
                for c in range(3):
                    tone = spread[block, c, rows, :]
                    tone = tone if WIDE == BLOCK else jnp.concatenate([tone, tone], axis=1)
                    sums[c] = sums[c] + tone * weight
            run = transmit
            for shift in (1, 2, 4):
                run = run * jnp.where(sub >= shift, roll_rows(run, shift), 1.0)
            prefix = jnp.where(sub >= 1, roll_rows(run, 1), 1.0)
            total = run[SUB - 1 :, :]
            if before is not None:
                prefix = prefix * before
                total = total * before
            before = total
            prefix_ref[h, p, j] = prefix
            for c in range(3):
                piece_sum = prefix * sums[c]
                segment_ref[h, p, j, c] = piece_sum
                colours[c] = piece_sum if j == 0 else colours[c] + piece_sum
        rows = [jnp.sum(colours[c], axis=0, keepdims=True) for c in range(3)] + [1.0 - before]
        for c in range(4):
            for k in range(WIDE // BLOCK):
                place = (c * (WIDE // BLOCK) + k) * PIECES + p
                pieces[pl.ds(place, 1), :] = rows[c][:, k * BLOCK : (k + 1) * BLOCK]
        return carry

    lax.fori_loop(0, PIECES, piece, 0, unroll=UNROLL)


def backward_half(
    h, blocks, live, features_ref, moments_ref, table, prefix_ref, segment_ref, cotangent, moved
):
    sub = iota((SUB, WIDE), 0)
    nothing = jnp.zeros((16, WIDE), bf16)
    none = jnp.zeros((16, WIDE), f32)
    lanes = slice(h * WIDE, (h + 1) * WIDE)

    def piece(p, carry):
        features = features_ref[p, :, lanes]
        monomials = moments_ref[p, :, lanes]
        cot = jnp.concatenate(
            [
                cotangent[pl.ds(pl.multiple_of((k * PIECES + p) * SUB, SUB), SUB), :]
                for k in range(WIDE // BLOCK)
            ],
            axis=1,
        )
        heads = [part.astype(f32) for part in split(cot, 3)]
        tones = [none, none] + [heads[part] for part in (0, 1, 2, 0, 1, 0)] + [none]
        tones = jnp.concatenate(tones, axis=0).astype(bf16)
        colour_rows = jnp.concatenate([heads[0], heads[1]], axis=0).astype(bf16)
        for_gradient = jnp.concatenate([monomials, nothing], axis=0)
        for_weight = jnp.concatenate([nothing, colour_rows], axis=0)
        state = []
        for j, block in enumerate(two_blocks(p, blocks, live)):
            exponent = exponents(table, features, block)
            tone = jnp.dot(table[block], tones, preferred_element_type=f32)
            transmit = prefix_ref[h, p, j]
            alphas, weights = [], []
            for t in range(STEPS):
                alpha = jnp.exp2(exponent[t * SUB : (t + 1) * SUB])
                weight = alpha * transmit
                transmit = transmit - weight
                alphas.append(alpha)
                weights.append(weight)
            seen = segment_ref[h, p, j, 0] * cot[0:1]
            for c in (1, 2):
                seen = seen + segment_ref[h, p, j, c] * cot[c : c + 1]
            run = seen
            for shift in (1, 2, 4):
                run = run + jnp.where(sub < SUB - shift, roll_rows(run, -shift), 0.0)
            state.append((tone, transmit, alphas, weights, run))
        behind = state[1][1][SUB - 1 :, :] * cot[3:4]
        parts = [None, None]
        for j in (1, 0):
            tone, transmit, alphas, weights, run = state[j]
            after = jnp.where(sub < SUB - 1, roll_rows(run, -1), 0.0) + behind
            behind = behind + run[0:1]
            ahead = after / transmit
            gradients = [None] * STEPS
            for t in reversed(range(STEPS)):
                gap = tone[t * SUB : (t + 1) * SUB] - ahead
                gradients[t] = weights[t] * gap
                ahead = ahead + alphas[t] * gap
            parts[j] = split(jnp.concatenate(gradients, axis=0), 2)
            parts[j] += split(jnp.concatenate(weights, axis=0), 2)
        both = [jnp.concatenate([parts[0][k], parts[1][k]], axis=0) for k in range(4)]
        total = None
        for k in range(2):
            rows = (for_gradient, for_weight)[k]
            term = lax.dot_general(
                jnp.concatenate([rows, rows], axis=1),
                jnp.concatenate(both[2 * k : 2 * k + 2], axis=1),
                (((1,), (1,)), ((), ())),
                preferred_element_type=f32,
            )
            total = term if total is None else total + term
        for j in range(2):
            rows = pl.ds(pl.multiple_of((j * PIECES + p) * 32, 32), 32)
            part = total[:, j * BLOCK : (j + 1) * BLOCK]
            moved[rows, :] = part if h == 0 else moved[rows, :] + part
        return carry

    lax.fori_loop(0, PIECES, piece, 0, unroll=UNROLL)


def gather_moments(first_row, second_row, moved, summed):
    numbers = iota((2 * SUB, PIECES), 0).astype(f32)
    lane = iota((BLOCK, BLOCK), 0)
    unshuffle = (lane % SUB) * STEPS + lane // SUB == iota((BLOCK, BLOCK), 1)
    unshuffle = jnp.where(unshuffle, 1.0, 0.0).astype(bf16)
    for group in range(3):
        features = range(group * SUB, group * SUB + SUB)
        features = [f for f in features if f < 9] + [16 + f - 9 for f in features if 9 <= f < 12]
        features += [24 + f - 12 for f in range(group * SUB, group * SUB + SUB) if 12 <= f < 15]
        if not features:
            continue
        total = None
        for j, row in enumerate((first_row, second_row)):
            pick = jnp.where(jnp.broadcast_to(row, (2 * SUB, PIECES)) == numbers, 1.0, 0.0)
            values = [
                moved[pl.ds(j * PIECES * 32 + f, PIECES, stride=32), :] for f in features
            ]
            term = exact_pick(pick, jnp.concatenate(values, axis=1))
            total = term if total is None else total + term
        stacked = jnp.concatenate(
            [total[:, k * BLOCK : (k + 1) * BLOCK] for k in range(len(features))], axis=0
        )
        ordered = None
        for part in reversed(split(stacked, 3)):
            term = jnp.dot(part, unshuffle, preferred_element_type=f32)
            ordered = term if ordered is None else ordered + term
        for k, f in enumerate(features):
            summed[f] = ordered[k * 2 * SUB : (k + 1) * 2 * SUB]


def pull_splat(half, pool, summed, grads_ref):
    means = [plane(pool, half, r) for r in range(3)]
    (centre_u, centre_v, conic_xx, conic_xy, conic_yy), geometry_pull = jax.vjp(
        geometry, *means, *[plane(pool, half, r) for r in range(3, 10)]
    )
    basis, harmonics_pull = jax.vjp(harmonics, *means)
    opacity = 1.0 / (1.0 + jnp.exp(-plane(pool, half, 10)))
    sums = [summed[f, half * SUB : (half + 1) * SUB] for f in range(9)]
    total, sum_x, sum_y = sums[:3]
    sum_xx, sum_xy, sum_yy = sums[3] + sums[4], sums[5] + sums[6], sums[7] + sums[8]
    off_x = sum_x - centre_u * total
    off_y = sum_y - centre_v * total
    grad_xx = -0.5 * (sum_xx - centre_u * (sum_x + off_x))
    grad_xy = -(sum_xy - centre_u * sum_y - centre_v * off_x)
    grad_yy = -0.5 * (sum_yy - centre_v * (sum_y + off_y))
    grad_u = conic_xx * off_x + conic_xy * off_y
    grad_v = conic_xy * off_x + conic_yy * off_y
    grads = geometry_pull((grad_u, grad_v, grad_xx, grad_xy, grad_yy))
    tone_grads = []
    for c in range(3):
        grad = summed[16 + c, half * SUB : (half + 1) * SUB] + summed[24 + c, half * SUB : (half + 1) * SUB]
        raw = raw_colour(pool, half, basis, c)
        tone_grads.append(jnp.where(raw > 0, grad, jnp.where(raw == 0, 0.5 * grad, 0.0)))
    basis_grads = []
    for k in range(1, 16):
        basis_grads.append(
            sum(tone_grads[c] * plane(pool, half, 11 + 16 * c + k) for c in range(3))
        )
    mean_grads = harmonics_pull(tuple(basis_grads))
    for r in range(10):
        put_plane(grads_ref, half, r, grads[r] + mean_grads[r] if r < 3 else grads[r])
    put_plane(grads_ref, half, 10, total * (1.0 - opacity))
    for c in range(3):
        put_plane(grads_ref, half, 11 + 16 * c, tone_grads[c] * harmonic_zero)
        for k in range(1, 16):
            put_plane(grads_ref, half, 11 + 16 * c + k, tone_grads[c] * basis[k - 1])


PARTS = 4 * WIDE // BLOCK
MESSAGE = SLOTS * PARTS


def put_slots(ref, values):
    for k in range(SLOTS):
        for r in range(PARTS):
            ref[pl.ds(k * PARTS + r, 32, stride=MESSAGE), :] = values[
                k * 32 : (k + 1) * 32, r * BLOCK : (r + 1) * BLOCK
            ]


def get_slots(ref):
    return jnp.concatenate(
        [
            jnp.concatenate(
                [ref[pl.ds(k * PARTS + r, 32, stride=MESSAGE), :] for r in range(PARTS)], axis=1
            )
            for k in range(SLOTS)
        ],
        axis=0,
    )


def route(owner_row, cell_row, me):
    owner_col = to_column(owner_row)
    far_row = owner_row - me.astype(f32)
    far_row = jnp.where(far_row < 0, far_row + float(PIECES), far_row)
    far_col = to_column(far_row)
    square = (PIECES, PIECES)
    same = jnp.broadcast_to(owner_row, square) == jnp.broadcast_to(owner_col, square)
    first, second = iota(square, 0), iota(square, 1)
    rank_row = jnp.sum(jnp.where(same & (first < second), 1.0, 0.0), axis=0, keepdims=True)
    rank_col = jnp.sum(jnp.where(same & (second < first), 1.0, 0.0), axis=1, keepdims=True)
    slots = SLOTS * 32
    pack = jnp.broadcast_to(rank_row * 32.0 + far_row, (slots, PIECES)) == iota((slots, PIECES), 0).astype(f32)
    pack = jnp.where(pack, 1.0, 0.0)
    unpack = jnp.broadcast_to(rank_col * 32.0 + far_col, (PIECES, slots)) == iota((PIECES, slots), 1).astype(f32)
    unpack = jnp.where(unpack, 1.0, 0.0)
    label_col = jnp.sum(pack * (cell_row + 1.0), axis=1, keepdims=True) - 1.0
    lane = iota((32, BLOCK), 1)
    label_rows = jnp.where(lane == 0, label_col[:32], jnp.where(lane == 1, label_col[32:], -1.0))
    return pack, unpack, label_rows


def composite(h, grid, target, background):
    def at(depth, channel):
        return grid[depth * SUB : (depth + 1) * SUB, channel * WIDE : (channel + 1) * WIDE]

    in_front = jnp.ones((TILE_DEV, WIDE), f32)
    seen = [jnp.zeros((TILE_DEV, WIDE), f32) for _ in range(3)]
    fronts = []
    for depth in range(MAXD):
        fronts.append(in_front)
        seen = [seen[c] + in_front * at(depth, c) for c in range(3)]
        in_front = in_front * (1.0 - at(depth, 3))
    residual = [
        seen[c] + in_front * background[c] - target[c, :, h * WIDE : (h + 1) * WIDE] for c in range(3)
    ]
    behind = [jnp.full((TILE_DEV, WIDE), background[c], f32) for c in range(3)]
    rows = [None] * MAXD
    for depth in reversed(range(MAXD)):
        through = 1.0 - at(depth, 3)
        by_trans = residual[0] * behind[0] + residual[1] * behind[1] + residual[2] * behind[2]
        rows[depth] = jnp.concatenate(
            [fronts[depth] * residual[c] for c in range(3)] + [fronts[depth] * by_trans], axis=1
        )
        behind = [at(depth, c) + through * behind[c] for c in range(3)]
    return jnp.concatenate(rows, axis=0)


def step_kernel(
    params_hbm,
    blocks_hbm,
    live_hbm,
    owner_hbm,
    cell_hbm,
    target_hbm,
    background_hbm,
    features_hbm,
    moments_hbm,
    grads_ref,
    blocks,
    live,
    background,
    block_rows,
    owner,
    cell,
    target,
    features,
    moments,
    pool,
    stage,
    turned,
    table,
    spread,
    prefix,
    segment,
    pieces,
    sent,
    got,
    replies,
    answers,
    labels,
    got_labels,
    cotangent,
    moved,
    summed,
    local_sem,
    halo_send,
    halo_recv,
    edge_send,
    edge_recv,
    label_send,
    label_recv,
    send_sem,
    recv_sem,
    reply_send,
    reply_recv,
):
    regions, region = lax.axis_size("region"), lax.axis_index("region")
    count, me = lax.axis_size("dom"), lax.axis_index("dom")
    upper, lower = lax.rem(region + 1, regions), lax.rem(region + regions - 1, regions)

    def block_rows_of(ref, b):
        return ref.at[pl.ds(b * ROWS, PARAMS)]

    fetches = []

    def fetch(src, dst):
        copy = pltpu.make_async_copy(src, dst, local_sem.at[len(fetches)])
        copy.start()
        fetches.append(copy)
        return copy

    routing = [fetch(owner_hbm, owner), fetch(cell_hbm, cell)]
    own = [
        fetch(params_hbm.at[:, pl.ds(b * BLOCK, BLOCK)], block_rows_of(pool, b)) for b in range(BLOCKS)
    ]
    scalars = [fetch(blocks_hbm, blocks), fetch(live_hbm, live), fetch(features_hbm, features)]
    later = [
        fetch(blocks_hbm, block_rows),
        fetch(target_hbm, target),
        fetch(background_hbm, background),
        fetch(moments_hbm, moments),
    ]

    barrier = pltpu.get_barrier_semaphore()

    def signal(**where):
        pl.semaphore_signal(barrier, inc=1, device_id=where, device_id_type=MESH)

    def greet(d, carry):
        signal(dom=lax.rem(me + d, count))
        return carry

    signal(region=upper)
    signal(region=lower)
    lax.fori_loop(1, count, greet, 0)

    for copy in routing:
        copy.wait()
    pack, unpack, label_rows = route(owner[...].astype(f32), cell[...].astype(f32), me)
    for d in range(32):
        labels[d] = label_rows[d : d + 1]
    pl.semaphore_wait(barrier, count + 1)

    def remote(src, dst, send, recv, **where):
        return pltpu.make_async_remote_copy(
            src_ref=src, dst_ref=dst, send_sem=send, recv_sem=recv, device_id=where, device_id_type=MESH
        )

    def label(d, many=1):
        rows = pl.ds(d, many)
        return remote(
            labels.at[rows], got_labels.at[rows], label_send, label_recv, dom=lax.rem(me + d, count)
        )

    def message(d, many):
        return pl.ds(pl.multiple_of(d * MESSAGE, MESSAGE), many * MESSAGE)

    def payload(h, d, many=1):
        rows = message(d, many)
        return remote(
            sent.at[h, rows], got.at[h, rows], send_sem.at[h], recv_sem.at[h], dom=lax.rem(me + d, count)
        )

    def reply(h, d, many=1):
        rows = message(d, many)
        return remote(
            replies.at[h, rows],
            answers.at[h, rows],
            reply_send.at[h],
            reply_recv.at[h],
            dom=lax.rem(me + count - d, count),
        )

    def start_all(copy):
        def one(d, carry):
            copy(d).start()
            return carry

        lax.fori_loop(1, count, one, 0, unroll=START_UNROLL)

    others = count - 1

    halo = [
        remote(
            params_hbm.at[:, pl.ds((BLOCKS - 1) * BLOCK, BLOCK)],
            block_rows_of(pool, LOW),
            halo_send.at[0],
            halo_recv.at[0],
            region=upper,
        ),
        remote(
            params_hbm.at[:, pl.ds(0, BLOCK)],
            block_rows_of(pool, HIGH),
            halo_send.at[1],
            halo_recv.at[1],
            region=lower,
        ),
    ]
    for copy in halo:
        copy.start()
    start_all(label)
    got_labels[0] = labels[0]

    for copy in own:
        copy.wait()
    for b in range(POOL, 2 * SUB):
        pool[b * ROWS : b * ROWS + PARAMS, :] = pool[0:PARAMS, :]
    tabulate(0, SUB, pool, stage, turned, table, spread)
    for copy in halo:
        copy.wait_recv()
    tabulate(1, POOL - SUB, pool, stage, turned, table, spread)
    lane = iota((BLOCK, COLS), 1)
    table[DEAD] = jnp.where(lane == 0, -1e30, 0.0).astype(bf16)
    spread[DEAD] = jnp.zeros((3, BLOCK, BLOCK), f32)

    for copy in scalars:
        copy.wait()
    for h in range(HALVES):
        forward_half(h, blocks, live, features, table, spread, prefix, segment, pieces)
        rendered = [pieces[r * PIECES : (r + 1) * PIECES, :] for r in range(PARTS)]
        rendered = jnp.concatenate(rendered, axis=1)
        put_slots(sent.at[h], exact_pick(pack, rendered))
        start_all(functools.partial(payload, h))
        got[h, :MESSAGE] = sent[h, :MESSAGE]

    for copy in later:
        copy.wait()
    label(1, others).wait()
    arrived = jnp.concatenate([got_labels[d] for d in range(32)], axis=0)
    arrived_col = jnp.concatenate([arrived[:, 0:1], arrived[:, 1:2]], axis=0)
    arrived_row = to_row(arrived_col)
    slots = SLOTS * 32

    def cell_of(place):
        return ((place % TILE_DEV) * MAXD + place // TILE_DEV).astype(f32)

    gather = jnp.broadcast_to(arrived_row, (CELLS, slots)) == cell_of(iota((CELLS, slots), 0))
    gather = jnp.where(gather, 1.0, 0.0)
    scatter = jnp.broadcast_to(arrived_col, (slots, CELLS)) == cell_of(iota((slots, CELLS), 1))
    scatter = jnp.where(scatter, 1.0, 0.0)
    colours = [background[c] for c in range(3)]
    for h in range(HALVES):
        payload(h, 1, others).wait()
        grid = exact_pick(gather, get_slots(got.at[h]))
        put_slots(replies.at[h], exact_pick(scatter, composite(h, grid, target, colours)))
        start_all(functools.partial(reply, h))
        answers[h, :MESSAGE] = replies[h, :MESSAGE]

    for h in range(HALVES):
        reply(h, 1, others).wait()
        back = exact_pick(unpack, get_slots(answers.at[h]))
        for k in range(WIDE // BLOCK):
            for c in range(SUB):
                lanes = slice(c * WIDE + k * BLOCK, c * WIDE + (k + 1) * BLOCK)
                rows = back[:, lanes] if c < 4 else jnp.zeros((PIECES, BLOCK), f32)
                cotangent[pl.ds(k * PIECES * SUB + c, PIECES, stride=SUB), :] = rows
        backward_half(
            h, blocks, live, features, moments, table, prefix, segment, cotangent, moved
        )

    rows = own_block(block_rows[...]).astype(f32)
    gather_moments(rows[0:1], rows[1:2], moved, summed)
    pull_splat(1, pool, summed, grads_ref)
    edges = [
        remote(block_rows_of(grads_ref, HIGH), block_rows_of(grads_ref, FROM_LEFT), edge_send.at[0], edge_recv.at[0], region=upper),
        remote(block_rows_of(grads_ref, LOW), block_rows_of(grads_ref, FROM_RIGHT), edge_send.at[1], edge_recv.at[1], region=lower),
    ]
    for copy in edges:
        copy.start()
    pull_splat(0, pool, summed, grads_ref)
    for copy in halo:
        copy.wait_send()
    for copy in edges:
        copy.wait()


def whole(memory=pltpu.VMEM):
    return pl.BlockSpec(memory_space=memory)


def step(*operands):
    shape = jax.ShapeDtypeStruct
    vmem, smem, dma = pltpu.VMEM, pltpu.SMEM, pltpu.SemaphoreType.DMA
    slots = vmem((HALVES, 32 * MESSAGE, BLOCK), f32)
    label = vmem((32, 1, BLOCK), f32)
    return pl.pallas_call(
        step_kernel,
        out_shape=shape(((FROM_RIGHT + 1) * ROWS, BLOCK), f32),
        in_specs=[whole(pltpu.HBM)] * 9,
        out_specs=whole(),
        scratch_shapes=[
            smem((2, PIECES), jnp.int32),
            smem((1, PIECES), jnp.int32),
            smem((3,), f32),
            vmem((2, PIECES), jnp.int32),
            vmem((1, PIECES), jnp.int32),
            vmem((1, PIECES), jnp.int32),
            vmem((3, TILE_DEV, PIX), f32),
            vmem((PIECES, 32, PIX), bf16),
            vmem((PIECES, 16, PIX), bf16),
            vmem((2 * SUB * ROWS, BLOCK), f32),
            vmem((SUB * COLS, BLOCK), f32),
            vmem((BLOCK, BLOCK), f32),
            vmem((TAB, BLOCK, COLS), bf16),
            vmem((TAB, 3, BLOCK, BLOCK), f32),
            vmem((HALVES, PIECES, 2, SUB, WIDE), f32),
            vmem((HALVES, PIECES, 2, 3, SUB, WIDE), f32),
            vmem((4 * WIDE // BLOCK * PIECES, BLOCK), f32),
            slots,
            slots,
            slots,
            slots,
            label,
            label,
            vmem((WIDE // BLOCK * PIECES * SUB, BLOCK), f32),
            vmem((2 * PIECES * 32, BLOCK), f32),
            vmem((32, 2 * SUB, BLOCK), f32),
            dma((17,)),
            dma((2,)),
            dma((2,)),
            dma((2,)),
            dma((2,)),
            dma,
            dma,
            dma((HALVES,)),
            dma((HALVES,)),
            dma((HALVES,)),
            dma((HALVES,)),
        ],
        compiler_params=pltpu.CompilerParams(
            collective_id=0, has_side_effects=True, vmem_limit_bytes=VMEM_LIMIT
        ),
        name="render_step",
    )(*operands)


def adam_kernel(
    grads_ref, params_ref, first_ref, second_ref,
    gradient_ref, new_params_ref, new_first_ref, new_second_ref,
):
    for b in range(BLOCKS):
        cols = slice(b * BLOCK, (b + 1) * BLOCK)
        gradient = grads_ref[b * ROWS : b * ROWS + PARAMS, :]
        if b == 0:
            gradient = gradient + grads_ref[FROM_LEFT * ROWS : FROM_LEFT * ROWS + PARAMS, :]
        if b == BLOCKS - 1:
            gradient = gradient + grads_ref[FROM_RIGHT * ROWS : FROM_RIGHT * ROWS + PARAMS, :]
        new_first = beta_one * first_ref[:, cols] + (1 - beta_one) * gradient
        new_second = beta_two * second_ref[:, cols] + (1 - beta_two) * gradient * gradient
        update = (
            new_first
            / (1 - beta_one**adam_step)
            / (jnp.sqrt(new_second / (1 - beta_two**adam_step)) + tiny)
        )
        gradient_ref[:, cols] = gradient
        new_params_ref[:, cols] = params_ref[:, cols] - rate * update
        new_first_ref[:, cols] = new_first
        new_second_ref[:, cols] = new_second


def adam(*operands):
    return pl.pallas_call(
        adam_kernel,
        out_shape=(jax.ShapeDtypeStruct((PARAMS, BLOCKS * BLOCK), f32),) * 4,
        in_specs=[whole()] * 4,
        out_specs=(whole(),) * 4,
        compiler_params=pltpu.CompilerParams(vmem_limit_bytes=8 * 1024 * 1024),
        name="adam",
    )(*operands)


def on_device(
    params,
    first_moment,
    second_moment,
    piece_blocks,
    piece_live,
    piece_owner,
    piece_cell,
    target,
    background,
):
    grads = step(
        params,
        piece_blocks[0].T,
        piece_live,
        piece_owner,
        piece_cell,
        jnp.transpose(target[0], (1, 0, 2)),
        background,
        jnp.asarray(exponent_features()),
        jnp.asarray(moment_features()),
    )
    return adam(grads, params, first_moment, second_moment)


def solution(mesh):
    in_specs = (
        P(None, ("region", "dom")),
        P(None, ("region", "dom")),
        P(None, ("region", "dom")),
        P(("region", "dom"), None, None),
        P(("region", "dom"), None),
        P(("region", "dom"), None),
        P(("region", "dom"), None),
        P(("region", "dom"), None, None, None),
        P(),
    )
    out_specs = (
        P(None, ("region", "dom")),
        P(None, ("region", "dom")),
        P(None, ("region", "dom")),
        P(None, ("region", "dom")),
    )
    return jax.shard_map(
        on_device, mesh=mesh, in_specs=in_specs, out_specs=out_specs, check_vma=False
    )
```

```python
import functools
import math

import jax
import jax.numpy as jnp
import ml_dtypes
import numpy as np
from jax import lax
from jax.experimental import pallas as pl
from jax.experimental.pallas import tpu as pltpu
from jax.sharding import PartitionSpec as P

PARAMS = 59
TSIDE = 16
WIN = 8
BLOCK = 128
BLOCKS = 8
MAXD = 8
PIECES = 32
PIX = 256
TILE_DEV = 8
CELLS = 64
POOL = 10
SLOTS = 2
SUB = 8
STEPS = BLOCK // SUB
TAB = POOL + 1
PLANES = 16
ROWS = 64
COLS = 96
UNROLL = 8
MIDDLE_UNROLL = 4
START_UNROLL = 1
HALVES = 2
WIDE = PIX // HALVES
LOW = BLOCKS
HIGH = BLOCKS + 1
DEAD = POOL
FROM_LEFT = 2 * SUB
FROM_RIGHT = FROM_LEFT + 1
ORIGIN_X = 64.0
ORIGIN_Y = 32.0

harmonic_zero = 0.28209479177387814
harmonic_one = 0.4886025119029199
harmonic_two = (
    1.0925484305920792,
    -1.0925484305920792,
    0.31539156525252005,
    -1.0925484305920792,
    0.5462742152960396,
)
harmonic_three = (
    -0.5900435899266435,
    2.890611442640554,
    -0.4570457994644658,
    0.3731763325901154,
    -0.4570457994644658,
    1.445305721320277,
    -0.5900435899266435,
)
beta_one = 0.9
beta_two = 0.999
rate = 0.001
adam_step = 100
tiny = 1e-08

f32 = jnp.float32
bf16 = jnp.bfloat16
MESH = pl.DeviceIdType.MESH
VMEM_LIMIT = 60 * 1024 * 1024


def pixel_monomials():
    bf = ml_dtypes.bfloat16
    tile = np.arange(PIECES)[:, None]
    pixel = np.arange(PIX)[None, :]
    x = (TSIDE * (tile % WIN) + pixel % TSIDE + 0.5 - ORIGIN_X).astype(np.float32)
    y = (TSIDE * (tile // WIN) + pixel // TSIDE + 0.5 - ORIGIN_Y).astype(np.float32)

    def two(value):
        head = value.astype(bf).astype(np.float32)
        return [head, value - head]

    return [np.ones_like(x), x, y] + two(x * x) + two(x * y) + two(y * y)


def exponent_features():
    rows = [row for row in pixel_monomials() for _ in range(3)]
    rows += [np.zeros_like(rows[0])] * (32 - len(rows))
    return np.stack(rows, axis=1).astype(ml_dtypes.bfloat16)


def moment_features():
    rows = pixel_monomials()
    rows += [np.zeros_like(rows[0])] * (16 - len(rows))
    return np.stack(rows, axis=1).astype(ml_dtypes.bfloat16)


def split(value, parts):
    out = []
    rest = value
    for part in range(parts):
        head = rest.astype(bf16)
        out.append(head)
        if part < parts - 1:
            rest = rest - head.astype(f32)
    return out


def exact_pick(onehot, value):
    picks = onehot.astype(bf16)
    total = None
    for part in reversed(split(value, 3)):
        term = jnp.dot(picks, part, preferred_element_type=f32)
        total = term if total is None else total + term
    return total


def iota(shape, dim):
    return lax.broadcasted_iota(jnp.int32, shape, dim)


def to_column(row):
    n = row.shape[1]
    spread = jnp.broadcast_to(row, (n, n))
    return jnp.sum(jnp.where(iota((n, n), 0) == iota((n, n), 1), spread, 0.0), axis=1, keepdims=True)


def to_row(column):
    n = column.shape[0]
    spread = jnp.broadcast_to(column, (n, n))
    return jnp.sum(jnp.where(iota((n, n), 0) == iota((n, n), 1), spread, 0.0), axis=0, keepdims=True)


def geometry(mean_x, mean_y, mean_z, log_a, log_b, log_c, quat_w, quat_x, quat_y, quat_z):
    screen_px = float(WIN * TSIDE)
    scales = (jnp.exp(log_a), jnp.exp(log_b), jnp.exp(log_c))
    norm = 1.0 / jnp.sqrt(quat_w * quat_w + quat_x * quat_x + quat_y * quat_y + quat_z * quat_z)
    quat_w, quat_x, quat_y, quat_z = quat_w * norm, quat_x * norm, quat_y * norm, quat_z * norm
    rotation = [
        [
            1 - 2 * (quat_y * quat_y + quat_z * quat_z),
            2 * (quat_x * quat_y - quat_w * quat_z),
            2 * (quat_x * quat_z + quat_w * quat_y),
        ],
        [
            2 * (quat_x * quat_y + quat_w * quat_z),
            1 - 2 * (quat_x * quat_x + quat_z * quat_z),
            2 * (quat_y * quat_z - quat_w * quat_x),
        ],
        [
            2 * (quat_x * quat_z - quat_w * quat_y),
            2 * (quat_y * quat_z + quat_w * quat_x),
            1 - 2 * (quat_x * quat_x + quat_y * quat_y),
        ],
    ]
    focal_px = 0.3125 * screen_px
    inv_z = 1.0 / mean_z
    ratio_x, ratio_y = mean_x * inv_z, mean_y * inv_z
    focal_z = focal_px * inv_z
    rows = []
    for ratio, axis in ((ratio_x, 0), (ratio_y, 1)):
        rows.append(
            [
                focal_z * (rotation[axis][col] - ratio * rotation[2][col]) * scales[col]
                for col in range(3)
            ]
        )
    sigma_xx = rows[0][0] * rows[0][0] + rows[0][1] * rows[0][1] + rows[0][2] * rows[0][2] + 0.3
    sigma_xy = rows[0][0] * rows[1][0] + rows[0][1] * rows[1][1] + rows[0][2] * rows[1][2]
    sigma_yy = rows[1][0] * rows[1][0] + rows[1][1] * rows[1][1] + rows[1][2] * rows[1][2] + 0.3
    inv_det = 1.0 / (sigma_xx * sigma_yy - sigma_xy * sigma_xy)
    return (
        focal_px * ratio_x + (0.5 * screen_px - ORIGIN_X),
        focal_px * ratio_y + (0.5 * screen_px - ORIGIN_Y),
        sigma_yy * inv_det,
        -sigma_xy * inv_det,
        sigma_xx * inv_det,
    )


def harmonics(mean_x, mean_y, mean_z):
    inv_length = 1.0 / jnp.sqrt(mean_x * mean_x + mean_y * mean_y + mean_z * mean_z)
    dir_x, dir_y, dir_z = mean_x * inv_length, mean_y * inv_length, mean_z * inv_length
    sq_x, sq_y, sq_z = dir_x * dir_x, dir_y * dir_y, dir_z * dir_z
    return (
        -harmonic_one * dir_y,
        harmonic_one * dir_z,
        -harmonic_one * dir_x,
        harmonic_two[0] * dir_x * dir_y,
        harmonic_two[1] * dir_y * dir_z,
        harmonic_two[2] * (2 * sq_z - sq_x - sq_y),
        harmonic_two[3] * dir_x * dir_z,
        harmonic_two[4] * (sq_x - sq_y),
        harmonic_three[0] * dir_y * (3 * sq_x - sq_y),
        harmonic_three[1] * dir_x * dir_y * dir_z,
        harmonic_three[2] * dir_y * (4 * sq_z - sq_x - sq_y),
        harmonic_three[3] * dir_z * (2 * sq_z - 3 * sq_x - 3 * sq_y),
        harmonic_three[4] * dir_x * (4 * sq_z - sq_x - sq_y),
        harmonic_three[5] * dir_z * (sq_x - sq_y),
        harmonic_three[6] * dir_x * (sq_x - 3 * sq_y),
    )


def plane(ref, half, row):
    return ref[pl.ds(half * SUB * ROWS + row, SUB, stride=ROWS), :]


def put_plane(ref, half, row, value):
    ref[pl.ds(half * SUB * ROWS + row, SUB, stride=ROWS), :] = value


def raw_colour(pool, half, basis, colour):
    total = harmonic_zero * plane(pool, half, 11 + 16 * colour) + 0.5
    for k in range(1, 16):
        total = total + plane(pool, half, 11 + 16 * colour + k) * basis[k - 1]
    return total


def own_block(number):
    return jnp.where(number == 0, LOW, jnp.where(number == POOL - 1, HIGH, number - 1))


def roll_rows(value, shift):
    return pltpu.roll(value, shift % SUB, axis=0)


def tabulate(half, count, pool, stage, turned, table, spread):
    region = lax.axis_index("region")
    regions = lax.axis_size("region")
    means = [plane(pool, half, r) for r in range(3)]
    centre_u, centre_v, conic_xx, conic_xy, conic_yy = geometry(
        *means, *[plane(pool, half, r) for r in range(3, 10)]
    )
    opacity = 1.0 / (1.0 + jnp.exp(-plane(pool, half, 10)))
    log2_e = 1.0 / math.log(2.0)
    slope_x = conic_xx * centre_u + conic_xy * centre_v
    slope_y = conic_xy * centre_u + conic_yy * centre_v
    constant = jnp.log(opacity) - 0.5 * (centre_u * slope_x + centre_v * slope_y)
    constant = log2_e * constant
    if half:
        row = iota((SUB, BLOCK), 0)
        absent = ((row == LOW - SUB) & (region == 0)) | ((row == HIGH - SUB) & (region == regions - 1))
        constant = jnp.where(absent, -1e30, constant)
    terms = [
        constant,
        log2_e * slope_x,
        log2_e * slope_y,
        (-0.5 * log2_e) * conic_xx,
        (-log2_e) * conic_xy,
        (-0.5 * log2_e) * conic_yy,
    ]
    stage[...] = jnp.zeros_like(stage)

    def put(row, value):
        stage[pl.ds(row, SUB, stride=COLS), :] = value

    row = 0
    for term, copies in zip(terms, (1, 1, 1, 2, 2, 2)):
        parts = [part.astype(f32) for part in split(term, 3)]
        for _ in range(copies):
            for part in parts:
                put(row, part)
                row += 1
    basis = harmonics(*means)
    for c in range(3):
        tone = jnp.maximum(raw_colour(pool, half, basis, c), 0.0)
        parts = [part.astype(f32) for part in split(tone, 3)]
        for group, part in enumerate((0, 0, 0, 1, 1, 2)):
            put(32 + group * SUB + c, parts[part])
        put(80 + c, tone)

    def turn(b, carry):
        turned[:, :COLS] = stage[pl.ds(pl.multiple_of(b * COLS, COLS), COLS), :].T
        ordered = jnp.concatenate(
            [turned[pl.ds(t, SUB, stride=STEPS), :] for t in range(STEPS)], axis=0
        )
        table[half * SUB + b] = ordered[:, :COLS].astype(bf16)
        for c in range(3):
            spread[half * SUB + b, c] = jnp.broadcast_to(ordered[:, 80 + c : 81 + c], (BLOCK, BLOCK))
        return carry

    lax.fori_loop(0, count, turn, 0, unroll=2)


def exponents(table, features, block):
    return jnp.dot(table[block, :, :32], features, preferred_element_type=f32)


def two_blocks(p, blocks, live):
    first = own_block(blocks[0, p])
    second = jnp.where(live[0, p] > 1, own_block(blocks[1, p]), DEAD)
    return first, second


def forward_half(
    h, blocks, live, features_ref, table, spread, prefix_ref, segment_ref, pieces, alphas_ref
):
    sub = iota((SUB, WIDE), 0)

    def piece(p, carry):
        features = features_ref[p, :, h * WIDE : (h + 1) * WIDE]
        before = None
        colours = [None] * 3
        for j, block in enumerate(two_blocks(p, blocks, live)):
            exponent = exponents(table, features, block)
            transmit = jnp.ones((SUB, WIDE), f32)
            sums = [jnp.zeros((SUB, WIDE), f32) for _ in range(3)]
            for t in range(STEPS):
                rows = slice(t * SUB, (t + 1) * SUB)
                alpha = jnp.exp2(exponent[rows])
                alphas_ref[h, p, j, rows] = alpha
                weight = alpha * transmit
                transmit = transmit - weight
                for c in range(3):
                    tone = spread[block, c, rows, :]
                    tone = tone if WIDE == BLOCK else jnp.concatenate([tone, tone], axis=1)
                    sums[c] = sums[c] + tone * weight
            run = transmit
            for shift in (1, 2, 4):
                run = run * jnp.where(sub >= shift, roll_rows(run, shift), 1.0)
            prefix = jnp.where(sub >= 1, roll_rows(run, 1), 1.0)
            total = run[SUB - 1 :, :]
            if before is not None:
                prefix = prefix * before
                total = total * before
            before = total
            prefix_ref[h, p, j] = prefix
            for c in range(3):
                piece_sum = prefix * sums[c]
                segment_ref[h, p, j, c] = piece_sum
                colours[c] = piece_sum if j == 0 else colours[c] + piece_sum
        rows = [jnp.sum(colours[c], axis=0, keepdims=True) for c in range(3)] + [1.0 - before]
        for c in range(4):
            for k in range(WIDE // BLOCK):
                place = (c * (WIDE // BLOCK) + k) * PIECES + p
                pieces[pl.ds(place, 1), :] = rows[c][:, k * BLOCK : (k + 1) * BLOCK]
        return carry

    lax.fori_loop(0, PIECES, piece, 0, unroll=UNROLL)


def weigh_half(h, prefix_ref, alphas_ref, weights_ref, ends_ref, weight_parts_ref):
    def piece(p, carry):
        for j in range(2):
            transmit = prefix_ref[h, p, j]
            weights = []
            for t in range(STEPS):
                rows = slice(t * SUB, (t + 1) * SUB)
                weight = alphas_ref[h, p, j, rows] * transmit
                transmit = transmit - weight
                weights_ref[h, p, j, rows] = weight
                weights.append(weight)
            ends_ref[h, p, j] = transmit
            weight_parts_ref[h, p, j * BLOCK : (j + 1) * BLOCK] = jnp.concatenate(
                split(jnp.concatenate(weights, axis=0), 2), axis=1
            )
        return carry

    lax.fori_loop(0, PIECES, piece, 0, unroll=MIDDLE_UNROLL)


def backward_half(
    h, blocks, live, moments_ref, table, segment_ref, alphas_ref, weights_ref, ends_ref, weight_parts_ref,
    cotangent, moved,
):
    sub = iota((SUB, WIDE), 0)
    nothing = jnp.zeros((16, WIDE), bf16)
    none = jnp.zeros((16, WIDE), f32)
    lanes = slice(h * WIDE, (h + 1) * WIDE)

    def piece(p, carry):
        monomials = moments_ref[p, :, lanes]
        cot = jnp.concatenate(
            [
                cotangent[pl.ds(pl.multiple_of((k * PIECES + p) * SUB, SUB), SUB), :]
                for k in range(WIDE // BLOCK)
            ],
            axis=1,
        )
        heads = [part.astype(f32) for part in split(cot, 3)]
        tones = [none, none] + [heads[part] for part in (0, 1, 2, 0, 1, 0)] + [none]
        tones = jnp.concatenate(tones, axis=0).astype(bf16)
        colour_rows = jnp.concatenate([heads[0], heads[1]], axis=0).astype(bf16)
        for_gradient = jnp.concatenate([monomials, nothing], axis=0)
        for_weight = jnp.concatenate([nothing, colour_rows], axis=0)
        state = []
        for j, block in enumerate(two_blocks(p, blocks, live)):
            tone = jnp.dot(table[block], tones, preferred_element_type=f32)
            seen = segment_ref[h, p, j, 0] * cot[0:1]
            for c in (1, 2):
                seen = seen + segment_ref[h, p, j, c] * cot[c : c + 1]
            run = seen
            for shift in (1, 2, 4):
                run = run + jnp.where(sub < SUB - shift, roll_rows(run, -shift), 0.0)
            state.append((tone, run))
        behind = ends_ref[h, p, 1, SUB - 1 :, :] * cot[3:4]
        parts = [None, None]
        for j in (1, 0):
            tone, run = state[j]
            after = jnp.where(sub < SUB - 1, roll_rows(run, -1), 0.0) + behind
            behind = behind + run[0:1]
            ahead = after / ends_ref[h, p, j]
            gradients = [None] * STEPS
            for t in reversed(range(STEPS)):
                rows = slice(t * SUB, (t + 1) * SUB)
                gap = tone[rows] - ahead
                gradients[t] = weights_ref[h, p, j, rows] * gap
                ahead = ahead + alphas_ref[h, p, j, rows] * gap
            parts[j] = jnp.concatenate(split(jnp.concatenate(gradients, axis=0), 2), axis=1)
        both = [jnp.concatenate(parts, axis=0), weight_parts_ref[h, p]]
        total = None
        for k in range(2):
            rows = (for_gradient, for_weight)[k]
            term = lax.dot_general(
                jnp.concatenate([rows, rows], axis=1),
                both[k],
                (((1,), (1,)), ((), ())),
                preferred_element_type=f32,
            )
            total = term if total is None else total + term
        for j in range(2):
            rows = pl.ds(pl.multiple_of((j * PIECES + p) * 32, 32), 32)
            part = total[:, j * BLOCK : (j + 1) * BLOCK]
            moved[rows, :] = part if h == 0 else moved[rows, :] + part
        return carry

    lax.fori_loop(0, PIECES, piece, 0, unroll=UNROLL)


def gather_moments(first_row, second_row, moved, summed):
    numbers = iota((2 * SUB, PIECES), 0).astype(f32)
    lane = iota((BLOCK, BLOCK), 0)
    unshuffle = (lane % SUB) * STEPS + lane // SUB == iota((BLOCK, BLOCK), 1)
    unshuffle = jnp.where(unshuffle, 1.0, 0.0).astype(bf16)
    for group in range(3):
        features = range(group * SUB, group * SUB + SUB)
        features = [f for f in features if f < 9] + [16 + f - 9 for f in features if 9 <= f < 12]
        features += [24 + f - 12 for f in range(group * SUB, group * SUB + SUB) if 12 <= f < 15]
        if not features:
            continue
        total = None
        for j, row in enumerate((first_row, second_row)):
            pick = jnp.where(jnp.broadcast_to(row, (2 * SUB, PIECES)) == numbers, 1.0, 0.0)
            values = [
                moved[pl.ds(j * PIECES * 32 + f, PIECES, stride=32), :] for f in features
            ]
            term = exact_pick(pick, jnp.concatenate(values, axis=1))
            total = term if total is None else total + term
        stacked = jnp.concatenate(
            [total[:, k * BLOCK : (k + 1) * BLOCK] for k in range(len(features))], axis=0
        )
        ordered = None
        for part in reversed(split(stacked, 3)):
            term = jnp.dot(part, unshuffle, preferred_element_type=f32)
            ordered = term if ordered is None else ordered + term
        for k, f in enumerate(features):
            summed[f] = ordered[k * 2 * SUB : (k + 1) * 2 * SUB]


def pull_splat(half, pool, summed, grads_ref):
    means = [plane(pool, half, r) for r in range(3)]
    (centre_u, centre_v, conic_xx, conic_xy, conic_yy), geometry_pull = jax.vjp(
        geometry, *means, *[plane(pool, half, r) for r in range(3, 10)]
    )
    basis, harmonics_pull = jax.vjp(harmonics, *means)
    opacity = 1.0 / (1.0 + jnp.exp(-plane(pool, half, 10)))
    sums = [summed[f, half * SUB : (half + 1) * SUB] for f in range(9)]
    total, sum_x, sum_y = sums[:3]
    sum_xx, sum_xy, sum_yy = sums[3] + sums[4], sums[5] + sums[6], sums[7] + sums[8]
    off_x = sum_x - centre_u * total
    off_y = sum_y - centre_v * total
    grad_xx = -0.5 * (sum_xx - centre_u * (sum_x + off_x))
    grad_xy = -(sum_xy - centre_u * sum_y - centre_v * off_x)
    grad_yy = -0.5 * (sum_yy - centre_v * (sum_y + off_y))
    grad_u = conic_xx * off_x + conic_xy * off_y
    grad_v = conic_xy * off_x + conic_yy * off_y
    grads = geometry_pull((grad_u, grad_v, grad_xx, grad_xy, grad_yy))
    tone_grads = []
    for c in range(3):
        grad = summed[16 + c, half * SUB : (half + 1) * SUB] + summed[24 + c, half * SUB : (half + 1) * SUB]
        raw = raw_colour(pool, half, basis, c)
        tone_grads.append(jnp.where(raw > 0, grad, jnp.where(raw == 0, 0.5 * grad, 0.0)))
    basis_grads = []
    for k in range(1, 16):
        basis_grads.append(
            sum(tone_grads[c] * plane(pool, half, 11 + 16 * c + k) for c in range(3))
        )
    mean_grads = harmonics_pull(tuple(basis_grads))
    for r in range(10):
        put_plane(grads_ref, half, r, grads[r] + mean_grads[r] if r < 3 else grads[r])
    put_plane(grads_ref, half, 10, total * (1.0 - opacity))
    for c in range(3):
        put_plane(grads_ref, half, 11 + 16 * c, tone_grads[c] * harmonic_zero)
        for k in range(1, 16):
            put_plane(grads_ref, half, 11 + 16 * c + k, tone_grads[c] * basis[k - 1])


PARTS = 4 * WIDE // BLOCK
MESSAGE = SLOTS * PARTS


def put_slots(ref, values):
    for k in range(SLOTS):
        for r in range(PARTS):
            ref[pl.ds(k * PARTS + r, 32, stride=MESSAGE), :] = values[
                k * 32 : (k + 1) * 32, r * BLOCK : (r + 1) * BLOCK
            ]


def get_slots(ref):
    return jnp.concatenate(
        [
            jnp.concatenate(
                [ref[pl.ds(k * PARTS + r, 32, stride=MESSAGE), :] for r in range(PARTS)], axis=1
            )
            for k in range(SLOTS)
        ],
        axis=0,
    )


def route(owner_row, cell_row, me):
    owner_col = to_column(owner_row)
    far_row = owner_row - me.astype(f32)
    far_row = jnp.where(far_row < 0, far_row + float(PIECES), far_row)
    far_col = to_column(far_row)
    square = (PIECES, PIECES)
    same = jnp.broadcast_to(owner_row, square) == jnp.broadcast_to(owner_col, square)
    first, second = iota(square, 0), iota(square, 1)
    rank_row = jnp.sum(jnp.where(same & (first < second), 1.0, 0.0), axis=0, keepdims=True)
    rank_col = jnp.sum(jnp.where(same & (second < first), 1.0, 0.0), axis=1, keepdims=True)
    slots = SLOTS * 32
    pack = jnp.broadcast_to(rank_row * 32.0 + far_row, (slots, PIECES)) == iota((slots, PIECES), 0).astype(f32)
    pack = jnp.where(pack, 1.0, 0.0)
    unpack = jnp.broadcast_to(rank_col * 32.0 + far_col, (PIECES, slots)) == iota((PIECES, slots), 1).astype(f32)
    unpack = jnp.where(unpack, 1.0, 0.0)
    label_col = jnp.sum(pack * (cell_row + 1.0), axis=1, keepdims=True) - 1.0
    lane = iota((32, BLOCK), 1)
    label_rows = jnp.where(lane == 0, label_col[:32], jnp.where(lane == 1, label_col[32:], -1.0))
    return pack, unpack, label_rows


def composite(h, grid, target, background):
    def at(depth, channel):
        return grid[depth * SUB : (depth + 1) * SUB, channel * WIDE : (channel + 1) * WIDE]

    in_front = jnp.ones((TILE_DEV, WIDE), f32)
    seen = [jnp.zeros((TILE_DEV, WIDE), f32) for _ in range(3)]
    fronts = []
    for depth in range(MAXD):
        fronts.append(in_front)
        seen = [seen[c] + in_front * at(depth, c) for c in range(3)]
        in_front = in_front * (1.0 - at(depth, 3))
    residual = [
        seen[c] + in_front * background[c] - target[c, :, h * WIDE : (h + 1) * WIDE] for c in range(3)
    ]
    behind = [jnp.full((TILE_DEV, WIDE), background[c], f32) for c in range(3)]
    rows = [None] * MAXD
    for depth in reversed(range(MAXD)):
        through = 1.0 - at(depth, 3)
        by_trans = residual[0] * behind[0] + residual[1] * behind[1] + residual[2] * behind[2]
        rows[depth] = jnp.concatenate(
            [fronts[depth] * residual[c] for c in range(3)] + [fronts[depth] * by_trans], axis=1
        )
        behind = [at(depth, c) + through * behind[c] for c in range(3)]
    return jnp.concatenate(rows, axis=0)


def step_kernel(
    params_hbm,
    blocks_hbm,
    live_hbm,
    owner_hbm,
    cell_hbm,
    target_hbm,
    background_hbm,
    features_hbm,
    moments_hbm,
    grads_ref,
    blocks,
    live,
    background,
    block_rows,
    owner,
    cell,
    target,
    features,
    moments,
    pool,
    stage,
    turned,
    table,
    spread,
    prefix,
    segment,
    alphas,
    weights,
    ends,
    weight_parts,
    pieces,
    sent,
    got,
    replies,
    answers,
    labels,
    got_labels,
    cotangent,
    moved,
    summed,
    local_sem,
    halo_send,
    halo_recv,
    edge_send,
    edge_recv,
    label_send,
    label_recv,
    send_sem,
    recv_sem,
    reply_send,
    reply_recv,
):
    regions, region = lax.axis_size("region"), lax.axis_index("region")
    count, me = lax.axis_size("dom"), lax.axis_index("dom")
    upper, lower = lax.rem(region + 1, regions), lax.rem(region + regions - 1, regions)

    def block_rows_of(ref, b):
        return ref.at[pl.ds(b * ROWS, PARAMS)]

    fetches = []

    def fetch(src, dst):
        copy = pltpu.make_async_copy(src, dst, local_sem.at[len(fetches)])
        copy.start()
        fetches.append(copy)
        return copy

    routing = [fetch(owner_hbm, owner), fetch(cell_hbm, cell)]
    own = [
        fetch(params_hbm.at[:, pl.ds(b * BLOCK, BLOCK)], block_rows_of(pool, b)) for b in range(BLOCKS)
    ]
    scalars = [fetch(blocks_hbm, blocks), fetch(live_hbm, live), fetch(features_hbm, features)]
    later = [
        fetch(blocks_hbm, block_rows),
        fetch(target_hbm, target),
        fetch(background_hbm, background),
        fetch(moments_hbm, moments),
    ]

    barrier = pltpu.get_barrier_semaphore()

    def signal(**where):
        pl.semaphore_signal(barrier, inc=1, device_id=where, device_id_type=MESH)

    def greet(d, carry):
        signal(dom=lax.rem(me + d, count))
        return carry

    signal(region=upper)
    signal(region=lower)
    lax.fori_loop(1, count, greet, 0)

    for copy in routing:
        copy.wait()
    pack, unpack, label_rows = route(owner[...].astype(f32), cell[...].astype(f32), me)
    for d in range(32):
        labels[d] = label_rows[d : d + 1]
    pl.semaphore_wait(barrier, count + 1)

    def remote(src, dst, send, recv, **where):
        return pltpu.make_async_remote_copy(
            src_ref=src, dst_ref=dst, send_sem=send, recv_sem=recv, device_id=where, device_id_type=MESH
        )

    def label(d, many=1):
        rows = pl.ds(d, many)
        return remote(
            labels.at[rows], got_labels.at[rows], label_send, label_recv, dom=lax.rem(me + d, count)
        )

    def message(d, many):
        return pl.ds(pl.multiple_of(d * MESSAGE, MESSAGE), many * MESSAGE)

    def payload(h, d, many=1):
        rows = message(d, many)
        return remote(
            sent.at[h, rows], got.at[h, rows], send_sem.at[h], recv_sem.at[h], dom=lax.rem(me + d, count)
        )

    def reply(h, d, many=1):
        rows = message(d, many)
        return remote(
            replies.at[h, rows],
            answers.at[h, rows],
            reply_send.at[h],
            reply_recv.at[h],
            dom=lax.rem(me + count - d, count),
        )

    def start_all(copy):
        def one(d, carry):
            copy(d).start()
            return carry

        lax.fori_loop(1, count, one, 0, unroll=START_UNROLL)

    others = count - 1

    halo = [
        remote(
            params_hbm.at[:, pl.ds((BLOCKS - 1) * BLOCK, BLOCK)],
            block_rows_of(pool, LOW),
            halo_send.at[0],
            halo_recv.at[0],
            region=upper,
        ),
        remote(
            params_hbm.at[:, pl.ds(0, BLOCK)],
            block_rows_of(pool, HIGH),
            halo_send.at[1],
            halo_recv.at[1],
            region=lower,
        ),
    ]
    for copy in halo:
        copy.start()
    start_all(label)
    got_labels[0] = labels[0]

    for copy in own:
        copy.wait()
    for b in range(POOL, 2 * SUB):
        pool[b * ROWS : b * ROWS + PARAMS, :] = pool[0:PARAMS, :]
    tabulate(0, SUB, pool, stage, turned, table, spread)
    for copy in halo:
        copy.wait_recv()
    tabulate(1, POOL - SUB, pool, stage, turned, table, spread)
    lane = iota((BLOCK, COLS), 1)
    table[DEAD] = jnp.where(lane == 0, -1e30, 0.0).astype(bf16)
    spread[DEAD] = jnp.zeros((3, BLOCK, BLOCK), f32)

    for copy in scalars:
        copy.wait()
    for h in range(HALVES):
        forward_half(h, blocks, live, features, table, spread, prefix, segment, pieces, alphas)
        rendered = [pieces[r * PIECES : (r + 1) * PIECES, :] for r in range(PARTS)]
        rendered = jnp.concatenate(rendered, axis=1)
        put_slots(sent.at[h], exact_pick(pack, rendered))
        start_all(functools.partial(payload, h))
        got[h, :MESSAGE] = sent[h, :MESSAGE]

    weigh_half(0, prefix, alphas, weights, ends, weight_parts)
    for copy in later:
        copy.wait()
    label(1, others).wait()
    arrived = jnp.concatenate([got_labels[d] for d in range(32)], axis=0)
    arrived_col = jnp.concatenate([arrived[:, 0:1], arrived[:, 1:2]], axis=0)
    arrived_row = to_row(arrived_col)
    slots = SLOTS * 32

    def cell_of(place):
        return ((place % TILE_DEV) * MAXD + place // TILE_DEV).astype(f32)

    gather = jnp.broadcast_to(arrived_row, (CELLS, slots)) == cell_of(iota((CELLS, slots), 0))
    gather = jnp.where(gather, 1.0, 0.0)
    scatter = jnp.broadcast_to(arrived_col, (slots, CELLS)) == cell_of(iota((slots, CELLS), 1))
    scatter = jnp.where(scatter, 1.0, 0.0)
    colours = [background[c] for c in range(3)]
    for h in range(HALVES):
        payload(h, 1, others).wait()
        grid = exact_pick(gather, get_slots(got.at[h]))
        put_slots(replies.at[h], exact_pick(scatter, composite(h, grid, target, colours)))
        start_all(functools.partial(reply, h))
        answers[h, :MESSAGE] = replies[h, :MESSAGE]
        if h + 1 < HALVES:
            weigh_half(h + 1, prefix, alphas, weights, ends, weight_parts)

    for h in range(HALVES):
        reply(h, 1, others).wait()
        back = exact_pick(unpack, get_slots(answers.at[h]))
        for k in range(WIDE // BLOCK):
            for c in range(SUB):
                lanes = slice(c * WIDE + k * BLOCK, c * WIDE + (k + 1) * BLOCK)
                rows = back[:, lanes] if c < 4 else jnp.zeros((PIECES, BLOCK), f32)
                cotangent[pl.ds(k * PIECES * SUB + c, PIECES, stride=SUB), :] = rows
        backward_half(
            h, blocks, live, moments, table, segment, alphas, weights, ends, weight_parts, cotangent, moved
        )

    rows = own_block(block_rows[...]).astype(f32)
    gather_moments(rows[0:1], rows[1:2], moved, summed)
    pull_splat(1, pool, summed, grads_ref)
    edges = [
        remote(block_rows_of(grads_ref, HIGH), block_rows_of(grads_ref, FROM_LEFT), edge_send.at[0], edge_recv.at[0], region=upper),
        remote(block_rows_of(grads_ref, LOW), block_rows_of(grads_ref, FROM_RIGHT), edge_send.at[1], edge_recv.at[1], region=lower),
    ]
    for copy in edges:
        copy.start()
    pull_splat(0, pool, summed, grads_ref)
    for copy in halo:
        copy.wait_send()
    for copy in edges:
        copy.wait()


def whole(memory=pltpu.VMEM):
    return pl.BlockSpec(memory_space=memory)


def step(*operands):
    shape = jax.ShapeDtypeStruct
    vmem, smem, dma = pltpu.VMEM, pltpu.SMEM, pltpu.SemaphoreType.DMA
    slots = vmem((HALVES, 32 * MESSAGE, BLOCK), f32)
    label = vmem((32, 1, BLOCK), f32)
    return pl.pallas_call(
        step_kernel,
        out_shape=shape(((FROM_RIGHT + 1) * ROWS, BLOCK), f32),
        in_specs=[whole(pltpu.HBM)] * 9,
        out_specs=whole(),
        scratch_shapes=[
            smem((2, PIECES), jnp.int32),
            smem((1, PIECES), jnp.int32),
            smem((3,), f32),
            vmem((2, PIECES), jnp.int32),
            vmem((1, PIECES), jnp.int32),
            vmem((1, PIECES), jnp.int32),
            vmem((3, TILE_DEV, PIX), f32),
            vmem((PIECES, 32, PIX), bf16),
            vmem((PIECES, 16, PIX), bf16),
            vmem((2 * SUB * ROWS, BLOCK), f32),
            vmem((SUB * COLS, BLOCK), f32),
            vmem((BLOCK, BLOCK), f32),
            vmem((TAB, BLOCK, COLS), bf16),
            vmem((TAB, 3, BLOCK, BLOCK), f32),
            vmem((HALVES, PIECES, 2, SUB, WIDE), f32),
            vmem((HALVES, PIECES, 2, 3, SUB, WIDE), f32),
            vmem((HALVES, PIECES, 2, BLOCK, WIDE), f32),
            vmem((HALVES, PIECES, 2, BLOCK, WIDE), f32),
            vmem((HALVES, PIECES, 2, SUB, WIDE), f32),
            vmem((HALVES, PIECES, 2 * BLOCK, 2 * WIDE), bf16),
            vmem((4 * WIDE // BLOCK * PIECES, BLOCK), f32),
            slots,
            slots,
            slots,
            slots,
            label,
            label,
            vmem((WIDE // BLOCK * PIECES * SUB, BLOCK), f32),
            vmem((2 * PIECES * 32, BLOCK), f32),
            vmem((32, 2 * SUB, BLOCK), f32),
            dma((17,)),
            dma((2,)),
            dma((2,)),
            dma((2,)),
            dma((2,)),
            dma,
            dma,
            dma((HALVES,)),
            dma((HALVES,)),
            dma((HALVES,)),
            dma((HALVES,)),
        ],
        compiler_params=pltpu.CompilerParams(
            collective_id=0, has_side_effects=True, vmem_limit_bytes=VMEM_LIMIT
        ),
        name="render_step",
    )(*operands)


def adam_kernel(
    grads_ref, params_ref, first_ref, second_ref,
    gradient_ref, new_params_ref, new_first_ref, new_second_ref,
):
    for b in range(BLOCKS):
        cols = slice(b * BLOCK, (b + 1) * BLOCK)
        gradient = grads_ref[b * ROWS : b * ROWS + PARAMS, :]
        if b == 0:
            gradient = gradient + grads_ref[FROM_LEFT * ROWS : FROM_LEFT * ROWS + PARAMS, :]
        if b == BLOCKS - 1:
            gradient = gradient + grads_ref[FROM_RIGHT * ROWS : FROM_RIGHT * ROWS + PARAMS, :]
        new_first = beta_one * first_ref[:, cols] + (1 - beta_one) * gradient
        new_second = beta_two * second_ref[:, cols] + (1 - beta_two) * gradient * gradient
        update = (
            new_first
            / (1 - beta_one**adam_step)
            / (jnp.sqrt(new_second / (1 - beta_two**adam_step)) + tiny)
        )
        gradient_ref[:, cols] = gradient
        new_params_ref[:, cols] = params_ref[:, cols] - rate * update
        new_first_ref[:, cols] = new_first
        new_second_ref[:, cols] = new_second


def adam(*operands):
    return pl.pallas_call(
        adam_kernel,
        out_shape=(jax.ShapeDtypeStruct((PARAMS, BLOCKS * BLOCK), f32),) * 4,
        in_specs=[whole()] * 4,
        out_specs=(whole(),) * 4,
        compiler_params=pltpu.CompilerParams(vmem_limit_bytes=8 * 1024 * 1024),
        name="adam",
    )(*operands)


def on_device(
    params,
    first_moment,
    second_moment,
    piece_blocks,
    piece_live,
    piece_owner,
    piece_cell,
    target,
    background,
):
    grads = step(
        params,
        piece_blocks[0].T,
        piece_live,
        piece_owner,
        piece_cell,
        jnp.transpose(target[0], (1, 0, 2)),
        background,
        jnp.asarray(exponent_features()),
        jnp.asarray(moment_features()),
    )
    return adam(grads, params, first_moment, second_moment)


def solution(mesh):
    in_specs = (
        P(None, ("region", "dom")),
        P(None, ("region", "dom")),
        P(None, ("region", "dom")),
        P(("region", "dom"), None, None),
        P(("region", "dom"), None),
        P(("region", "dom"), None),
        P(("region", "dom"), None),
        P(("region", "dom"), None, None, None),
        P(),
    )
    out_specs = (
        P(None, ("region", "dom")),
        P(None, ("region", "dom")),
        P(None, ("region", "dom")),
        P(None, ("region", "dom")),
    )
    return jax.shard_map(
        on_device, mesh=mesh, in_specs=in_specs, out_specs=out_specs, check_vma=False
    )
```

```python
import functools
import math

import jax
import jax.numpy as jnp
import ml_dtypes
import numpy as np
from jax import lax
from jax.experimental import pallas as pl
from jax.experimental.pallas import tpu as pltpu
from jax.sharding import PartitionSpec as P

PARAMS = 59
TSIDE = 16
WIN = 8
BLOCK = 128
BLOCKS = 8
MAXD = 8
PIECES = 32
PIX = 256
TILE_DEV = 8
CELLS = 64
POOL = 10
SLOTS = 2
SUB = 8
STEPS = BLOCK // SUB
TAB = POOL + 1
PLANES = 16
ROWS = 64
COLS = 96
UNROLL = 16
MIDDLE_UNROLL = 4
START_UNROLL = 1
HALVES = 2
WIDE = PIX // HALVES
LOW = BLOCKS
HIGH = BLOCKS + 1
DEAD = POOL
FROM_LEFT = 2 * SUB
FROM_RIGHT = FROM_LEFT + 1
ORIGIN_X = 64.0
ORIGIN_Y = 32.0

harmonic_zero = 0.28209479177387814
harmonic_one = 0.4886025119029199
harmonic_two = (
    1.0925484305920792,
    -1.0925484305920792,
    0.31539156525252005,
    -1.0925484305920792,
    0.5462742152960396,
)
harmonic_three = (
    -0.5900435899266435,
    2.890611442640554,
    -0.4570457994644658,
    0.3731763325901154,
    -0.4570457994644658,
    1.445305721320277,
    -0.5900435899266435,
)
beta_one = 0.9
beta_two = 0.999
rate = 0.001
adam_step = 100
tiny = 1e-08

f32 = jnp.float32
bf16 = jnp.bfloat16
MESH = pl.DeviceIdType.MESH
VMEM_LIMIT = 60 * 1024 * 1024


def pixel_monomials():
    bf = ml_dtypes.bfloat16
    tile = np.arange(PIECES)[:, None]
    pixel = np.arange(PIX)[None, :]
    x = (TSIDE * (tile % WIN) + pixel % TSIDE + 0.5 - ORIGIN_X).astype(np.float32)
    y = (TSIDE * (tile // WIN) + pixel // TSIDE + 0.5 - ORIGIN_Y).astype(np.float32)

    def two(value):
        head = value.astype(bf).astype(np.float32)
        return [head, value - head]

    return [np.ones_like(x), x, y] + two(x * x) + two(x * y) + two(y * y)


def exponent_features():
    rows = [row for row in pixel_monomials() for _ in range(3)]
    rows += [np.zeros_like(rows[0])] * (32 - len(rows))
    return np.stack(rows, axis=1).astype(ml_dtypes.bfloat16)


def moment_features():
    rows = pixel_monomials()
    rows += [np.zeros_like(rows[0])] * (16 - len(rows))
    return np.stack(rows, axis=1).astype(ml_dtypes.bfloat16)


def split(value, parts):
    out = []
    rest = value
    for part in range(parts):
        head = rest.astype(bf16)
        out.append(head)
        if part < parts - 1:
            rest = rest - head.astype(f32)
    return out


def exact_pick(onehot, value):
    picks = onehot.astype(bf16)
    total = None
    for part in reversed(split(value, 3)):
        term = jnp.dot(picks, part, preferred_element_type=f32)
        total = term if total is None else total + term
    return total


def iota(shape, dim):
    return lax.broadcasted_iota(jnp.int32, shape, dim)


def to_column(row):
    n = row.shape[1]
    spread = jnp.broadcast_to(row, (n, n))
    return jnp.sum(jnp.where(iota((n, n), 0) == iota((n, n), 1), spread, 0.0), axis=1, keepdims=True)


def to_row(column):
    n = column.shape[0]
    spread = jnp.broadcast_to(column, (n, n))
    return jnp.sum(jnp.where(iota((n, n), 0) == iota((n, n), 1), spread, 0.0), axis=0, keepdims=True)


def geometry(mean_x, mean_y, mean_z, log_a, log_b, log_c, quat_w, quat_x, quat_y, quat_z):
    screen_px = float(WIN * TSIDE)
    scales = (jnp.exp(log_a), jnp.exp(log_b), jnp.exp(log_c))
    norm = 1.0 / jnp.sqrt(quat_w * quat_w + quat_x * quat_x + quat_y * quat_y + quat_z * quat_z)
    quat_w, quat_x, quat_y, quat_z = quat_w * norm, quat_x * norm, quat_y * norm, quat_z * norm
    rotation = [
        [
            1 - 2 * (quat_y * quat_y + quat_z * quat_z),
            2 * (quat_x * quat_y - quat_w * quat_z),
            2 * (quat_x * quat_z + quat_w * quat_y),
        ],
        [
            2 * (quat_x * quat_y + quat_w * quat_z),
            1 - 2 * (quat_x * quat_x + quat_z * quat_z),
            2 * (quat_y * quat_z - quat_w * quat_x),
        ],
        [
            2 * (quat_x * quat_z - quat_w * quat_y),
            2 * (quat_y * quat_z + quat_w * quat_x),
            1 - 2 * (quat_x * quat_x + quat_y * quat_y),
        ],
    ]
    focal_px = 0.3125 * screen_px
    inv_z = 1.0 / mean_z
    ratio_x, ratio_y = mean_x * inv_z, mean_y * inv_z
    focal_z = focal_px * inv_z
    rows = []
    for ratio, axis in ((ratio_x, 0), (ratio_y, 1)):
        rows.append(
            [
                focal_z * (rotation[axis][col] - ratio * rotation[2][col]) * scales[col]
                for col in range(3)
            ]
        )
    sigma_xx = rows[0][0] * rows[0][0] + rows[0][1] * rows[0][1] + rows[0][2] * rows[0][2] + 0.3
    sigma_xy = rows[0][0] * rows[1][0] + rows[0][1] * rows[1][1] + rows[0][2] * rows[1][2]
    sigma_yy = rows[1][0] * rows[1][0] + rows[1][1] * rows[1][1] + rows[1][2] * rows[1][2] + 0.3
    inv_det = 1.0 / (sigma_xx * sigma_yy - sigma_xy * sigma_xy)
    return (
        focal_px * ratio_x + (0.5 * screen_px - ORIGIN_X),
        focal_px * ratio_y + (0.5 * screen_px - ORIGIN_Y),
        sigma_yy * inv_det,
        -sigma_xy * inv_det,
        sigma_xx * inv_det,
    )


def harmonics(mean_x, mean_y, mean_z):
    inv_length = 1.0 / jnp.sqrt(mean_x * mean_x + mean_y * mean_y + mean_z * mean_z)
    dir_x, dir_y, dir_z = mean_x * inv_length, mean_y * inv_length, mean_z * inv_length
    sq_x, sq_y, sq_z = dir_x * dir_x, dir_y * dir_y, dir_z * dir_z
    return (
        -harmonic_one * dir_y,
        harmonic_one * dir_z,
        -harmonic_one * dir_x,
        harmonic_two[0] * dir_x * dir_y,
        harmonic_two[1] * dir_y * dir_z,
        harmonic_two[2] * (2 * sq_z - sq_x - sq_y),
        harmonic_two[3] * dir_x * dir_z,
        harmonic_two[4] * (sq_x - sq_y),
        harmonic_three[0] * dir_y * (3 * sq_x - sq_y),
        harmonic_three[1] * dir_x * dir_y * dir_z,
        harmonic_three[2] * dir_y * (4 * sq_z - sq_x - sq_y),
        harmonic_three[3] * dir_z * (2 * sq_z - 3 * sq_x - 3 * sq_y),
        harmonic_three[4] * dir_x * (4 * sq_z - sq_x - sq_y),
        harmonic_three[5] * dir_z * (sq_x - sq_y),
        harmonic_three[6] * dir_x * (sq_x - 3 * sq_y),
    )


def plane(ref, half, row):
    return ref[pl.ds(half * SUB * ROWS + row, SUB, stride=ROWS), :]


def put_plane(ref, half, row, value):
    ref[pl.ds(half * SUB * ROWS + row, SUB, stride=ROWS), :] = value


def raw_colour(pool, half, basis, colour):
    total = harmonic_zero * plane(pool, half, 11 + 16 * colour) + 0.5
    for k in range(1, 16):
        total = total + plane(pool, half, 11 + 16 * colour + k) * basis[k - 1]
    return total


def own_block(number):
    return jnp.where(number == 0, LOW, jnp.where(number == POOL - 1, HIGH, number - 1))


def roll_rows(value, shift):
    return pltpu.roll(value, shift % SUB, axis=0)


def tabulate(half, count, pool, stage, turned, table, spread):
    region = lax.axis_index("region")
    regions = lax.axis_size("region")
    means = [plane(pool, half, r) for r in range(3)]
    centre_u, centre_v, conic_xx, conic_xy, conic_yy = geometry(
        *means, *[plane(pool, half, r) for r in range(3, 10)]
    )
    opacity = 1.0 / (1.0 + jnp.exp(-plane(pool, half, 10)))
    log2_e = 1.0 / math.log(2.0)
    slope_x = conic_xx * centre_u + conic_xy * centre_v
    slope_y = conic_xy * centre_u + conic_yy * centre_v
    constant = jnp.log(opacity) - 0.5 * (centre_u * slope_x + centre_v * slope_y)
    constant = log2_e * constant
    if half:
        row = iota((SUB, BLOCK), 0)
        absent = ((row == LOW - SUB) & (region == 0)) | ((row == HIGH - SUB) & (region == regions - 1))
        constant = jnp.where(absent, -1e30, constant)
    terms = [
        constant,
        log2_e * slope_x,
        log2_e * slope_y,
        (-0.5 * log2_e) * conic_xx,
        (-log2_e) * conic_xy,
        (-0.5 * log2_e) * conic_yy,
    ]
    stage[...] = jnp.zeros_like(stage)

    def put(row, value):
        stage[pl.ds(row, SUB, stride=COLS), :] = value

    row = 0
    for term, copies in zip(terms, (1, 1, 1, 2, 2, 2)):
        parts = [part.astype(f32) for part in split(term, 3)]
        for _ in range(copies):
            for part in parts:
                put(row, part)
                row += 1
    basis = harmonics(*means)
    for c in range(3):
        tone = jnp.maximum(raw_colour(pool, half, basis, c), 0.0)
        parts = [part.astype(f32) for part in split(tone, 3)]
        for group, part in enumerate((0, 0, 0, 1, 1, 2)):
            put(32 + group * SUB + c, parts[part])
        put(80 + c, tone)

    def turn(b, carry):
        turned[:, :COLS] = stage[pl.ds(pl.multiple_of(b * COLS, COLS), COLS), :].T
        ordered = jnp.concatenate(
            [turned[pl.ds(t, SUB, stride=STEPS), :] for t in range(STEPS)], axis=0
        )
        table[half * SUB + b] = ordered[:, :COLS].astype(bf16)
        for c in range(3):
            spread[half * SUB + b, c] = jnp.broadcast_to(ordered[:, 80 + c : 81 + c], (BLOCK, BLOCK))
        return carry

    lax.fori_loop(0, count, turn, 0, unroll=2)


def exponents(table, features, block):
    return jnp.dot(table[block, :, :32], features, preferred_element_type=f32)


def two_blocks(p, blocks, live):
    first = own_block(blocks[0, p])
    second = jnp.where(live[0, p] > 1, own_block(blocks[1, p]), DEAD)
    return first, second


def forward_half(
    h, blocks, live, features_ref, table, spread, prefix_ref, segment_ref, pieces, alphas_ref
):
    sub = iota((SUB, WIDE), 0)

    def piece(p, carry):
        features = features_ref[p, :, h * WIDE : (h + 1) * WIDE]
        before = None
        colours = [None] * 3
        for j, block in enumerate(two_blocks(p, blocks, live)):
            exponent = exponents(table, features, block)
            transmit = jnp.ones((SUB, WIDE), f32)
            sums = [jnp.zeros((SUB, WIDE), f32) for _ in range(3)]
            for t in range(STEPS):
                rows = slice(t * SUB, (t + 1) * SUB)
                alpha = jnp.exp2(exponent[rows])
                alphas_ref[h, p, j, rows] = alpha
                weight = alpha * transmit
                transmit = transmit - weight
                for c in range(3):
                    tone = spread[block, c, rows, :]
                    tone = tone if WIDE == BLOCK else jnp.concatenate([tone, tone], axis=1)
                    sums[c] = sums[c] + tone * weight
            run = transmit
            for shift in (1, 2, 4):
                run = run * jnp.where(sub >= shift, roll_rows(run, shift), 1.0)
            prefix = jnp.where(sub >= 1, roll_rows(run, 1), 1.0)
            total = run[SUB - 1 :, :]
            if before is not None:
                prefix = prefix * before
                total = total * before
            before = total
            prefix_ref[h, p, j] = prefix
            for c in range(3):
                piece_sum = prefix * sums[c]
                segment_ref[h, p, j, c] = piece_sum
                colours[c] = piece_sum if j == 0 else colours[c] + piece_sum
        rows = [jnp.sum(colours[c], axis=0, keepdims=True) for c in range(3)] + [1.0 - before]
        for c in range(4):
            for k in range(WIDE // BLOCK):
                place = (c * (WIDE // BLOCK) + k) * PIECES + p
                pieces[pl.ds(place, 1), :] = rows[c][:, k * BLOCK : (k + 1) * BLOCK]
        return carry

    lax.fori_loop(0, PIECES, piece, 0, unroll=UNROLL)


def weigh_half(h, prefix_ref, alphas_ref, weights_ref, ends_ref, weight_parts_ref):
    def piece(p, carry):
        for j in range(2):
            transmit = prefix_ref[h, p, j]
            weights = []
            for t in range(STEPS):
                rows = slice(t * SUB, (t + 1) * SUB)
                weight = alphas_ref[h, p, j, rows] * transmit
                transmit = transmit - weight
                weights_ref[h, p, j, rows] = weight
                weights.append(weight)
            ends_ref[h, p, j] = transmit
            weight_parts_ref[h, p, j * BLOCK : (j + 1) * BLOCK] = jnp.concatenate(
                split(jnp.concatenate(weights, axis=0), 2), axis=1
            )
        return carry

    lax.fori_loop(0, PIECES, piece, 0, unroll=MIDDLE_UNROLL)


def backward_half(
    h, blocks, live, moments_ref, table, segment_ref, alphas_ref, weights_ref, ends_ref, weight_parts_ref,
    cotangent, moved,
):
    sub = iota((SUB, WIDE), 0)
    nothing = jnp.zeros((16, WIDE), bf16)
    none = jnp.zeros((16, WIDE), f32)
    lanes = slice(h * WIDE, (h + 1) * WIDE)

    def piece(p, carry):
        monomials = moments_ref[p, :, lanes]
        cot = jnp.concatenate(
            [
                cotangent[pl.ds(pl.multiple_of((k * PIECES + p) * SUB, SUB), SUB), :]
                for k in range(WIDE // BLOCK)
            ],
            axis=1,
        )
        heads = [part.astype(f32) for part in split(cot, 3)]
        tones = [none, none] + [heads[part] for part in (0, 1, 2, 0, 1, 0)] + [none]
        tones = jnp.concatenate(tones, axis=0).astype(bf16)
        colour_rows = jnp.concatenate([heads[0], heads[1]], axis=0).astype(bf16)
        for_gradient = jnp.concatenate([monomials, nothing], axis=0)
        for_weight = jnp.concatenate([nothing, colour_rows], axis=0)
        state = []
        for j, block in enumerate(two_blocks(p, blocks, live)):
            tone = jnp.dot(table[block], tones, preferred_element_type=f32)
            seen = segment_ref[h, p, j, 0] * cot[0:1]
            for c in (1, 2):
                seen = seen + segment_ref[h, p, j, c] * cot[c : c + 1]
            run = seen
            for shift in (1, 2, 4):
                run = run + jnp.where(sub < SUB - shift, roll_rows(run, -shift), 0.0)
            state.append((tone, run))
        behind = ends_ref[h, p, 1, SUB - 1 :, :] * cot[3:4]
        parts = [None, None]
        for j in (1, 0):
            tone, run = state[j]
            after = jnp.where(sub < SUB - 1, roll_rows(run, -1), 0.0) + behind
            behind = behind + run[0:1]
            ahead = after / ends_ref[h, p, j]
            gradients = [None] * STEPS
            for t in reversed(range(STEPS)):
                rows = slice(t * SUB, (t + 1) * SUB)
                gap = tone[rows] - ahead
                gradients[t] = weights_ref[h, p, j, rows] * gap
                ahead = ahead + alphas_ref[h, p, j, rows] * gap
            parts[j] = jnp.concatenate(split(jnp.concatenate(gradients, axis=0), 2), axis=1)
        both = [jnp.concatenate(parts, axis=0), weight_parts_ref[h, p]]
        total = None
        for k in range(2):
            rows = (for_gradient, for_weight)[k]
            term = lax.dot_general(
                jnp.concatenate([rows, rows], axis=1),
                both[k],
                (((1,), (1,)), ((), ())),
                preferred_element_type=f32,
            )
            total = term if total is None else total + term
        for j in range(2):
            rows = pl.ds(pl.multiple_of((j * PIECES + p) * 32, 32), 32)
            part = total[:, j * BLOCK : (j + 1) * BLOCK]
            moved[rows, :] = part if h == 0 else moved[rows, :] + part
        return carry

    lax.fori_loop(0, PIECES, piece, 0, unroll=UNROLL)


def gather_moments(first_row, second_row, moved, summed):
    numbers = iota((2 * SUB, PIECES), 0).astype(f32)
    lane = iota((BLOCK, BLOCK), 0)
    unshuffle = (lane % SUB) * STEPS + lane // SUB == iota((BLOCK, BLOCK), 1)
    unshuffle = jnp.where(unshuffle, 1.0, 0.0).astype(bf16)
    for group in range(3):
        features = range(group * SUB, group * SUB + SUB)
        features = [f for f in features if f < 9] + [16 + f - 9 for f in features if 9 <= f < 12]
        features += [24 + f - 12 for f in range(group * SUB, group * SUB + SUB) if 12 <= f < 15]
        if not features:
            continue
        total = None
        for j, row in enumerate((first_row, second_row)):
            pick = jnp.where(jnp.broadcast_to(row, (2 * SUB, PIECES)) == numbers, 1.0, 0.0)
            values = [
                moved[pl.ds(j * PIECES * 32 + f, PIECES, stride=32), :] for f in features
            ]
            term = exact_pick(pick, jnp.concatenate(values, axis=1))
            total = term if total is None else total + term
        stacked = jnp.concatenate(
            [total[:, k * BLOCK : (k + 1) * BLOCK] for k in range(len(features))], axis=0
        )
        ordered = None
        for part in reversed(split(stacked, 3)):
            term = jnp.dot(part, unshuffle, preferred_element_type=f32)
            ordered = term if ordered is None else ordered + term
        for k, f in enumerate(features):
            summed[f] = ordered[k * 2 * SUB : (k + 1) * 2 * SUB]


def pull_splat(half, pool, summed, grads_ref):
    means = [plane(pool, half, r) for r in range(3)]
    (centre_u, centre_v, conic_xx, conic_xy, conic_yy), geometry_pull = jax.vjp(
        geometry, *means, *[plane(pool, half, r) for r in range(3, 10)]
    )
    basis, harmonics_pull = jax.vjp(harmonics, *means)
    opacity = 1.0 / (1.0 + jnp.exp(-plane(pool, half, 10)))
    sums = [summed[f, half * SUB : (half + 1) * SUB] for f in range(9)]
    total, sum_x, sum_y = sums[:3]
    sum_xx, sum_xy, sum_yy = sums[3] + sums[4], sums[5] + sums[6], sums[7] + sums[8]
    off_x = sum_x - centre_u * total
    off_y = sum_y - centre_v * total
    grad_xx = -0.5 * (sum_xx - centre_u * (sum_x + off_x))
    grad_xy = -(sum_xy - centre_u * sum_y - centre_v * off_x)
    grad_yy = -0.5 * (sum_yy - centre_v * (sum_y + off_y))
    grad_u = conic_xx * off_x + conic_xy * off_y
    grad_v = conic_xy * off_x + conic_yy * off_y
    grads = geometry_pull((grad_u, grad_v, grad_xx, grad_xy, grad_yy))
    tone_grads = []
    for c in range(3):
        grad = summed[16 + c, half * SUB : (half + 1) * SUB] + summed[24 + c, half * SUB : (half + 1) * SUB]
        raw = raw_colour(pool, half, basis, c)
        tone_grads.append(jnp.where(raw > 0, grad, jnp.where(raw == 0, 0.5 * grad, 0.0)))
    basis_grads = []
    for k in range(1, 16):
        basis_grads.append(
            sum(tone_grads[c] * plane(pool, half, 11 + 16 * c + k) for c in range(3))
        )
    mean_grads = harmonics_pull(tuple(basis_grads))
    for r in range(10):
        put_plane(grads_ref, half, r, grads[r] + mean_grads[r] if r < 3 else grads[r])
    put_plane(grads_ref, half, 10, total * (1.0 - opacity))
    for c in range(3):
        put_plane(grads_ref, half, 11 + 16 * c, tone_grads[c] * harmonic_zero)
        for k in range(1, 16):
            put_plane(grads_ref, half, 11 + 16 * c + k, tone_grads[c] * basis[k - 1])


PARTS = 4 * WIDE // BLOCK
MESSAGE = SLOTS * PARTS


def put_slots(ref, values):
    for k in range(SLOTS):
        for r in range(PARTS):
            ref[pl.ds(k * PARTS + r, 32, stride=MESSAGE), :] = values[
                k * 32 : (k + 1) * 32, r * BLOCK : (r + 1) * BLOCK
            ]


def get_slots(ref):
    return jnp.concatenate(
        [
            jnp.concatenate(
                [ref[pl.ds(k * PARTS + r, 32, stride=MESSAGE), :] for r in range(PARTS)], axis=1
            )
            for k in range(SLOTS)
        ],
        axis=0,
    )


def route(owner_row, cell_row, me):
    owner_col = to_column(owner_row)
    far_row = owner_row - me.astype(f32)
    far_row = jnp.where(far_row < 0, far_row + float(PIECES), far_row)
    far_col = to_column(far_row)
    square = (PIECES, PIECES)
    same = jnp.broadcast_to(owner_row, square) == jnp.broadcast_to(owner_col, square)
    first, second = iota(square, 0), iota(square, 1)
    rank_row = jnp.sum(jnp.where(same & (first < second), 1.0, 0.0), axis=0, keepdims=True)
    rank_col = jnp.sum(jnp.where(same & (second < first), 1.0, 0.0), axis=1, keepdims=True)
    slots = SLOTS * 32
    pack = jnp.broadcast_to(rank_row * 32.0 + far_row, (slots, PIECES)) == iota((slots, PIECES), 0).astype(f32)
    pack = jnp.where(pack, 1.0, 0.0)
    unpack = jnp.broadcast_to(rank_col * 32.0 + far_col, (PIECES, slots)) == iota((PIECES, slots), 1).astype(f32)
    unpack = jnp.where(unpack, 1.0, 0.0)
    label_col = jnp.sum(pack * (cell_row + 1.0), axis=1, keepdims=True) - 1.0
    lane = iota((32, BLOCK), 1)
    label_rows = jnp.where(lane == 0, label_col[:32], jnp.where(lane == 1, label_col[32:], -1.0))
    return pack, unpack, label_rows


def composite(h, grid, target, background):
    def at(depth, channel):
        return grid[depth * SUB : (depth + 1) * SUB, channel * WIDE : (channel + 1) * WIDE]

    in_front = jnp.ones((TILE_DEV, WIDE), f32)
    seen = [jnp.zeros((TILE_DEV, WIDE), f32) for _ in range(3)]
    fronts = []
    for depth in range(MAXD):
        fronts.append(in_front)
        seen = [seen[c] + in_front * at(depth, c) for c in range(3)]
        in_front = in_front * (1.0 - at(depth, 3))
    residual = [
        seen[c] + in_front * background[c] - target[c, :, h * WIDE : (h + 1) * WIDE] for c in range(3)
    ]
    behind = [jnp.full((TILE_DEV, WIDE), background[c], f32) for c in range(3)]
    rows = [None] * MAXD
    for depth in reversed(range(MAXD)):
        through = 1.0 - at(depth, 3)
        by_trans = residual[0] * behind[0] + residual[1] * behind[1] + residual[2] * behind[2]
        rows[depth] = jnp.concatenate(
            [fronts[depth] * residual[c] for c in range(3)] + [fronts[depth] * by_trans], axis=1
        )
        behind = [at(depth, c) + through * behind[c] for c in range(3)]
    return jnp.concatenate(rows, axis=0)


def step_kernel(
    params_hbm,
    blocks_hbm,
    live_hbm,
    owner_hbm,
    cell_hbm,
    target_hbm,
    background_hbm,
    features_hbm,
    moments_hbm,
    grads_ref,
    blocks,
    live,
    background,
    block_rows,
    owner,
    cell,
    target,
    features,
    moments,
    pool,
    stage,
    turned,
    table,
    spread,
    prefix,
    segment,
    alphas,
    weights,
    ends,
    weight_parts,
    pieces,
    sent,
    got,
    replies,
    answers,
    labels,
    got_labels,
    cotangent,
    moved,
    summed,
    local_sem,
    halo_send,
    halo_recv,
    edge_send,
    edge_recv,
    label_send,
    label_recv,
    send_sem,
    recv_sem,
    reply_send,
    reply_recv,
):
    regions, region = lax.axis_size("region"), lax.axis_index("region")
    count, me = lax.axis_size("dom"), lax.axis_index("dom")
    upper, lower = lax.rem(region + 1, regions), lax.rem(region + regions - 1, regions)

    def block_rows_of(ref, b):
        return ref.at[pl.ds(b * ROWS, PARAMS)]

    fetches = []

    def fetch(src, dst):
        copy = pltpu.make_async_copy(src, dst, local_sem.at[len(fetches)])
        copy.start()
        fetches.append(copy)
        return copy

    routing = [fetch(owner_hbm, owner), fetch(cell_hbm, cell)]
    own = [
        fetch(params_hbm.at[:, pl.ds(b * BLOCK, BLOCK)], block_rows_of(pool, b)) for b in range(BLOCKS)
    ]
    scalars = [fetch(blocks_hbm, blocks), fetch(live_hbm, live), fetch(features_hbm, features)]
    later = [
        fetch(blocks_hbm, block_rows),
        fetch(target_hbm, target),
        fetch(background_hbm, background),
        fetch(moments_hbm, moments),
    ]

    barrier = pltpu.get_barrier_semaphore()

    def signal(**where):
        pl.semaphore_signal(barrier, inc=1, device_id=where, device_id_type=MESH)

    def greet(d, carry):
        signal(dom=lax.rem(me + d, count))
        return carry

    signal(region=upper)
    signal(region=lower)
    lax.fori_loop(1, count, greet, 0)

    for copy in routing:
        copy.wait()
    pack, unpack, label_rows = route(owner[...].astype(f32), cell[...].astype(f32), me)
    for d in range(32):
        labels[d] = label_rows[d : d + 1]
    pl.semaphore_wait(barrier, count + 1)

    def remote(src, dst, send, recv, **where):
        return pltpu.make_async_remote_copy(
            src_ref=src, dst_ref=dst, send_sem=send, recv_sem=recv, device_id=where, device_id_type=MESH
        )

    def label(d, many=1):
        rows = pl.ds(d, many)
        return remote(
            labels.at[rows], got_labels.at[rows], label_send, label_recv, dom=lax.rem(me + d, count)
        )

    def message(d, many):
        return pl.ds(pl.multiple_of(d * MESSAGE, MESSAGE), many * MESSAGE)

    def payload(h, d, many=1):
        rows = message(d, many)
        return remote(
            sent.at[h, rows], got.at[h, rows], send_sem.at[h], recv_sem.at[h], dom=lax.rem(me + d, count)
        )

    def reply(h, d, many=1):
        rows = message(d, many)
        return remote(
            replies.at[h, rows],
            answers.at[h, rows],
            reply_send.at[h],
            reply_recv.at[h],
            dom=lax.rem(me + count - d, count),
        )

    def start_all(copy):
        def one(d, carry):
            copy(count - d).start()
            return carry

        lax.fori_loop(1, count, one, 0, unroll=START_UNROLL)

    others = count - 1

    halo = [
        remote(
            params_hbm.at[:, pl.ds((BLOCKS - 1) * BLOCK, BLOCK)],
            block_rows_of(pool, LOW),
            halo_send.at[0],
            halo_recv.at[0],
            region=upper,
        ),
        remote(
            params_hbm.at[:, pl.ds(0, BLOCK)],
            block_rows_of(pool, HIGH),
            halo_send.at[1],
            halo_recv.at[1],
            region=lower,
        ),
    ]
    for copy in halo:
        copy.start()

    for copy in own:
        copy.wait()
    for b in range(POOL, 2 * SUB):
        pool[b * ROWS : b * ROWS + PARAMS, :] = pool[0:PARAMS, :]
    tabulate(0, SUB, pool, stage, turned, table, spread)
    start_all(label)
    got_labels[0] = labels[0]
    for copy in halo:
        copy.wait_recv()
    tabulate(1, POOL - SUB, pool, stage, turned, table, spread)
    lane = iota((BLOCK, COLS), 1)
    table[DEAD] = jnp.where(lane == 0, -1e30, 0.0).astype(bf16)
    spread[DEAD] = jnp.zeros((3, BLOCK, BLOCK), f32)

    for copy in scalars:
        copy.wait()
    for h in range(HALVES):
        forward_half(h, blocks, live, features, table, spread, prefix, segment, pieces, alphas)
        rendered = [pieces[r * PIECES : (r + 1) * PIECES, :] for r in range(PARTS)]
        rendered = jnp.concatenate(rendered, axis=1)
        put_slots(sent.at[h], exact_pick(pack, rendered))
        start_all(functools.partial(payload, h))
        got[h, :MESSAGE] = sent[h, :MESSAGE]

    weigh_half(0, prefix, alphas, weights, ends, weight_parts)
    for copy in later:
        copy.wait()
    label(1, others).wait()
    arrived = jnp.concatenate([got_labels[d] for d in range(32)], axis=0)
    arrived_col = jnp.concatenate([arrived[:, 0:1], arrived[:, 1:2]], axis=0)
    arrived_row = to_row(arrived_col)
    slots = SLOTS * 32

    def cell_of(place):
        return ((place % TILE_DEV) * MAXD + place // TILE_DEV).astype(f32)

    gather = jnp.broadcast_to(arrived_row, (CELLS, slots)) == cell_of(iota((CELLS, slots), 0))
    gather = jnp.where(gather, 1.0, 0.0)
    scatter = jnp.broadcast_to(arrived_col, (slots, CELLS)) == cell_of(iota((slots, CELLS), 1))
    scatter = jnp.where(scatter, 1.0, 0.0)
    colours = [background[c] for c in range(3)]
    for h in range(HALVES):
        payload(h, 1, others).wait()
        grid = exact_pick(gather, get_slots(got.at[h]))
        put_slots(replies.at[h], exact_pick(scatter, composite(h, grid, target, colours)))
        start_all(functools.partial(reply, h))
        answers[h, :MESSAGE] = replies[h, :MESSAGE]
        if h + 1 < HALVES:
            weigh_half(h + 1, prefix, alphas, weights, ends, weight_parts)

    for h in range(HALVES):
        reply(h, 1, others).wait()
        back = exact_pick(unpack, get_slots(answers.at[h]))
        for k in range(WIDE // BLOCK):
            for c in range(SUB):
                lanes = slice(c * WIDE + k * BLOCK, c * WIDE + (k + 1) * BLOCK)
                rows = back[:, lanes] if c < 4 else jnp.zeros((PIECES, BLOCK), f32)
                cotangent[pl.ds(k * PIECES * SUB + c, PIECES, stride=SUB), :] = rows
        backward_half(
            h, blocks, live, moments, table, segment, alphas, weights, ends, weight_parts, cotangent, moved
        )

    rows = own_block(block_rows[...]).astype(f32)
    gather_moments(rows[0:1], rows[1:2], moved, summed)
    pull_splat(1, pool, summed, grads_ref)
    edges = [
        remote(block_rows_of(grads_ref, HIGH), block_rows_of(grads_ref, FROM_LEFT), edge_send.at[0], edge_recv.at[0], region=upper),
        remote(block_rows_of(grads_ref, LOW), block_rows_of(grads_ref, FROM_RIGHT), edge_send.at[1], edge_recv.at[1], region=lower),
    ]
    for copy in edges:
        copy.start()
    pull_splat(0, pool, summed, grads_ref)
    for copy in halo:
        copy.wait_send()
    for copy in edges:
        copy.wait()


def whole(memory=pltpu.VMEM):
    return pl.BlockSpec(memory_space=memory)


def step(*operands):
    shape = jax.ShapeDtypeStruct
    vmem, smem, dma = pltpu.VMEM, pltpu.SMEM, pltpu.SemaphoreType.DMA
    slots = vmem((HALVES, 32 * MESSAGE, BLOCK), f32)
    label = vmem((32, 1, BLOCK), f32)
    return pl.pallas_call(
        step_kernel,
        out_shape=shape(((FROM_RIGHT + 1) * ROWS, BLOCK), f32),
        in_specs=[whole(pltpu.HBM)] * 9,
        out_specs=whole(),
        scratch_shapes=[
            smem((2, PIECES), jnp.int32),
            smem((1, PIECES), jnp.int32),
            smem((3,), f32),
            vmem((2, PIECES), jnp.int32),
            vmem((1, PIECES), jnp.int32),
            vmem((1, PIECES), jnp.int32),
            vmem((3, TILE_DEV, PIX), f32),
            vmem((PIECES, 32, PIX), bf16),
            vmem((PIECES, 16, PIX), bf16),
            vmem((2 * SUB * ROWS, BLOCK), f32),
            vmem((SUB * COLS, BLOCK), f32),
            vmem((BLOCK, BLOCK), f32),
            vmem((TAB, BLOCK, COLS), bf16),
            vmem((TAB, 3, BLOCK, BLOCK), f32),
            vmem((HALVES, PIECES, 2, SUB, WIDE), f32),
            vmem((HALVES, PIECES, 2, 3, SUB, WIDE), f32),
            vmem((HALVES, PIECES, 2, BLOCK, WIDE), f32),
            vmem((HALVES, PIECES, 2, BLOCK, WIDE), f32),
            vmem((HALVES, PIECES, 2, SUB, WIDE), f32),
            vmem((HALVES, PIECES, 2 * BLOCK, 2 * WIDE), bf16),
            vmem((4 * WIDE // BLOCK * PIECES, BLOCK), f32),
            slots,
            slots,
            slots,
            slots,
            label,
            label,
            vmem((WIDE // BLOCK * PIECES * SUB, BLOCK), f32),
            vmem((2 * PIECES * 32, BLOCK), f32),
            vmem((32, 2 * SUB, BLOCK), f32),
            dma((17,)),
            dma((2,)),
            dma((2,)),
            dma((2,)),
            dma((2,)),
            dma,
            dma,
            dma((HALVES,)),
            dma((HALVES,)),
            dma((HALVES,)),
            dma((HALVES,)),
        ],
        compiler_params=pltpu.CompilerParams(
            collective_id=0, has_side_effects=True, vmem_limit_bytes=VMEM_LIMIT
        ),
        name="render_step",
    )(*operands)


def adam_kernel(
    grads_ref, params_ref, first_ref, second_ref,
    gradient_ref, new_params_ref, new_first_ref, new_second_ref,
):
    for b in range(BLOCKS):
        cols = slice(b * BLOCK, (b + 1) * BLOCK)
        gradient = grads_ref[b * ROWS : b * ROWS + PARAMS, :]
        if b == 0:
            gradient = gradient + grads_ref[FROM_LEFT * ROWS : FROM_LEFT * ROWS + PARAMS, :]
        if b == BLOCKS - 1:
            gradient = gradient + grads_ref[FROM_RIGHT * ROWS : FROM_RIGHT * ROWS + PARAMS, :]
        new_first = beta_one * first_ref[:, cols] + (1 - beta_one) * gradient
        new_second = beta_two * second_ref[:, cols] + (1 - beta_two) * gradient * gradient
        update = (
            new_first
            / (1 - beta_one**adam_step)
            / (jnp.sqrt(new_second / (1 - beta_two**adam_step)) + tiny)
        )
        gradient_ref[:, cols] = gradient
        new_params_ref[:, cols] = params_ref[:, cols] - rate * update
        new_first_ref[:, cols] = new_first
        new_second_ref[:, cols] = new_second


def adam(*operands):
    return pl.pallas_call(
        adam_kernel,
        out_shape=(jax.ShapeDtypeStruct((PARAMS, BLOCKS * BLOCK), f32),) * 4,
        in_specs=[whole()] * 4,
        out_specs=(whole(),) * 4,
        compiler_params=pltpu.CompilerParams(vmem_limit_bytes=8 * 1024 * 1024),
        name="adam",
    )(*operands)


def on_device(
    params,
    first_moment,
    second_moment,
    piece_blocks,
    piece_live,
    piece_owner,
    piece_cell,
    target,
    background,
):
    grads = step(
        params,
        piece_blocks[0].T,
        piece_live,
        piece_owner,
        piece_cell,
        jnp.transpose(target[0], (1, 0, 2)),
        background,
        jnp.asarray(exponent_features()),
        jnp.asarray(moment_features()),
    )
    return adam(grads, params, first_moment, second_moment)


def solution(mesh):
    in_specs = (
        P(None, ("region", "dom")),
        P(None, ("region", "dom")),
        P(None, ("region", "dom")),
        P(("region", "dom"), None, None),
        P(("region", "dom"), None),
        P(("region", "dom"), None),
        P(("region", "dom"), None),
        P(("region", "dom"), None, None, None),
        P(),
    )
    out_specs = (
        P(None, ("region", "dom")),
        P(None, ("region", "dom")),
        P(None, ("region", "dom")),
        P(None, ("region", "dom")),
    )
    return jax.shard_map(
        on_device, mesh=mesh, in_specs=in_specs, out_specs=out_specs, check_vma=False
    )
```

```python
import functools
import math

import jax
import jax.numpy as jnp
import ml_dtypes
import numpy as np
from jax import lax
from jax.experimental import pallas as pl
from jax.experimental.pallas import tpu as pltpu
from jax.sharding import PartitionSpec as P

PARAMS = 59
TSIDE = 16
WIN = 8
BLOCK = 128
BLOCKS = 8
MAXD = 8
PIECES = 32
PIX = 256
TILE_DEV = 8
CELLS = 64
POOL = 10
SLOTS = 2
SUB = 8
STEPS = BLOCK // SUB
TAB = POOL + 1
PLANES = 16
ROWS = 64
COLS = 96
UNROLL = 16
MIDDLE_UNROLL = 4
START_UNROLL = 1
HALVES = 2
WIDE = PIX // HALVES
LOW = BLOCKS
HIGH = BLOCKS + 1
DEAD = POOL
FROM_LEFT = 2 * SUB
FROM_RIGHT = FROM_LEFT + 1
ORIGIN_X = 64.0
ORIGIN_Y = 32.0

harmonic_zero = 0.28209479177387814
harmonic_one = 0.4886025119029199
harmonic_two = (
    1.0925484305920792,
    -1.0925484305920792,
    0.31539156525252005,
    -1.0925484305920792,
    0.5462742152960396,
)
harmonic_three = (
    -0.5900435899266435,
    2.890611442640554,
    -0.4570457994644658,
    0.3731763325901154,
    -0.4570457994644658,
    1.445305721320277,
    -0.5900435899266435,
)
beta_one = 0.9
beta_two = 0.999
rate = 0.001
adam_step = 100
tiny = 1e-08

f32 = jnp.float32
bf16 = jnp.bfloat16
MESH = pl.DeviceIdType.MESH
VMEM_LIMIT = 60 * 1024 * 1024


def pixel_monomials():
    bf = ml_dtypes.bfloat16
    tile = np.arange(PIECES)[:, None]
    pixel = np.arange(PIX)[None, :]
    x = (TSIDE * (tile % WIN) + pixel % TSIDE + 0.5 - ORIGIN_X).astype(np.float32)
    y = (TSIDE * (tile // WIN) + pixel // TSIDE + 0.5 - ORIGIN_Y).astype(np.float32)

    def two(value):
        head = value.astype(bf).astype(np.float32)
        return [head, value - head]

    return [np.ones_like(x), x, y] + two(x * x) + two(x * y) + two(y * y)


def exponent_features():
    rows = [row for row in pixel_monomials() for _ in range(3)]
    rows += [np.zeros_like(rows[0])] * (32 - len(rows))
    return np.stack(rows, axis=1).astype(ml_dtypes.bfloat16)


def moment_features():
    rows = pixel_monomials()
    rows += [np.zeros_like(rows[0])] * (16 - len(rows))
    return np.stack(rows, axis=1).astype(ml_dtypes.bfloat16)


def split(value, parts):
    out = []
    rest = value
    for part in range(parts):
        head = rest.astype(bf16)
        out.append(head)
        if part < parts - 1:
            rest = rest - head.astype(f32)
    return out


def exact_pick(onehot, value):
    picks = onehot.astype(bf16)
    total = None
    for part in reversed(split(value, 3)):
        term = jnp.dot(picks, part, preferred_element_type=f32)
        total = term if total is None else total + term
    return total


def iota(shape, dim):
    return lax.broadcasted_iota(jnp.int32, shape, dim)


def to_column(row):
    n = row.shape[1]
    spread = jnp.broadcast_to(row, (n, n))
    return jnp.sum(jnp.where(iota((n, n), 0) == iota((n, n), 1), spread, 0.0), axis=1, keepdims=True)


def to_row(column):
    n = column.shape[0]
    spread = jnp.broadcast_to(column, (n, n))
    return jnp.sum(jnp.where(iota((n, n), 0) == iota((n, n), 1), spread, 0.0), axis=0, keepdims=True)


def geometry(mean_x, mean_y, mean_z, log_a, log_b, log_c, quat_w, quat_x, quat_y, quat_z):
    screen_px = float(WIN * TSIDE)
    scales = (jnp.exp(log_a), jnp.exp(log_b), jnp.exp(log_c))
    norm = 1.0 / jnp.sqrt(quat_w * quat_w + quat_x * quat_x + quat_y * quat_y + quat_z * quat_z)
    quat_w, quat_x, quat_y, quat_z = quat_w * norm, quat_x * norm, quat_y * norm, quat_z * norm
    rotation = [
        [
            1 - 2 * (quat_y * quat_y + quat_z * quat_z),
            2 * (quat_x * quat_y - quat_w * quat_z),
            2 * (quat_x * quat_z + quat_w * quat_y),
        ],
        [
            2 * (quat_x * quat_y + quat_w * quat_z),
            1 - 2 * (quat_x * quat_x + quat_z * quat_z),
            2 * (quat_y * quat_z - quat_w * quat_x),
        ],
        [
            2 * (quat_x * quat_z - quat_w * quat_y),
            2 * (quat_y * quat_z + quat_w * quat_x),
            1 - 2 * (quat_x * quat_x + quat_y * quat_y),
        ],
    ]
    focal_px = 0.3125 * screen_px
    inv_z = 1.0 / mean_z
    ratio_x, ratio_y = mean_x * inv_z, mean_y * inv_z
    focal_z = focal_px * inv_z
    rows = []
    for ratio, axis in ((ratio_x, 0), (ratio_y, 1)):
        rows.append(
            [
                focal_z * (rotation[axis][col] - ratio * rotation[2][col]) * scales[col]
                for col in range(3)
            ]
        )
    sigma_xx = rows[0][0] * rows[0][0] + rows[0][1] * rows[0][1] + rows[0][2] * rows[0][2] + 0.3
    sigma_xy = rows[0][0] * rows[1][0] + rows[0][1] * rows[1][1] + rows[0][2] * rows[1][2]
    sigma_yy = rows[1][0] * rows[1][0] + rows[1][1] * rows[1][1] + rows[1][2] * rows[1][2] + 0.3
    inv_det = 1.0 / (sigma_xx * sigma_yy - sigma_xy * sigma_xy)
    return (
        focal_px * ratio_x + (0.5 * screen_px - ORIGIN_X),
        focal_px * ratio_y + (0.5 * screen_px - ORIGIN_Y),
        sigma_yy * inv_det,
        -sigma_xy * inv_det,
        sigma_xx * inv_det,
    )


def harmonics(mean_x, mean_y, mean_z):
    inv_length = 1.0 / jnp.sqrt(mean_x * mean_x + mean_y * mean_y + mean_z * mean_z)
    dir_x, dir_y, dir_z = mean_x * inv_length, mean_y * inv_length, mean_z * inv_length
    sq_x, sq_y, sq_z = dir_x * dir_x, dir_y * dir_y, dir_z * dir_z
    return (
        -harmonic_one * dir_y,
        harmonic_one * dir_z,
        -harmonic_one * dir_x,
        harmonic_two[0] * dir_x * dir_y,
        harmonic_two[1] * dir_y * dir_z,
        harmonic_two[2] * (2 * sq_z - sq_x - sq_y),
        harmonic_two[3] * dir_x * dir_z,
        harmonic_two[4] * (sq_x - sq_y),
        harmonic_three[0] * dir_y * (3 * sq_x - sq_y),
        harmonic_three[1] * dir_x * dir_y * dir_z,
        harmonic_three[2] * dir_y * (4 * sq_z - sq_x - sq_y),
        harmonic_three[3] * dir_z * (2 * sq_z - 3 * sq_x - 3 * sq_y),
        harmonic_three[4] * dir_x * (4 * sq_z - sq_x - sq_y),
        harmonic_three[5] * dir_z * (sq_x - sq_y),
        harmonic_three[6] * dir_x * (sq_x - 3 * sq_y),
    )


def plane(ref, half, row):
    return ref[pl.ds(half * SUB * ROWS + row, SUB, stride=ROWS), :]


def put_plane(ref, half, row, value):
    ref[pl.ds(half * SUB * ROWS + row, SUB, stride=ROWS), :] = value


def raw_colour(pool, half, basis, colour):
    total = harmonic_zero * plane(pool, half, 11 + 16 * colour) + 0.5
    for k in range(1, 16):
        total = total + plane(pool, half, 11 + 16 * colour + k) * basis[k - 1]
    return total


def own_block(number):
    return jnp.where(number == 0, LOW, jnp.where(number == POOL - 1, HIGH, number - 1))


def roll_rows(value, shift):
    return pltpu.roll(value, shift % SUB, axis=0)


def tabulate(half, count, pool, stage, turned, table, spread):
    region = lax.axis_index("region")
    regions = lax.axis_size("region")
    means = [plane(pool, half, r) for r in range(3)]
    centre_u, centre_v, conic_xx, conic_xy, conic_yy = geometry(
        *means, *[plane(pool, half, r) for r in range(3, 10)]
    )
    opacity = 1.0 / (1.0 + jnp.exp(-plane(pool, half, 10)))
    log2_e = 1.0 / math.log(2.0)
    slope_x = conic_xx * centre_u + conic_xy * centre_v
    slope_y = conic_xy * centre_u + conic_yy * centre_v
    constant = jnp.log(opacity) - 0.5 * (centre_u * slope_x + centre_v * slope_y)
    constant = log2_e * constant
    if half:
        row = iota((SUB, BLOCK), 0)
        absent = ((row == LOW - SUB) & (region == 0)) | ((row == HIGH - SUB) & (region == regions - 1))
        constant = jnp.where(absent, -1e30, constant)
    terms = [
        constant,
        log2_e * slope_x,
        log2_e * slope_y,
        (-0.5 * log2_e) * conic_xx,
        (-log2_e) * conic_xy,
        (-0.5 * log2_e) * conic_yy,
    ]
    stage[...] = jnp.zeros_like(stage)

    def put(row, value):
        stage[pl.ds(row, SUB, stride=COLS), :] = value

    row = 0
    for term, copies in zip(terms, (1, 1, 1, 2, 2, 2)):
        parts = [part.astype(f32) for part in split(term, 3)]
        for _ in range(copies):
            for part in parts:
                put(row, part)
                row += 1
    basis = harmonics(*means)
    for c in range(3):
        tone = jnp.maximum(raw_colour(pool, half, basis, c), 0.0)
        parts = [part.astype(f32) for part in split(tone, 3)]
        for group, part in enumerate((0, 0, 0, 1, 1, 2)):
            put(32 + group * SUB + c, parts[part])
        put(80 + c, tone)

    def turn(b, carry):
        turned[:, :COLS] = stage[pl.ds(pl.multiple_of(b * COLS, COLS), COLS), :].T
        ordered = jnp.concatenate(
            [turned[pl.ds(t, SUB, stride=STEPS), :] for t in range(STEPS)], axis=0
        )
        table[half * SUB + b] = ordered[:, :COLS].astype(bf16)
        for c in range(3):
            spread[half * SUB + b, c] = jnp.broadcast_to(ordered[:, 80 + c : 81 + c], (BLOCK, BLOCK))
        return carry

    lax.fori_loop(0, count, turn, 0, unroll=2)


def exponents(table, features, block):
    return jnp.dot(table[block, :, :32], features, preferred_element_type=f32)


def two_blocks(p, blocks, live):
    first = own_block(blocks[0, p])
    second = jnp.where(live[0, p] > 1, own_block(blocks[1, p]), DEAD)
    return first, second


def forward_half(
    h, blocks, live, features_ref, table, spread, prefix_ref, segment_ref, pieces, alphas_ref
):
    sub = iota((SUB, WIDE), 0)

    def piece(p, carry):
        features = features_ref[p, :, h * WIDE : (h + 1) * WIDE]
        before = None
        colours = [None] * 3
        for j, block in enumerate(two_blocks(p, blocks, live)):
            exponent = exponents(table, features, block)
            transmit = jnp.ones((SUB, WIDE), f32)
            sums = [jnp.zeros((SUB, WIDE), f32) for _ in range(3)]
            for t in range(STEPS):
                rows = slice(t * SUB, (t + 1) * SUB)
                alpha = jnp.exp2(exponent[rows])
                alphas_ref[h, p, j, rows] = alpha
                weight = alpha * transmit
                transmit = transmit - weight
                for c in range(3):
                    tone = spread[block, c, rows, :]
                    tone = tone if WIDE == BLOCK else jnp.concatenate([tone, tone], axis=1)
                    sums[c] = sums[c] + tone * weight
            run = transmit
            for shift in (1, 2, 4):
                run = run * jnp.where(sub >= shift, roll_rows(run, shift), 1.0)
            prefix = jnp.where(sub >= 1, roll_rows(run, 1), 1.0)
            total = run[SUB - 1 :, :]
            if before is not None:
                prefix = prefix * before
                total = total * before
            before = total
            prefix_ref[h, p, j] = prefix
            for c in range(3):
                piece_sum = prefix * sums[c]
                segment_ref[h, p, j, c] = piece_sum
                colours[c] = piece_sum if j == 0 else colours[c] + piece_sum
        rows = [jnp.sum(colours[c], axis=0, keepdims=True) for c in range(3)] + [1.0 - before]
        for c in range(4):
            for k in range(WIDE // BLOCK):
                place = (c * (WIDE // BLOCK) + k) * PIECES + p
                pieces[pl.ds(place, 1), :] = rows[c][:, k * BLOCK : (k + 1) * BLOCK]
        return carry

    lax.fori_loop(0, PIECES, piece, 0, unroll=UNROLL)


def weigh_half(h, prefix_ref, alphas_ref, weights_ref, ends_ref, weight_parts_ref):
    def piece(p, carry):
        for j in range(2):
            transmit = prefix_ref[h, p, j]
            weights = []
            for t in range(STEPS):
                rows = slice(t * SUB, (t + 1) * SUB)
                weight = alphas_ref[h, p, j, rows] * transmit
                transmit = transmit - weight
                weights_ref[h, p, j, rows] = weight
                weights.append(weight)
            ends_ref[h, p, j] = transmit
            weight_parts_ref[h, p, j * BLOCK : (j + 1) * BLOCK] = jnp.concatenate(
                split(jnp.concatenate(weights, axis=0), 2), axis=1
            )
        return carry

    lax.fori_loop(0, PIECES, piece, 0, unroll=MIDDLE_UNROLL)


def backward_half(
    h, blocks, live, moments_ref, table, segment_ref, alphas_ref, weights_ref, ends_ref, weight_parts_ref,
    cotangent, moved,
):
    sub = iota((SUB, WIDE), 0)
    nothing = jnp.zeros((16, WIDE), bf16)
    none = jnp.zeros((16, WIDE), f32)
    lanes = slice(h * WIDE, (h + 1) * WIDE)

    def piece(p, carry):
        monomials = moments_ref[p, :, lanes]
        cot = jnp.concatenate(
            [
                cotangent[pl.ds(pl.multiple_of((k * PIECES + p) * SUB, SUB), SUB), :]
                for k in range(WIDE // BLOCK)
            ],
            axis=1,
        )
        heads = [part.astype(f32) for part in split(cot, 3)]
        tones = [none, none] + [heads[part] for part in (0, 1, 2, 0, 1, 0)] + [none]
        tones = jnp.concatenate(tones, axis=0).astype(bf16)
        colour_rows = jnp.concatenate([heads[0], heads[1]], axis=0).astype(bf16)
        for_gradient = jnp.concatenate([monomials, nothing], axis=0)
        for_weight = jnp.concatenate([nothing, colour_rows], axis=0)
        state = []
        for j, block in enumerate(two_blocks(p, blocks, live)):
            tone = jnp.dot(table[block], tones, preferred_element_type=f32)
            seen = segment_ref[h, p, j, 0] * cot[0:1]
            for c in (1, 2):
                seen = seen + segment_ref[h, p, j, c] * cot[c : c + 1]
            run = seen
            for shift in (1, 2, 4):
                run = run + jnp.where(sub < SUB - shift, roll_rows(run, -shift), 0.0)
            state.append((tone, run))
        behind = ends_ref[h, p, 1, SUB - 1 :, :] * cot[3:4]
        parts = [None, None]
        for j in (1, 0):
            tone, run = state[j]
            after = jnp.where(sub < SUB - 1, roll_rows(run, -1), 0.0) + behind
            behind = behind + run[0:1]
            ahead = after / ends_ref[h, p, j]
            gradients = [None] * STEPS
            for t in reversed(range(STEPS)):
                rows = slice(t * SUB, (t + 1) * SUB)
                gap = tone[rows] - ahead
                gradients[t] = weights_ref[h, p, j, rows] * gap
                ahead = ahead + alphas_ref[h, p, j, rows] * gap
            parts[j] = jnp.concatenate(split(jnp.concatenate(gradients, axis=0), 2), axis=1)
        both = [jnp.concatenate(parts, axis=0), weight_parts_ref[h, p]]
        total = None
        for k in range(2):
            rows = (for_gradient, for_weight)[k]
            term = lax.dot_general(
                jnp.concatenate([rows, rows], axis=1),
                both[k],
                (((1,), (1,)), ((), ())),
                preferred_element_type=f32,
            )
            total = term if total is None else total + term
        for j in range(2):
            rows = pl.ds(pl.multiple_of((j * PIECES + p) * 32, 32), 32)
            part = total[:, j * BLOCK : (j + 1) * BLOCK]
            moved[rows, :] = part if h == 0 else moved[rows, :] + part
        return carry

    lax.fori_loop(0, PIECES, piece, 0, unroll=UNROLL)


def gather_moments(first_row, second_row, moved, summed):
    numbers = iota((2 * SUB, PIECES), 0).astype(f32)
    lane = iota((BLOCK, BLOCK), 0)
    unshuffle = (lane % SUB) * STEPS + lane // SUB == iota((BLOCK, BLOCK), 1)
    unshuffle = jnp.where(unshuffle, 1.0, 0.0).astype(bf16)
    for group in range(3):
        features = range(group * SUB, group * SUB + SUB)
        features = [f for f in features if f < 9] + [16 + f - 9 for f in features if 9 <= f < 12]
        features += [24 + f - 12 for f in range(group * SUB, group * SUB + SUB) if 12 <= f < 15]
        if not features:
            continue
        total = None
        for j, row in enumerate((first_row, second_row)):
            pick = jnp.where(jnp.broadcast_to(row, (2 * SUB, PIECES)) == numbers, 1.0, 0.0)
            values = [
                moved[pl.ds(j * PIECES * 32 + f, PIECES, stride=32), :] for f in features
            ]
            term = exact_pick(pick, jnp.concatenate(values, axis=1))
            total = term if total is None else total + term
        stacked = jnp.concatenate(
            [total[:, k * BLOCK : (k + 1) * BLOCK] for k in range(len(features))], axis=0
        )
        ordered = None
        for part in reversed(split(stacked, 3)):
            term = jnp.dot(part, unshuffle, preferred_element_type=f32)
            ordered = term if ordered is None else ordered + term
        for k, f in enumerate(features):
            summed[f] = ordered[k * 2 * SUB : (k + 1) * 2 * SUB]


def pull_splat(half, pool, summed, grads_ref):
    means = [plane(pool, half, r) for r in range(3)]
    (centre_u, centre_v, conic_xx, conic_xy, conic_yy), geometry_pull = jax.vjp(
        geometry, *means, *[plane(pool, half, r) for r in range(3, 10)]
    )
    basis, harmonics_pull = jax.vjp(harmonics, *means)
    opacity = 1.0 / (1.0 + jnp.exp(-plane(pool, half, 10)))
    sums = [summed[f, half * SUB : (half + 1) * SUB] for f in range(9)]
    total, sum_x, sum_y = sums[:3]
    sum_xx, sum_xy, sum_yy = sums[3] + sums[4], sums[5] + sums[6], sums[7] + sums[8]
    off_x = sum_x - centre_u * total
    off_y = sum_y - centre_v * total
    grad_xx = -0.5 * (sum_xx - centre_u * (sum_x + off_x))
    grad_xy = -(sum_xy - centre_u * sum_y - centre_v * off_x)
    grad_yy = -0.5 * (sum_yy - centre_v * (sum_y + off_y))
    grad_u = conic_xx * off_x + conic_xy * off_y
    grad_v = conic_xy * off_x + conic_yy * off_y
    grads = geometry_pull((grad_u, grad_v, grad_xx, grad_xy, grad_yy))
    tone_grads = []
    for c in range(3):
        grad = summed[16 + c, half * SUB : (half + 1) * SUB] + summed[24 + c, half * SUB : (half + 1) * SUB]
        raw = raw_colour(pool, half, basis, c)
        tone_grads.append(jnp.where(raw > 0, grad, jnp.where(raw == 0, 0.5 * grad, 0.0)))
    basis_grads = []
    for k in range(1, 16):
        basis_grads.append(
            sum(tone_grads[c] * plane(pool, half, 11 + 16 * c + k) for c in range(3))
        )
    mean_grads = harmonics_pull(tuple(basis_grads))
    for r in range(10):
        put_plane(grads_ref, half, r, grads[r] + mean_grads[r] if r < 3 else grads[r])
    put_plane(grads_ref, half, 10, total * (1.0 - opacity))
    for c in range(3):
        put_plane(grads_ref, half, 11 + 16 * c, tone_grads[c] * harmonic_zero)
        for k in range(1, 16):
            put_plane(grads_ref, half, 11 + 16 * c + k, tone_grads[c] * basis[k - 1])


PARTS = 4 * WIDE // BLOCK
MESSAGE = SLOTS * PARTS


def put_slots(ref, values):
    for k in range(SLOTS):
        for r in range(PARTS):
            ref[pl.ds(k * PARTS + r, 32, stride=MESSAGE), :] = values[
                k * 32 : (k + 1) * 32, r * BLOCK : (r + 1) * BLOCK
            ]


def get_slots(ref):
    return jnp.concatenate(
        [
            jnp.concatenate(
                [ref[pl.ds(k * PARTS + r, 32, stride=MESSAGE), :] for r in range(PARTS)], axis=1
            )
            for k in range(SLOTS)
        ],
        axis=0,
    )


def route(owner_row, cell_row, me):
    owner_col = to_column(owner_row)
    far_row = owner_row - me.astype(f32)
    far_row = jnp.where(far_row < 0, far_row + float(PIECES), far_row)
    far_col = to_column(far_row)
    square = (PIECES, PIECES)
    same = jnp.broadcast_to(owner_row, square) == jnp.broadcast_to(owner_col, square)
    first, second = iota(square, 0), iota(square, 1)
    rank_row = jnp.sum(jnp.where(same & (first < second), 1.0, 0.0), axis=0, keepdims=True)
    rank_col = jnp.sum(jnp.where(same & (second < first), 1.0, 0.0), axis=1, keepdims=True)
    slots = SLOTS * 32
    pack = jnp.broadcast_to(rank_row * 32.0 + far_row, (slots, PIECES)) == iota((slots, PIECES), 0).astype(f32)
    pack = jnp.where(pack, 1.0, 0.0)
    unpack = jnp.broadcast_to(rank_col * 32.0 + far_col, (PIECES, slots)) == iota((PIECES, slots), 1).astype(f32)
    unpack = jnp.where(unpack, 1.0, 0.0)
    label_col = jnp.sum(pack * (cell_row + 1.0), axis=1, keepdims=True) - 1.0
    lane = iota((32, BLOCK), 1)
    label_rows = jnp.where(lane == 0, label_col[:32], jnp.where(lane == 1, label_col[32:], -1.0))
    return pack, unpack, label_rows


def composite(h, grid, target, background):
    def at(depth, channel):
        return grid[depth * SUB : (depth + 1) * SUB, channel * WIDE : (channel + 1) * WIDE]

    in_front = jnp.ones((TILE_DEV, WIDE), f32)
    seen = [jnp.zeros((TILE_DEV, WIDE), f32) for _ in range(3)]
    fronts = []
    for depth in range(MAXD):
        fronts.append(in_front)
        seen = [seen[c] + in_front * at(depth, c) for c in range(3)]
        in_front = in_front * (1.0 - at(depth, 3))
    residual = [
        seen[c] + in_front * background[c] - target[c, :, h * WIDE : (h + 1) * WIDE] for c in range(3)
    ]
    behind = [jnp.full((TILE_DEV, WIDE), background[c], f32) for c in range(3)]
    rows = [None] * MAXD
    for depth in reversed(range(MAXD)):
        through = 1.0 - at(depth, 3)
        by_trans = residual[0] * behind[0] + residual[1] * behind[1] + residual[2] * behind[2]
        rows[depth] = jnp.concatenate(
            [fronts[depth] * residual[c] for c in range(3)] + [fronts[depth] * by_trans], axis=1
        )
        behind = [at(depth, c) + through * behind[c] for c in range(3)]
    return jnp.concatenate(rows, axis=0)


def step_kernel(
    params_hbm,
    blocks_hbm,
    live_hbm,
    owner_hbm,
    cell_hbm,
    target_hbm,
    background_hbm,
    features_hbm,
    moments_hbm,
    grads_ref,
    blocks,
    live,
    background,
    block_rows,
    owner,
    cell,
    target,
    features,
    moments,
    pool,
    stage,
    turned,
    table,
    spread,
    prefix,
    segment,
    alphas,
    weights,
    ends,
    weight_parts,
    pieces,
    sent,
    got,
    replies,
    answers,
    labels,
    got_labels,
    cotangent,
    moved,
    summed,
    local_sem,
    halo_send,
    halo_recv,
    edge_send,
    edge_recv,
    label_send,
    label_recv,
    send_sem,
    recv_sem,
    reply_send,
    reply_recv,
):
    regions, region = lax.axis_size("region"), lax.axis_index("region")
    count, me = lax.axis_size("dom"), lax.axis_index("dom")
    upper, lower = lax.rem(region + 1, regions), lax.rem(region + regions - 1, regions)

    def block_rows_of(ref, b):
        return ref.at[pl.ds(b * ROWS, PARAMS)]

    fetches = []

    def fetch(src, dst):
        copy = pltpu.make_async_copy(src, dst, local_sem.at[len(fetches)])
        copy.start()
        fetches.append(copy)
        return copy

    routing = [fetch(owner_hbm, owner), fetch(cell_hbm, cell)]
    own = [
        fetch(params_hbm.at[:, pl.ds(b * BLOCK, BLOCK)], block_rows_of(pool, b)) for b in range(BLOCKS)
    ]
    scalars = [fetch(blocks_hbm, blocks), fetch(live_hbm, live), fetch(features_hbm, features)]
    later = [
        fetch(blocks_hbm, block_rows),
        fetch(target_hbm, target),
        fetch(background_hbm, background),
        fetch(moments_hbm, moments),
    ]

    barrier = pltpu.get_barrier_semaphore()

    def signal(**where):
        pl.semaphore_signal(barrier, inc=1, device_id=where, device_id_type=MESH)

    def greet(d, carry):
        signal(dom=lax.rem(me + d, count))
        return carry

    signal(region=upper)
    signal(region=lower)
    lax.fori_loop(1, count, greet, 0)

    for copy in routing:
        copy.wait()
    pack, unpack, label_rows = route(owner[...].astype(f32), cell[...].astype(f32), me)
    for d in range(32):
        labels[d] = label_rows[d : d + 1]
    pl.semaphore_wait(barrier, count + 1)

    def remote(src, dst, send, recv, **where):
        return pltpu.make_async_remote_copy(
            src_ref=src, dst_ref=dst, send_sem=send, recv_sem=recv, device_id=where, device_id_type=MESH
        )

    def label(d, many=1):
        rows = pl.ds(d, many)
        return remote(
            labels.at[rows], got_labels.at[rows], label_send, label_recv, dom=lax.rem(me + d, count)
        )

    def message(d, many):
        return pl.ds(pl.multiple_of(d * MESSAGE, MESSAGE), many * MESSAGE)

    def payload(h, d, many=1):
        rows = message(d, many)
        return remote(
            sent.at[h, rows], got.at[h, rows], send_sem.at[h], recv_sem.at[h], dom=lax.rem(me + d, count)
        )

    def reply(h, d, many=1):
        rows = message(d, many)
        return remote(
            replies.at[h, rows],
            answers.at[h, rows],
            reply_send.at[h],
            reply_recv.at[h],
            dom=lax.rem(me + count - d, count),
        )

    def start_all(copy, falling=True):
        def one(d, carry):
            copy(count - d if falling else d).start()
            return carry

        lax.fori_loop(1, count, one, 0, unroll=START_UNROLL)

    others = count - 1

    halo = [
        remote(
            params_hbm.at[:, pl.ds((BLOCKS - 1) * BLOCK, BLOCK)],
            block_rows_of(pool, LOW),
            halo_send.at[0],
            halo_recv.at[0],
            region=upper,
        ),
        remote(
            params_hbm.at[:, pl.ds(0, BLOCK)],
            block_rows_of(pool, HIGH),
            halo_send.at[1],
            halo_recv.at[1],
            region=lower,
        ),
    ]
    for copy in halo:
        copy.start()

    for copy in own:
        copy.wait()
    for b in range(POOL, 2 * SUB):
        pool[b * ROWS : b * ROWS + PARAMS, :] = pool[0:PARAMS, :]
    tabulate(0, SUB, pool, stage, turned, table, spread)
    start_all(label)
    got_labels[0] = labels[0]
    for copy in halo:
        copy.wait_recv()
    tabulate(1, POOL - SUB, pool, stage, turned, table, spread)
    lane = iota((BLOCK, COLS), 1)
    table[DEAD] = jnp.where(lane == 0, -1e30, 0.0).astype(bf16)
    spread[DEAD] = jnp.zeros((3, BLOCK, BLOCK), f32)

    for copy in scalars:
        copy.wait()
    for h in range(HALVES):
        forward_half(h, blocks, live, features, table, spread, prefix, segment, pieces, alphas)
        rendered = [pieces[r * PIECES : (r + 1) * PIECES, :] for r in range(PARTS)]
        rendered = jnp.concatenate(rendered, axis=1)
        put_slots(sent.at[h], exact_pick(pack, rendered))
        start_all(functools.partial(payload, h))
        got[h, :MESSAGE] = sent[h, :MESSAGE]

    weigh_half(0, prefix, alphas, weights, ends, weight_parts)
    for copy in later:
        copy.wait()
    label(1, others).wait()
    arrived = jnp.concatenate([got_labels[d] for d in range(32)], axis=0)
    arrived_col = jnp.concatenate([arrived[:, 0:1], arrived[:, 1:2]], axis=0)
    arrived_row = to_row(arrived_col)
    slots = SLOTS * 32

    def cell_of(place):
        return ((place % TILE_DEV) * MAXD + place // TILE_DEV).astype(f32)

    gather = jnp.broadcast_to(arrived_row, (CELLS, slots)) == cell_of(iota((CELLS, slots), 0))
    gather = jnp.where(gather, 1.0, 0.0)
    scatter = jnp.broadcast_to(arrived_col, (slots, CELLS)) == cell_of(iota((slots, CELLS), 1))
    scatter = jnp.where(scatter, 1.0, 0.0)
    colours = [background[c] for c in range(3)]
    for h in range(HALVES):
        payload(h, 1, others).wait()
        grid = exact_pick(gather, get_slots(got.at[h]))
        put_slots(replies.at[h], exact_pick(scatter, composite(h, grid, target, colours)))
        start_all(functools.partial(reply, h), falling=False)
        answers[h, :MESSAGE] = replies[h, :MESSAGE]
        if h + 1 < HALVES:
            weigh_half(h + 1, prefix, alphas, weights, ends, weight_parts)

    for h in range(HALVES):
        reply(h, 1, others).wait()
        back = exact_pick(unpack, get_slots(answers.at[h]))
        for k in range(WIDE // BLOCK):
            for c in range(SUB):
                lanes = slice(c * WIDE + k * BLOCK, c * WIDE + (k + 1) * BLOCK)
                rows = back[:, lanes] if c < 4 else jnp.zeros((PIECES, BLOCK), f32)
                cotangent[pl.ds(k * PIECES * SUB + c, PIECES, stride=SUB), :] = rows
        backward_half(
            h, blocks, live, moments, table, segment, alphas, weights, ends, weight_parts, cotangent, moved
        )

    rows = own_block(block_rows[...]).astype(f32)
    gather_moments(rows[0:1], rows[1:2], moved, summed)
    pull_splat(1, pool, summed, grads_ref)
    edges = [
        remote(block_rows_of(grads_ref, HIGH), block_rows_of(grads_ref, FROM_LEFT), edge_send.at[0], edge_recv.at[0], region=upper),
        remote(block_rows_of(grads_ref, LOW), block_rows_of(grads_ref, FROM_RIGHT), edge_send.at[1], edge_recv.at[1], region=lower),
    ]
    for copy in edges:
        copy.start()
    pull_splat(0, pool, summed, grads_ref)
    for copy in halo:
        copy.wait_send()
    for copy in edges:
        copy.wait()


def whole(memory=pltpu.VMEM):
    return pl.BlockSpec(memory_space=memory)


def step(*operands):
    shape = jax.ShapeDtypeStruct
    vmem, smem, dma = pltpu.VMEM, pltpu.SMEM, pltpu.SemaphoreType.DMA
    slots = vmem((HALVES, 32 * MESSAGE, BLOCK), f32)
    label = vmem((32, 1, BLOCK), f32)
    return pl.pallas_call(
        step_kernel,
        out_shape=shape(((FROM_RIGHT + 1) * ROWS, BLOCK), f32),
        in_specs=[whole(pltpu.HBM)] * 9,
        out_specs=whole(),
        scratch_shapes=[
            smem((2, PIECES), jnp.int32),
            smem((1, PIECES), jnp.int32),
            smem((3,), f32),
            vmem((2, PIECES), jnp.int32),
            vmem((1, PIECES), jnp.int32),
            vmem((1, PIECES), jnp.int32),
            vmem((3, TILE_DEV, PIX), f32),
            vmem((PIECES, 32, PIX), bf16),
            vmem((PIECES, 16, PIX), bf16),
            vmem((2 * SUB * ROWS, BLOCK), f32),
            vmem((SUB * COLS, BLOCK), f32),
            vmem((BLOCK, BLOCK), f32),
            vmem((TAB, BLOCK, COLS), bf16),
            vmem((TAB, 3, BLOCK, BLOCK), f32),
            vmem((HALVES, PIECES, 2, SUB, WIDE), f32),
            vmem((HALVES, PIECES, 2, 3, SUB, WIDE), f32),
            vmem((HALVES, PIECES, 2, BLOCK, WIDE), f32),
            vmem((HALVES, PIECES, 2, BLOCK, WIDE), f32),
            vmem((HALVES, PIECES, 2, SUB, WIDE), f32),
            vmem((HALVES, PIECES, 2 * BLOCK, 2 * WIDE), bf16),
            vmem((4 * WIDE // BLOCK * PIECES, BLOCK), f32),
            slots,
            slots,
            slots,
            slots,
            label,
            label,
            vmem((WIDE // BLOCK * PIECES * SUB, BLOCK), f32),
            vmem((2 * PIECES * 32, BLOCK), f32),
            vmem((32, 2 * SUB, BLOCK), f32),
            dma((17,)),
            dma((2,)),
            dma((2,)),
            dma((2,)),
            dma((2,)),
            dma,
            dma,
            dma((HALVES,)),
            dma((HALVES,)),
            dma((HALVES,)),
            dma((HALVES,)),
        ],
        compiler_params=pltpu.CompilerParams(
            collective_id=0, has_side_effects=True, vmem_limit_bytes=VMEM_LIMIT
        ),
        name="render_step",
    )(*operands)


def adam_kernel(
    grads_ref, params_ref, first_ref, second_ref,
    gradient_ref, new_params_ref, new_first_ref, new_second_ref,
):
    for b in range(BLOCKS):
        cols = slice(b * BLOCK, (b + 1) * BLOCK)
        gradient = grads_ref[b * ROWS : b * ROWS + PARAMS, :]
        if b == 0:
            gradient = gradient + grads_ref[FROM_LEFT * ROWS : FROM_LEFT * ROWS + PARAMS, :]
        if b == BLOCKS - 1:
            gradient = gradient + grads_ref[FROM_RIGHT * ROWS : FROM_RIGHT * ROWS + PARAMS, :]
        new_first = beta_one * first_ref[:, cols] + (1 - beta_one) * gradient
        new_second = beta_two * second_ref[:, cols] + (1 - beta_two) * gradient * gradient
        update = (
            new_first
            / (1 - beta_one**adam_step)
            / (jnp.sqrt(new_second / (1 - beta_two**adam_step)) + tiny)
        )
        gradient_ref[:, cols] = gradient
        new_params_ref[:, cols] = params_ref[:, cols] - rate * update
        new_first_ref[:, cols] = new_first
        new_second_ref[:, cols] = new_second


def adam(*operands):
    return pl.pallas_call(
        adam_kernel,
        out_shape=(jax.ShapeDtypeStruct((PARAMS, BLOCKS * BLOCK), f32),) * 4,
        in_specs=[whole()] * 4,
        out_specs=(whole(),) * 4,
        compiler_params=pltpu.CompilerParams(vmem_limit_bytes=8 * 1024 * 1024),
        name="adam",
    )(*operands)


def on_device(
    params,
    first_moment,
    second_moment,
    piece_blocks,
    piece_live,
    piece_owner,
    piece_cell,
    target,
    background,
):
    grads = step(
        params,
        piece_blocks[0].T,
        piece_live,
        piece_owner,
        piece_cell,
        jnp.transpose(target[0], (1, 0, 2)),
        background,
        jnp.asarray(exponent_features()),
        jnp.asarray(moment_features()),
    )
    return adam(grads, params, first_moment, second_moment)


def solution(mesh):
    in_specs = (
        P(None, ("region", "dom")),
        P(None, ("region", "dom")),
        P(None, ("region", "dom")),
        P(("region", "dom"), None, None),
        P(("region", "dom"), None),
        P(("region", "dom"), None),
        P(("region", "dom"), None),
        P(("region", "dom"), None, None, None),
        P(),
    )
    out_specs = (
        P(None, ("region", "dom")),
        P(None, ("region", "dom")),
        P(None, ("region", "dom")),
        P(None, ("region", "dom")),
    )
    return jax.shard_map(
        on_device, mesh=mesh, in_specs=in_specs, out_specs=out_specs, check_vma=False
    )
```

```python
import functools
import math

import jax
import jax.numpy as jnp
import ml_dtypes
import numpy as np
from jax import lax
from jax.experimental import pallas as pl
from jax.experimental.pallas import tpu as pltpu
from jax.sharding import PartitionSpec as P

PARAMS = 59
TSIDE = 16
WIN = 8
BLOCK = 128
BLOCKS = 8
MAXD = 8
PIECES = 32
PIX = 256
TILE_DEV = 8
CELLS = 64
POOL = 10
SLOTS = 2
SUB = 8
STEPS = BLOCK // SUB
TAB = POOL + 1
PLANES = 16
ROWS = 64
COLS = 96
UNROLL = 16
MIDDLE_UNROLL = 4
START_UNROLL = 1
HALVES = 2
WIDE = PIX // HALVES
LOW = BLOCKS
HIGH = BLOCKS + 1
DEAD = POOL
FROM_LEFT = BLOCKS
FROM_RIGHT = FROM_LEFT + 1
ORIGIN_X = 64.0
ORIGIN_Y = 32.0

harmonic_zero = 0.28209479177387814
harmonic_one = 0.4886025119029199
harmonic_two = (
    1.0925484305920792,
    -1.0925484305920792,
    0.31539156525252005,
    -1.0925484305920792,
    0.5462742152960396,
)
harmonic_three = (
    -0.5900435899266435,
    2.890611442640554,
    -0.4570457994644658,
    0.3731763325901154,
    -0.4570457994644658,
    1.445305721320277,
    -0.5900435899266435,
)
beta_one = 0.9
beta_two = 0.999
rate = 0.001
adam_step = 100
tiny = 1e-08

f32 = jnp.float32
bf16 = jnp.bfloat16
MESH = pl.DeviceIdType.MESH
VMEM_LIMIT = 60 * 1024 * 1024


def pixel_monomials():
    bf = ml_dtypes.bfloat16
    tile = np.arange(PIECES)[:, None]
    pixel = np.arange(PIX)[None, :]
    x = (TSIDE * (tile % WIN) + pixel % TSIDE + 0.5 - ORIGIN_X).astype(np.float32)
    y = (TSIDE * (tile // WIN) + pixel // TSIDE + 0.5 - ORIGIN_Y).astype(np.float32)

    def two(value):
        head = value.astype(bf).astype(np.float32)
        return [head, value - head]

    return [np.ones_like(x), x, y] + two(x * x) + two(x * y) + two(y * y)


def exponent_features():
    rows = [row for row in pixel_monomials() for _ in range(3)]
    rows += [np.zeros_like(rows[0])] * (32 - len(rows))
    return np.stack(rows, axis=1).astype(ml_dtypes.bfloat16)


def moment_features():
    rows = pixel_monomials()
    rows += [np.zeros_like(rows[0])] * (16 - len(rows))
    return np.stack(rows, axis=1).astype(ml_dtypes.bfloat16)


def split(value, parts):
    out = []
    rest = value
    for part in range(parts):
        head = rest.astype(bf16)
        out.append(head)
        if part < parts - 1:
            rest = rest - head.astype(f32)
    return out


def exact_pick(onehot, value):
    picks = onehot.astype(bf16)
    total = None
    for part in reversed(split(value, 3)):
        term = jnp.dot(picks, part, preferred_element_type=f32)
        total = term if total is None else total + term
    return total


def iota(shape, dim):
    return lax.broadcasted_iota(jnp.int32, shape, dim)


def to_column(row):
    n = row.shape[1]
    spread = jnp.broadcast_to(row, (n, n))
    return jnp.sum(jnp.where(iota((n, n), 0) == iota((n, n), 1), spread, 0.0), axis=1, keepdims=True)


def to_row(column):
    n = column.shape[0]
    spread = jnp.broadcast_to(column, (n, n))
    return jnp.sum(jnp.where(iota((n, n), 0) == iota((n, n), 1), spread, 0.0), axis=0, keepdims=True)


def geometry(mean_x, mean_y, mean_z, log_a, log_b, log_c, quat_w, quat_x, quat_y, quat_z):
    screen_px = float(WIN * TSIDE)
    scales = (jnp.exp(log_a), jnp.exp(log_b), jnp.exp(log_c))
    norm = 1.0 / jnp.sqrt(quat_w * quat_w + quat_x * quat_x + quat_y * quat_y + quat_z * quat_z)
    quat_w, quat_x, quat_y, quat_z = quat_w * norm, quat_x * norm, quat_y * norm, quat_z * norm
    rotation = [
        [
            1 - 2 * (quat_y * quat_y + quat_z * quat_z),
            2 * (quat_x * quat_y - quat_w * quat_z),
            2 * (quat_x * quat_z + quat_w * quat_y),
        ],
        [
            2 * (quat_x * quat_y + quat_w * quat_z),
            1 - 2 * (quat_x * quat_x + quat_z * quat_z),
            2 * (quat_y * quat_z - quat_w * quat_x),
        ],
        [
            2 * (quat_x * quat_z - quat_w * quat_y),
            2 * (quat_y * quat_z + quat_w * quat_x),
            1 - 2 * (quat_x * quat_x + quat_y * quat_y),
        ],
    ]
    focal_px = 0.3125 * screen_px
    inv_z = 1.0 / mean_z
    ratio_x, ratio_y = mean_x * inv_z, mean_y * inv_z
    focal_z = focal_px * inv_z
    rows = []
    for ratio, axis in ((ratio_x, 0), (ratio_y, 1)):
        rows.append(
            [
                focal_z * (rotation[axis][col] - ratio * rotation[2][col]) * scales[col]
                for col in range(3)
            ]
        )
    sigma_xx = rows[0][0] * rows[0][0] + rows[0][1] * rows[0][1] + rows[0][2] * rows[0][2] + 0.3
    sigma_xy = rows[0][0] * rows[1][0] + rows[0][1] * rows[1][1] + rows[0][2] * rows[1][2]
    sigma_yy = rows[1][0] * rows[1][0] + rows[1][1] * rows[1][1] + rows[1][2] * rows[1][2] + 0.3
    inv_det = 1.0 / (sigma_xx * sigma_yy - sigma_xy * sigma_xy)
    return (
        focal_px * ratio_x + (0.5 * screen_px - ORIGIN_X),
        focal_px * ratio_y + (0.5 * screen_px - ORIGIN_Y),
        sigma_yy * inv_det,
        -sigma_xy * inv_det,
        sigma_xx * inv_det,
    )


def harmonics(mean_x, mean_y, mean_z):
    inv_length = 1.0 / jnp.sqrt(mean_x * mean_x + mean_y * mean_y + mean_z * mean_z)
    dir_x, dir_y, dir_z = mean_x * inv_length, mean_y * inv_length, mean_z * inv_length
    sq_x, sq_y, sq_z = dir_x * dir_x, dir_y * dir_y, dir_z * dir_z
    return (
        -harmonic_one * dir_y,
        harmonic_one * dir_z,
        -harmonic_one * dir_x,
        harmonic_two[0] * dir_x * dir_y,
        harmonic_two[1] * dir_y * dir_z,
        harmonic_two[2] * (2 * sq_z - sq_x - sq_y),
        harmonic_two[3] * dir_x * dir_z,
        harmonic_two[4] * (sq_x - sq_y),
        harmonic_three[0] * dir_y * (3 * sq_x - sq_y),
        harmonic_three[1] * dir_x * dir_y * dir_z,
        harmonic_three[2] * dir_y * (4 * sq_z - sq_x - sq_y),
        harmonic_three[3] * dir_z * (2 * sq_z - 3 * sq_x - 3 * sq_y),
        harmonic_three[4] * dir_x * (4 * sq_z - sq_x - sq_y),
        harmonic_three[5] * dir_z * (sq_x - sq_y),
        harmonic_three[6] * dir_x * (sq_x - 3 * sq_y),
    )


def plane(ref, half, row):
    return ref[pl.ds(half * SUB * ROWS + row, SUB, stride=ROWS), :]


def put_plane(ref, half, row, value):
    ref[pl.ds(half * SUB * ROWS + row, SUB, stride=ROWS), :] = value


def raw_colour(pool, half, basis, colour):
    total = harmonic_zero * plane(pool, half, 11 + 16 * colour) + 0.5
    for k in range(1, 16):
        total = total + plane(pool, half, 11 + 16 * colour + k) * basis[k - 1]
    return total


def own_block(number):
    return jnp.where(number == 0, LOW, jnp.where(number == POOL - 1, HIGH, number - 1))


def roll_rows(value, shift):
    return pltpu.roll(value, shift % SUB, axis=0)


def tabulate(half, count, pool, stage, turned, table, spread):
    region = lax.axis_index("region")
    regions = lax.axis_size("region")
    means = [plane(pool, half, r) for r in range(3)]
    centre_u, centre_v, conic_xx, conic_xy, conic_yy = geometry(
        *means, *[plane(pool, half, r) for r in range(3, 10)]
    )
    opacity = 1.0 / (1.0 + jnp.exp(-plane(pool, half, 10)))
    log2_e = 1.0 / math.log(2.0)
    slope_x = conic_xx * centre_u + conic_xy * centre_v
    slope_y = conic_xy * centre_u + conic_yy * centre_v
    constant = jnp.log(opacity) - 0.5 * (centre_u * slope_x + centre_v * slope_y)
    constant = log2_e * constant
    if half:
        row = iota((SUB, BLOCK), 0)
        absent = ((row == LOW - SUB) & (region == 0)) | ((row == HIGH - SUB) & (region == regions - 1))
        constant = jnp.where(absent, -1e30, constant)
    terms = [
        constant,
        log2_e * slope_x,
        log2_e * slope_y,
        (-0.5 * log2_e) * conic_xx,
        (-log2_e) * conic_xy,
        (-0.5 * log2_e) * conic_yy,
    ]
    stage[...] = jnp.zeros_like(stage)

    def put(row, value):
        stage[pl.ds(row, SUB, stride=COLS), :] = value

    row = 0
    for term, copies in zip(terms, (1, 1, 1, 2, 2, 2)):
        parts = [part.astype(f32) for part in split(term, 3)]
        for _ in range(copies):
            for part in parts:
                put(row, part)
                row += 1
    basis = harmonics(*means)
    for c in range(3):
        tone = jnp.maximum(raw_colour(pool, half, basis, c), 0.0)
        parts = [part.astype(f32) for part in split(tone, 3)]
        for group, part in enumerate((0, 0, 0, 1, 1, 2)):
            put(32 + group * SUB + c, parts[part])
        put(80 + c, tone)

    def turn(b, carry):
        turned[:, :COLS] = stage[pl.ds(pl.multiple_of(b * COLS, COLS), COLS), :].T
        ordered = jnp.concatenate(
            [turned[pl.ds(t, SUB, stride=STEPS), :] for t in range(STEPS)], axis=0
        )
        table[half * SUB + b] = ordered[:, :COLS].astype(bf16)
        for c in range(3):
            spread[half * SUB + b, c] = jnp.broadcast_to(ordered[:, 80 + c : 81 + c], (BLOCK, BLOCK))
        return carry

    lax.fori_loop(0, count, turn, 0, unroll=2)


def exponents(table, features, block):
    return jnp.dot(table[block, :, :32], features, preferred_element_type=f32)


def two_blocks(p, blocks, live):
    first = own_block(blocks[0, p])
    second = jnp.where(live[0, p] > 1, own_block(blocks[1, p]), DEAD)
    return first, second


def forward_half(
    h, blocks, live, features_ref, table, spread, prefix_ref, segment_ref, pieces, alphas_ref
):
    sub = iota((SUB, WIDE), 0)

    def piece(p, carry):
        features = features_ref[p, :, h * WIDE : (h + 1) * WIDE]
        before = None
        colours = [None] * 3
        for j, block in enumerate(two_blocks(p, blocks, live)):
            exponent = exponents(table, features, block)
            transmit = jnp.ones((SUB, WIDE), f32)
            sums = [jnp.zeros((SUB, WIDE), f32) for _ in range(3)]
            for t in range(STEPS):
                rows = slice(t * SUB, (t + 1) * SUB)
                alpha = jnp.exp2(exponent[rows])
                alphas_ref[h, p, j, rows] = alpha
                weight = alpha * transmit
                transmit = transmit - weight
                for c in range(3):
                    tone = spread[block, c, rows, :]
                    tone = tone if WIDE == BLOCK else jnp.concatenate([tone, tone], axis=1)
                    sums[c] = sums[c] + tone * weight
            run = transmit
            for shift in (1, 2, 4):
                run = run * jnp.where(sub >= shift, roll_rows(run, shift), 1.0)
            prefix = jnp.where(sub >= 1, roll_rows(run, 1), 1.0)
            total = run[SUB - 1 :, :]
            if before is not None:
                prefix = prefix * before
                total = total * before
            before = total
            prefix_ref[h, p, j] = prefix
            for c in range(3):
                piece_sum = prefix * sums[c]
                segment_ref[h, p, j, c] = piece_sum
                colours[c] = piece_sum if j == 0 else colours[c] + piece_sum
        rows = [jnp.sum(colours[c], axis=0, keepdims=True) for c in range(3)] + [1.0 - before]
        for c in range(4):
            for k in range(WIDE // BLOCK):
                place = (c * (WIDE // BLOCK) + k) * PIECES + p
                pieces[pl.ds(place, 1), :] = rows[c][:, k * BLOCK : (k + 1) * BLOCK]
        return carry

    lax.fori_loop(0, PIECES, piece, 0, unroll=UNROLL)


def weigh_half(h, prefix_ref, alphas_ref, weights_ref, ends_ref, weight_parts_ref):
    def piece(p, carry):
        for j in range(2):
            transmit = prefix_ref[h, p, j]
            weights = []
            for t in range(STEPS):
                rows = slice(t * SUB, (t + 1) * SUB)
                weight = alphas_ref[h, p, j, rows] * transmit
                transmit = transmit - weight
                weights_ref[h, p, j, rows] = weight
                weights.append(weight)
            ends_ref[h, p, j] = transmit
            weight_parts_ref[h, p, j * BLOCK : (j + 1) * BLOCK] = jnp.concatenate(
                split(jnp.concatenate(weights, axis=0), 2), axis=1
            )
        return carry

    lax.fori_loop(0, PIECES, piece, 0, unroll=MIDDLE_UNROLL)


def backward_half(
    h, blocks, live, moments_ref, table, segment_ref, alphas_ref, weights_ref, ends_ref, weight_parts_ref,
    cotangent, moved,
):
    sub = iota((SUB, WIDE), 0)
    nothing = jnp.zeros((16, WIDE), bf16)
    none = jnp.zeros((16, WIDE), f32)
    lanes = slice(h * WIDE, (h + 1) * WIDE)

    def piece(p, carry):
        monomials = moments_ref[p, :, lanes]
        cot = jnp.concatenate(
            [
                cotangent[pl.ds(pl.multiple_of((k * PIECES + p) * SUB, SUB), SUB), :]
                for k in range(WIDE // BLOCK)
            ],
            axis=1,
        )
        heads = [part.astype(f32) for part in split(cot, 3)]
        tones = [none, none] + [heads[part] for part in (0, 1, 2, 0, 1, 0)] + [none]
        tones = jnp.concatenate(tones, axis=0).astype(bf16)
        colour_rows = jnp.concatenate([heads[0], heads[1]], axis=0).astype(bf16)
        for_gradient = jnp.concatenate([monomials, nothing], axis=0)
        for_weight = jnp.concatenate([nothing, colour_rows], axis=0)
        state = []
        for j, block in enumerate(two_blocks(p, blocks, live)):
            tone = jnp.dot(table[block], tones, preferred_element_type=f32)
            seen = segment_ref[h, p, j, 0] * cot[0:1]
            for c in (1, 2):
                seen = seen + segment_ref[h, p, j, c] * cot[c : c + 1]
            run = seen
            for shift in (1, 2, 4):
                run = run + jnp.where(sub < SUB - shift, roll_rows(run, -shift), 0.0)
            state.append((tone, run))
        behind = ends_ref[h, p, 1, SUB - 1 :, :] * cot[3:4]
        parts = [None, None]
        for j in (1, 0):
            tone, run = state[j]
            after = jnp.where(sub < SUB - 1, roll_rows(run, -1), 0.0) + behind
            behind = behind + run[0:1]
            ahead = after / ends_ref[h, p, j]
            gradients = [None] * STEPS
            for t in reversed(range(STEPS)):
                rows = slice(t * SUB, (t + 1) * SUB)
                gap = tone[rows] - ahead
                gradients[t] = weights_ref[h, p, j, rows] * gap
                ahead = ahead + alphas_ref[h, p, j, rows] * gap
            parts[j] = jnp.concatenate(split(jnp.concatenate(gradients, axis=0), 2), axis=1)
        both = [jnp.concatenate(parts, axis=0), weight_parts_ref[h, p]]
        total = None
        for k in range(2):
            rows = (for_gradient, for_weight)[k]
            term = lax.dot_general(
                jnp.concatenate([rows, rows], axis=1),
                both[k],
                (((1,), (1,)), ((), ())),
                preferred_element_type=f32,
            )
            total = term if total is None else total + term
        for j in range(2):
            rows = pl.ds(pl.multiple_of((j * PIECES + p) * 32, 32), 32)
            part = total[:, j * BLOCK : (j + 1) * BLOCK]
            moved[rows, :] = part if h == 0 else moved[rows, :] + part
        return carry

    lax.fori_loop(0, PIECES, piece, 0, unroll=UNROLL)


def gather_moments(first_row, second_row, moved, summed):
    numbers = iota((2 * SUB, PIECES), 0).astype(f32)
    lane = iota((BLOCK, BLOCK), 0)
    unshuffle = (lane % SUB) * STEPS + lane // SUB == iota((BLOCK, BLOCK), 1)
    unshuffle = jnp.where(unshuffle, 1.0, 0.0).astype(bf16)
    for group in range(3):
        features = range(group * SUB, group * SUB + SUB)
        features = [f for f in features if f < 9] + [16 + f - 9 for f in features if 9 <= f < 12]
        features += [24 + f - 12 for f in range(group * SUB, group * SUB + SUB) if 12 <= f < 15]
        if not features:
            continue
        total = None
        for j, row in enumerate((first_row, second_row)):
            pick = jnp.where(jnp.broadcast_to(row, (2 * SUB, PIECES)) == numbers, 1.0, 0.0)
            values = [
                moved[pl.ds(j * PIECES * 32 + f, PIECES, stride=32), :] for f in features
            ]
            term = exact_pick(pick, jnp.concatenate(values, axis=1))
            total = term if total is None else total + term
        stacked = jnp.concatenate(
            [total[:, k * BLOCK : (k + 1) * BLOCK] for k in range(len(features))], axis=0
        )
        ordered = None
        for part in reversed(split(stacked, 3)):
            term = jnp.dot(part, unshuffle, preferred_element_type=f32)
            ordered = term if ordered is None else ordered + term
        for k, f in enumerate(features):
            summed[f] = ordered[k * 2 * SUB : (k + 1) * 2 * SUB]


def pull_splat(half, pool, summed, grads_ref):
    means = [plane(pool, half, r) for r in range(3)]
    (centre_u, centre_v, conic_xx, conic_xy, conic_yy), geometry_pull = jax.vjp(
        geometry, *means, *[plane(pool, half, r) for r in range(3, 10)]
    )
    basis, harmonics_pull = jax.vjp(harmonics, *means)
    opacity = 1.0 / (1.0 + jnp.exp(-plane(pool, half, 10)))
    sums = [summed[f, half * SUB : (half + 1) * SUB] for f in range(9)]
    total, sum_x, sum_y = sums[:3]
    sum_xx, sum_xy, sum_yy = sums[3] + sums[4], sums[5] + sums[6], sums[7] + sums[8]
    off_x = sum_x - centre_u * total
    off_y = sum_y - centre_v * total
    grad_xx = -0.5 * (sum_xx - centre_u * (sum_x + off_x))
    grad_xy = -(sum_xy - centre_u * sum_y - centre_v * off_x)
    grad_yy = -0.5 * (sum_yy - centre_v * (sum_y + off_y))
    grad_u = conic_xx * off_x + conic_xy * off_y
    grad_v = conic_xy * off_x + conic_yy * off_y
    grads = geometry_pull((grad_u, grad_v, grad_xx, grad_xy, grad_yy))
    tone_grads = []
    for c in range(3):
        grad = summed[16 + c, half * SUB : (half + 1) * SUB] + summed[24 + c, half * SUB : (half + 1) * SUB]
        raw = raw_colour(pool, half, basis, c)
        tone_grads.append(jnp.where(raw > 0, grad, jnp.where(raw == 0, 0.5 * grad, 0.0)))
    basis_grads = []
    for k in range(1, 16):
        basis_grads.append(
            sum(tone_grads[c] * plane(pool, half, 11 + 16 * c + k) for c in range(3))
        )
    mean_grads = harmonics_pull(tuple(basis_grads))
    for r in range(10):
        put_plane(grads_ref, 0, r, grads[r] + mean_grads[r] if r < 3 else grads[r])
    put_plane(grads_ref, 0, 10, total * (1.0 - opacity))
    for c in range(3):
        put_plane(grads_ref, 0, 11 + 16 * c, tone_grads[c] * harmonic_zero)
        for k in range(1, 16):
            put_plane(grads_ref, 0, 11 + 16 * c + k, tone_grads[c] * basis[k - 1])


PARTS = 4 * WIDE // BLOCK
MESSAGE = SLOTS * PARTS


def put_slots(ref, values):
    for k in range(SLOTS):
        for r in range(PARTS):
            ref[pl.ds(k * PARTS + r, 32, stride=MESSAGE), :] = values[
                k * 32 : (k + 1) * 32, r * BLOCK : (r + 1) * BLOCK
            ]


def get_slots(ref):
    return jnp.concatenate(
        [
            jnp.concatenate(
                [ref[pl.ds(k * PARTS + r, 32, stride=MESSAGE), :] for r in range(PARTS)], axis=1
            )
            for k in range(SLOTS)
        ],
        axis=0,
    )


def route(owner_row, cell_row, me):
    owner_col = to_column(owner_row)
    far_row = owner_row - me.astype(f32)
    far_row = jnp.where(far_row < 0, far_row + float(PIECES), far_row)
    far_col = to_column(far_row)
    square = (PIECES, PIECES)
    same = jnp.broadcast_to(owner_row, square) == jnp.broadcast_to(owner_col, square)
    first, second = iota(square, 0), iota(square, 1)
    rank_row = jnp.sum(jnp.where(same & (first < second), 1.0, 0.0), axis=0, keepdims=True)
    rank_col = jnp.sum(jnp.where(same & (second < first), 1.0, 0.0), axis=1, keepdims=True)
    slots = SLOTS * 32
    pack = jnp.broadcast_to(rank_row * 32.0 + far_row, (slots, PIECES)) == iota((slots, PIECES), 0).astype(f32)
    pack = jnp.where(pack, 1.0, 0.0)
    unpack = jnp.broadcast_to(rank_col * 32.0 + far_col, (PIECES, slots)) == iota((PIECES, slots), 1).astype(f32)
    unpack = jnp.where(unpack, 1.0, 0.0)
    label_col = jnp.sum(pack * (cell_row + 1.0), axis=1, keepdims=True) - 1.0
    lane = iota((32, BLOCK), 1)
    label_rows = jnp.where(lane == 0, label_col[:32], jnp.where(lane == 1, label_col[32:], -1.0))
    return pack, unpack, label_rows


def composite(h, grid, target, background):
    def at(depth, channel):
        return grid[depth * SUB : (depth + 1) * SUB, channel * WIDE : (channel + 1) * WIDE]

    in_front = jnp.ones((TILE_DEV, WIDE), f32)
    seen = [jnp.zeros((TILE_DEV, WIDE), f32) for _ in range(3)]
    fronts = []
    for depth in range(MAXD):
        fronts.append(in_front)
        seen = [seen[c] + in_front * at(depth, c) for c in range(3)]
        in_front = in_front * (1.0 - at(depth, 3))
    residual = [
        seen[c] + in_front * background[c] - target[c, :, h * WIDE : (h + 1) * WIDE] for c in range(3)
    ]
    behind = [jnp.full((TILE_DEV, WIDE), background[c], f32) for c in range(3)]
    rows = [None] * MAXD
    for depth in reversed(range(MAXD)):
        through = 1.0 - at(depth, 3)
        by_trans = residual[0] * behind[0] + residual[1] * behind[1] + residual[2] * behind[2]
        rows[depth] = jnp.concatenate(
            [fronts[depth] * residual[c] for c in range(3)] + [fronts[depth] * by_trans], axis=1
        )
        behind = [at(depth, c) + through * behind[c] for c in range(3)]
    return jnp.concatenate(rows, axis=0)


def step_kernel(
    params_hbm,
    blocks_hbm,
    live_hbm,
    owner_hbm,
    cell_hbm,
    target_hbm,
    background_hbm,
    features_hbm,
    moments_hbm,
    grads_ref,
    blocks,
    live,
    background,
    block_rows,
    owner,
    cell,
    target,
    features,
    moments,
    pool,
    stage,
    turned,
    table,
    spread,
    prefix,
    segment,
    alphas,
    weights,
    ends,
    weight_parts,
    pieces,
    sent,
    got,
    replies,
    answers,
    labels,
    got_labels,
    cotangent,
    moved,
    summed,
    cut_grads,
    local_sem,
    halo_send,
    halo_recv,
    edge_send,
    edge_recv,
    label_send,
    label_recv,
    send_sem,
    recv_sem,
    reply_send,
    reply_recv,
):
    regions, region = lax.axis_size("region"), lax.axis_index("region")
    count, me = lax.axis_size("dom"), lax.axis_index("dom")
    upper, lower = lax.rem(region + 1, regions), lax.rem(region + regions - 1, regions)

    def block_rows_of(ref, b):
        return ref.at[pl.ds(b * ROWS, PARAMS)]

    fetches = []

    def fetch(src, dst):
        copy = pltpu.make_async_copy(src, dst, local_sem.at[len(fetches)])
        copy.start()
        fetches.append(copy)
        return copy

    routing = [fetch(owner_hbm, owner), fetch(cell_hbm, cell)]
    own = [
        fetch(params_hbm.at[:, pl.ds(b * BLOCK, BLOCK)], block_rows_of(pool, b)) for b in range(BLOCKS)
    ]
    scalars = [fetch(blocks_hbm, blocks), fetch(live_hbm, live), fetch(features_hbm, features)]
    later = [
        fetch(blocks_hbm, block_rows),
        fetch(target_hbm, target),
        fetch(background_hbm, background),
        fetch(moments_hbm, moments),
    ]

    barrier = pltpu.get_barrier_semaphore()

    def signal(**where):
        pl.semaphore_signal(barrier, inc=1, device_id=where, device_id_type=MESH)

    def greet(d, carry):
        signal(dom=lax.rem(me + d, count))
        return carry

    signal(region=upper)
    signal(region=lower)
    lax.fori_loop(1, count, greet, 0)

    for copy in routing:
        copy.wait()
    pack, unpack, label_rows = route(owner[...].astype(f32), cell[...].astype(f32), me)
    for d in range(32):
        labels[d] = label_rows[d : d + 1]
    pl.semaphore_wait(barrier, count + 1)

    def remote(src, dst, send, recv, **where):
        return pltpu.make_async_remote_copy(
            src_ref=src, dst_ref=dst, send_sem=send, recv_sem=recv, device_id=where, device_id_type=MESH
        )

    def label(d, many=1):
        rows = pl.ds(d, many)
        return remote(
            labels.at[rows], got_labels.at[rows], label_send, label_recv, dom=lax.rem(me + d, count)
        )

    def message(d, many):
        return pl.ds(pl.multiple_of(d * MESSAGE, MESSAGE), many * MESSAGE)

    def payload(h, d, many=1):
        rows = message(d, many)
        return remote(
            sent.at[h, rows], got.at[h, rows], send_sem.at[h], recv_sem.at[h], dom=lax.rem(me + d, count)
        )

    def reply(h, d, many=1):
        rows = message(d, many)
        return remote(
            replies.at[h, rows],
            answers.at[h, rows],
            reply_send.at[h],
            reply_recv.at[h],
            dom=lax.rem(me + count - d, count),
        )

    def start_all(copy):
        def one(d, carry):
            copy(count - d).start()
            return carry

        lax.fori_loop(1, count, one, 0, unroll=START_UNROLL)

    others = count - 1

    halo = [
        remote(
            params_hbm.at[:, pl.ds((BLOCKS - 1) * BLOCK, BLOCK)],
            block_rows_of(pool, LOW),
            halo_send.at[0],
            halo_recv.at[0],
            region=upper,
        ),
        remote(
            params_hbm.at[:, pl.ds(0, BLOCK)],
            block_rows_of(pool, HIGH),
            halo_send.at[1],
            halo_recv.at[1],
            region=lower,
        ),
    ]
    for copy in halo:
        copy.start()

    for copy in own:
        copy.wait()
    for b in range(POOL, 2 * SUB):
        pool[b * ROWS : b * ROWS + PARAMS, :] = pool[0:PARAMS, :]
    tabulate(0, SUB, pool, stage, turned, table, spread)
    start_all(label)
    got_labels[0] = labels[0]
    lane = iota((BLOCK, COLS), 1)
    table[DEAD] = jnp.where(lane == 0, -1e30, 0.0).astype(bf16)
    spread[DEAD] = jnp.zeros((3, BLOCK, BLOCK), f32)

    for copy in scalars:
        copy.wait()
    for copy in halo:
        copy.wait_recv()
    tabulate(1, POOL - SUB, pool, stage, turned, table, spread)
    for h in range(HALVES):
        forward_half(h, blocks, live, features, table, spread, prefix, segment, pieces, alphas)
        rendered = [pieces[r * PIECES : (r + 1) * PIECES, :] for r in range(PARTS)]
        rendered = jnp.concatenate(rendered, axis=1)
        put_slots(sent.at[h], exact_pick(pack, rendered))
        start_all(functools.partial(payload, h))
        got[h, :MESSAGE] = sent[h, :MESSAGE]

    weigh_half(0, prefix, alphas, weights, ends, weight_parts)
    for copy in later:
        copy.wait()
    label(1, others).wait()
    arrived = jnp.concatenate([got_labels[d] for d in range(32)], axis=0)
    arrived_col = jnp.concatenate([arrived[:, 0:1], arrived[:, 1:2]], axis=0)
    arrived_row = to_row(arrived_col)
    slots = SLOTS * 32

    def cell_of(place):
        return ((place % TILE_DEV) * MAXD + place // TILE_DEV).astype(f32)

    gather = jnp.broadcast_to(arrived_row, (CELLS, slots)) == cell_of(iota((CELLS, slots), 0))
    gather = jnp.where(gather, 1.0, 0.0)
    scatter = jnp.broadcast_to(arrived_col, (slots, CELLS)) == cell_of(iota((slots, CELLS), 1))
    scatter = jnp.where(scatter, 1.0, 0.0)
    colours = [background[c] for c in range(3)]
    for h in range(HALVES):
        payload(h, 1, others).wait()
        grid = exact_pick(gather, get_slots(got.at[h]))
        put_slots(replies.at[h], exact_pick(scatter, composite(h, grid, target, colours)))
        start_all(functools.partial(reply, h))
        answers[h, :MESSAGE] = replies[h, :MESSAGE]
        if h + 1 < HALVES:
            weigh_half(h + 1, prefix, alphas, weights, ends, weight_parts)

    for h in range(HALVES):
        reply(h, 1, others).wait()
        back = exact_pick(unpack, get_slots(answers.at[h]))
        for k in range(WIDE // BLOCK):
            for c in range(SUB):
                lanes = slice(c * WIDE + k * BLOCK, c * WIDE + (k + 1) * BLOCK)
                rows = back[:, lanes] if c < 4 else jnp.zeros((PIECES, BLOCK), f32)
                cotangent[pl.ds(k * PIECES * SUB + c, PIECES, stride=SUB), :] = rows
        backward_half(
            h, blocks, live, moments, table, segment, alphas, weights, ends, weight_parts, cotangent, moved
        )

    rows = own_block(block_rows[...]).astype(f32)
    gather_moments(rows[0:1], rows[1:2], moved, summed)
    pull_splat(1, pool, summed, cut_grads)
    edges = [
        remote(block_rows_of(cut_grads, HIGH - SUB), block_rows_of(grads_ref, FROM_LEFT), edge_send.at[0], edge_recv.at[0], region=upper),
        remote(block_rows_of(cut_grads, LOW - SUB), block_rows_of(grads_ref, FROM_RIGHT), edge_send.at[1], edge_recv.at[1], region=lower),
    ]
    for copy in edges:
        copy.start()
    pull_splat(0, pool, summed, grads_ref)
    for copy in halo:
        copy.wait_send()
    for copy in edges:
        copy.wait()


def whole(memory=pltpu.VMEM):
    return pl.BlockSpec(memory_space=memory)


def step(*operands):
    shape = jax.ShapeDtypeStruct
    vmem, smem, dma = pltpu.VMEM, pltpu.SMEM, pltpu.SemaphoreType.DMA
    slots = vmem((HALVES, 32 * MESSAGE, BLOCK), f32)
    label = vmem((32, 1, BLOCK), f32)
    return pl.pallas_call(
        step_kernel,
        out_shape=shape(((FROM_RIGHT + 1) * ROWS, BLOCK), f32),
        in_specs=[whole(pltpu.HBM)] * 9,
        out_specs=whole(),
        scratch_shapes=[
            smem((2, PIECES), jnp.int32),
            smem((1, PIECES), jnp.int32),
            smem((3,), f32),
            vmem((2, PIECES), jnp.int32),
            vmem((1, PIECES), jnp.int32),
            vmem((1, PIECES), jnp.int32),
            vmem((3, TILE_DEV, PIX), f32),
            vmem((PIECES, 32, PIX), bf16),
            vmem((PIECES, 16, PIX), bf16),
            vmem((2 * SUB * ROWS, BLOCK), f32),
            vmem((SUB * COLS, BLOCK), f32),
            vmem((BLOCK, BLOCK), f32),
            vmem((TAB, BLOCK, COLS), bf16),
            vmem((TAB, 3, BLOCK, BLOCK), f32),
            vmem((HALVES, PIECES, 2, SUB, WIDE), f32),
            vmem((HALVES, PIECES, 2, 3, SUB, WIDE), f32),
            vmem((HALVES, PIECES, 2, BLOCK, WIDE), f32),
            vmem((HALVES, PIECES, 2, BLOCK, WIDE), f32),
            vmem((HALVES, PIECES, 2, SUB, WIDE), f32),
            vmem((HALVES, PIECES, 2 * BLOCK, 2 * WIDE), bf16),
            vmem((4 * WIDE // BLOCK * PIECES, BLOCK), f32),
            slots,
            slots,
            slots,
            slots,
            label,
            label,
            vmem((WIDE // BLOCK * PIECES * SUB, BLOCK), f32),
            vmem((2 * PIECES * 32, BLOCK), f32),
            vmem((32, 2 * SUB, BLOCK), f32),
            vmem((SUB * ROWS, BLOCK), f32),
            dma((17,)),
            dma((2,)),
            dma((2,)),
            dma((2,)),
            dma((2,)),
            dma,
            dma,
            dma((HALVES,)),
            dma((HALVES,)),
            dma((HALVES,)),
            dma((HALVES,)),
        ],
        compiler_params=pltpu.CompilerParams(
            collective_id=0, has_side_effects=True, vmem_limit_bytes=VMEM_LIMIT
        ),
        name="render_step",
    )(*operands)


def adam_kernel(
    grads_ref, params_ref, first_ref, second_ref,
    gradient_ref, new_params_ref, new_first_ref, new_second_ref,
):
    for b in range(BLOCKS):
        cols = slice(b * BLOCK, (b + 1) * BLOCK)
        gradient = grads_ref[b * ROWS : b * ROWS + PARAMS, :]
        if b == 0:
            gradient = gradient + grads_ref[FROM_LEFT * ROWS : FROM_LEFT * ROWS + PARAMS, :]
        if b == BLOCKS - 1:
            gradient = gradient + grads_ref[FROM_RIGHT * ROWS : FROM_RIGHT * ROWS + PARAMS, :]
        new_first = beta_one * first_ref[:, cols] + (1 - beta_one) * gradient
        new_second = beta_two * second_ref[:, cols] + (1 - beta_two) * gradient * gradient
        update = (
            new_first
            / (1 - beta_one**adam_step)
            / (jnp.sqrt(new_second / (1 - beta_two**adam_step)) + tiny)
        )
        gradient_ref[:, cols] = gradient
        new_params_ref[:, cols] = params_ref[:, cols] - rate * update
        new_first_ref[:, cols] = new_first
        new_second_ref[:, cols] = new_second


def adam(*operands):
    return pl.pallas_call(
        adam_kernel,
        out_shape=(jax.ShapeDtypeStruct((PARAMS, BLOCKS * BLOCK), f32),) * 4,
        in_specs=[whole()] * 4,
        out_specs=(whole(),) * 4,
        compiler_params=pltpu.CompilerParams(vmem_limit_bytes=8 * 1024 * 1024),
        name="adam",
    )(*operands)


def on_device(
    params,
    first_moment,
    second_moment,
    piece_blocks,
    piece_live,
    piece_owner,
    piece_cell,
    target,
    background,
):
    grads = step(
        params,
        piece_blocks[0].T,
        piece_live,
        piece_owner,
        piece_cell,
        jnp.transpose(target[0], (1, 0, 2)),
        background,
        jnp.asarray(exponent_features()),
        jnp.asarray(moment_features()),
    )
    return adam(grads, params, first_moment, second_moment)


def solution(mesh):
    in_specs = (
        P(None, ("region", "dom")),
        P(None, ("region", "dom")),
        P(None, ("region", "dom")),
        P(("region", "dom"), None, None),
        P(("region", "dom"), None),
        P(("region", "dom"), None),
        P(("region", "dom"), None),
        P(("region", "dom"), None, None, None),
        P(),
    )
    out_specs = (
        P(None, ("region", "dom")),
        P(None, ("region", "dom")),
        P(None, ("region", "dom")),
        P(None, ("region", "dom")),
    )
    return jax.shard_map(
        on_device, mesh=mesh, in_specs=in_specs, out_specs=out_specs, check_vma=False
    )
```
